256 devices in a mesh: leaf: 64 (over z, x, core), mode: 4 (over y).
Axes of the slice: x: 4, y: 4, z: 8, core: 2. Of those that a mesh axis runs over, the one named last changes fastest.
Arguments:
- leaf_sizes: int32 [256], P('leaf'), may hold values from 1 to 128, 24576 in all
- leaf_stiffness: float32 [32768], P('leaf'), may hold values from 1 to 8
- coupling: float32 [3, 32768, 512], P(None, 'leaf', 'mode'), may hold values from -0.25 to 0.25
- omega_root: float32 [512], P('leaf'), may hold values from 1 to 8
- omega_mid: float32 [1024], P('leaf'), may hold values from 1 to 8
- omega_low: float32 [2048], P('leaf'), may hold values from 1 to 8
- start_leaf: float32 [256, 32768], P('mode', 'leaf'), may hold values from -6 to 6
- start_root: float32 [256, 512], P('mode', 'leaf'), may hold values from -6 to 6
- start_mid: float32 [256, 1024], P('mode', 'leaf'), may hold values from -6 to 6
- start_low: float32 [256, 2048], P('mode', 'leaf'), may hold values from -6 to 6
Outputs:
- vectors_leaf: float32 [256, 32768], P('mode', 'leaf')
- vectors_root: float32 [256, 512], P('mode', 'leaf')
- vectors_mid: float32 [256, 1024], P('mode', 'leaf')
- vectors_low: float32 [256, 2048], P('mode', 'leaf')
- mass_root: float32 [512, 512], P('leaf', 'mode')
- mass_mid: float32 [1024, 512], P('leaf', 'mode')
- mass_low: float32 [2048, 512], P('leaf', 'mode')
The draws below stay inside these ranges and needn't reach their ends.
Inputs may be any that keep to these rules, and one draw needn't show every extreme that they name: leaf_sizes[l] counts the live modal coordinates of substructure l; they sum to 24576 and the largest is 128.
All inputs are finite; a program needn't handle non-finite values. No bound on the sum of `leaf_sizes` on one device may be relied on, other than what follows from the above.
Results may differ from the reference program's by a relative error of at most 0.00013.
Values sent between devices are 32-bit elements; how exact they have to be, the bound alone decides.
A program may use at most 64 MiB of HBM per device.

```python
import math
import jax
import jax.numpy as jnp
import numpy as np
from jax import lax

NL = 128
NI = 512
P_SIZE = 256
ITERS = 3
LEAVES = 256
ROWS = 36352


def block_levels(key, shape, pieces, low, top_value):
    def one(dim, parts):
        draws = jax.random.uniform(jax.random.fold_in(jax.random.fold_in(key, 6), dim), (parts,), jnp.float32, low / len(pieces), top_value / len(pieces))
        return jnp.repeat(jnp.exp(draws), shape[dim] // parts).reshape((-1,) + (1,) * (len(shape) - dim - 1))

    loudness = one(*pieces[0])
    for cut in pieces[1:]:
        loudness = loudness * one(*cut)
    return loudness


def split_up(count, total, limit, skew):
    weights = [(1 << 20) // math.isqrt(standing ** skew) + 1 for standing in range(2, count + 1)]
    surplus, counts = total - limit - (count - 1), [1] * (count - 1)
    while surplus > 0:
        free = [i for i in range(count - 1) if counts[i] < limit]
        pool, remaining = sum([weights[i] for i in free]), surplus
        for i in free:
            addition = min(limit - counts[i], max(1, remaining * weights[i] // pool), surplus)
            counts[i] = counts[i] + addition
            surplus = surplus - addition
    return np.array([limit] + counts)


def ragged_sizes(key, count, total, bound, skew):
    if count == 2:
        one = jax.random.randint(key, (), max(1, total - bound), min(bound, total - 1) + 1)
        return jnp.stack([one, total - one])
    tallies = jnp.asarray(split_up(count, total, bound, skew), jnp.int32)
    couples = (count - 1) // 2
    source_of, receiver = tallies[1:1 + 2 * couples:2], tallies[2:2 + 2 * couples:2]
    room = jnp.minimum(source_of - 1, bound - receiver)
    shifted = jax.random.randint(jax.random.fold_in(key, 1), (couples,), 0, 1 << 20) % (room + 1)
    tallies = tallies.at[1:1 + 2 * couples:2].set(source_of - shifted).at[2:2 + 2 * couples:2].set(receiver + shifted)
    return tallies[jax.random.permutation(jax.random.fold_in(key, 2), count)]


def centred(own_key, dims, deviation, bound, split=(), held_as=jnp.bfloat16):
    result = jax.random.normal(own_key, dims, jnp.float32) * deviation
    if len(split) > 0:
        result = block_levels(own_key, dims, split, -0.22, 0.18) * result
    return jnp.clip(result, min=-bound, max=bound).astype(held_as)


def setup_inputs(seed: int = 0) -> dict:
    key_list = jax.random.split(jax.random.key(seed), 11)
    return {
        "leaf_sizes": ragged_sizes(key_list[0], LEAVES, LEAVES * NL * 3 // 4, NL, 2).astype(jnp.int32),
        "leaf_stiffness": jnp.clip(jnp.exp(math.log(8.0) - 2.0794415 * jax.random.uniform(key_list[1], (LEAVES * NL,), jnp.float32) ** block_levels(key_list[1], (LEAVES * NL,), ((0, 64),), -0.2, 0.2)), 1.0, 8.0),
        "coupling": centred(key_list[2], (3, LEAVES * NL, NI), NI ** -0.5, 0.25, ((1, 64), (2, 4)), jnp.float32),
        "omega_root": jnp.clip(jnp.exp(math.log(8.0) - 2.0794415 * jax.random.uniform(key_list[3], (NI,), jnp.float32) ** block_levels(key_list[3], (NI,), ((0, 64),), -0.2, 0.2)), 1.0, 8.0),
        "omega_mid": jnp.clip(jnp.exp(math.log(8.0) - 2.0794415 * jax.random.uniform(key_list[4], (2 * NI,), jnp.float32) ** block_levels(key_list[4], (2 * NI,), ((0, 64),), -0.2, 0.2)), 1.0, 8.0),
        "omega_low": jnp.clip(jnp.exp(math.log(8.0) - 2.0794415 * jax.random.uniform(key_list[5], (4 * NI,), jnp.float32) ** block_levels(key_list[5], (4 * NI,), ((0, 64),), -0.2, 0.2)), 1.0, 8.0),
        "start_leaf": centred(key_list[6], (P_SIZE, LEAVES * NL), 1.0, 6.0, ((0, 4), (1, 64)), jnp.float32),
        "start_root": centred(key_list[7], (P_SIZE, NI), 1.0, 6.0, ((0, 4), (1, 64)), jnp.float32),
        "start_mid": centred(key_list[8], (P_SIZE, 2 * NI), 1.0, 6.0, ((0, 4), (1, 64)), jnp.float32),
        "start_low": centred(key_list[9], (P_SIZE, 4 * NI), 1.0, 6.0, ((0, 4), (1, 64)), jnp.float32),
    }


def reference(leaf_sizes, leaf_stiffness, coupling, omega_root, omega_mid, omega_low, start_leaf, start_root, start_mid, start_low):
    precise = lax.Precision.HIGHEST
    leaf_count = leaf_sizes.shape[0]
    live_mask = (jnp.arange(NL)[None, :] < leaf_sizes[:, None]).astype(jnp.float32)
    inverse = live_mask / leaf_stiffness.reshape(leaf_count, NL)
    blocks = coupling.reshape(3, leaf_count, NL, NI)
    identity = jnp.eye(NI, dtype=jnp.float32)
    masses = []
    for tree_level in range(3):
        groups = 2 ** tree_level
        scaled = blocks[tree_level] * (inverse * inverse)[:, :, None]
        leaf_terms = jnp.einsum('nli,nlj->nij', scaled, blocks[tree_level], precision=precise)
        summed = leaf_terms.reshape(groups, leaf_count // groups, NI, NI).sum(axis=1)
        masses.append((summed + identity[None]).reshape(groups * NI, NI))
    omegas = [omega_root, omega_mid, omega_low]
    leaf_values = start_leaf.reshape(P_SIZE, leaf_count, NL) * live_mask[None]
    interface_values = [start_root, start_mid, start_low]
    for sweep_index in range(ITERS):
        coupled = jnp.zeros((P_SIZE, leaf_count, NL), jnp.float32)
        for tree_level in range(3):
            groups = 2 ** tree_level
            spread = jnp.repeat(interface_values[tree_level].reshape(P_SIZE, groups, NI), leaf_count // groups, axis=1)
            coupled = coupled + jnp.einsum('pni,nli->pnl', spread, blocks[tree_level], precision=precise)
        modal_mass = live_mask[None] * leaf_values - inverse[None] * coupled
        modal_next = modal_mass * inverse[None]
        mass_parts = []
        next_parts = []
        for tree_level in range(3):
            groups = 2 ** tree_level
            sums = jnp.einsum('pnl,nli->pni', modal_next, blocks[tree_level], precision=precise)
            sums = sums.reshape(P_SIZE, groups, leaf_count // groups, NI).sum(axis=2).reshape(P_SIZE, groups * NI)
            applied = interface_values[tree_level] - sums
            mass_parts.append(applied)
            next_parts.append(applied / omegas[tree_level][None, :])
        flat_next = jnp.concatenate([modal_next.reshape(P_SIZE, leaf_count * NL)] + next_parts, axis=1)
        flat_mass = jnp.concatenate([modal_mass.reshape(P_SIZE, leaf_count * NL)] + mass_parts, axis=1)
        gram_matrix = jnp.dot(flat_next, flat_mass.T, precision=precise) / ROWS
        gram_matrix = 0.5 * (gram_matrix + gram_matrix.T)
        lower_factor = jnp.linalg.cholesky(gram_matrix)
        solved = jax.scipy.linalg.solve_triangular(lower_factor, flat_next, lower=True)
        leaf_values = solved[:, :leaf_count * NL].reshape(P_SIZE, leaf_count, NL)
        first = leaf_count * NL
        interface_values = []
        for tree_level in range(3):
            extent = 2 ** tree_level * NI
            interface_values.append(solved[:, first:first + extent])
            first = first + extent
    return (leaf_values.reshape(P_SIZE, leaf_count * NL), interface_values[0], interface_values[1], interface_values[2], masses[0], masses[1], masses[2])
```

```python
import functools
import jax
import jax.numpy as jnp
from jax import lax
from jax.experimental import pallas as pl
from jax.experimental.pallas import tpu as pltpu
from jax.sharding import PartitionSpec as P

ITERS = 3
ROWS = 36352.0
SCALE = 2.0**-12
MESH = pl.DeviceIdType.MESH
HI = lax.Precision.HIGHEST
F32 = jnp.float32


def nt(a, b):
    return lax.dot_general(a, b, (((1,), (1,)), ((), ())), precision=HI, preferred_element_type=F32)


def nn(a, b):
    return lax.dot_general(a, b, (((1,), (0,)), ((), ())), precision=HI, preferred_element_type=F32)


def root_row(q, j):
    return q * 384 + 8 * j


def mid_row(half, j):
    return (2 * half + j // 8) * 384 + 128 + 16 * (j % 8)


def low_row(j):
    return (j // 4) * 384 + 256 + 32 * (j % 4)


def remote(src, dst, send, recv, leaf, mode):
    return pltpu.make_async_remote_copy(
        src_ref=src,
        dst_ref=dst,
        send_sem=send,
        recv_sem=recv,
        device_id=(leaf, mode),
        device_id_type=MESH,
    )


def sweeps_kernel(
    sizes_ref,
    stiff_ref,
    coupling_ref,
    leaf_ref,
    own_ref,
    gram_ref,
    next_ref,
    iface_ref,
    mroot_ref,
    mmid_ref,
    mlow_ref,
    gt,
    init,
    iv,
    tt,
    tp,
    rs,
    cs,
    cb,
    agp,
    ag,
    yl,
    iy,
    gp,
    grs,
    gc,
    gag,
    gy,
    mp,
    mrs,
    mc,
    ms,
    gsend,
    grecv,
    psend,
    precv,
    csend,
    crecv,
    ysend,
    yrecv,
):
    leaf = lax.axis_index("leaf")
    mode = lax.axis_index("mode")
    q = leaf // 16
    j = leaf % 16
    base = q * 16
    right = (mode + 1) % 4
    left = (mode + 3) % 4
    across = (mode + 2) % 4
    partner = q + 1 - 2 * (q % 2)
    half_base = q - q % 2
    far0 = (q + 2) % 4
    far1 = (partner + 2) % 4

    barrier = pltpu.get_barrier_semaphore()

    def greet_group(d, carry):
        pl.semaphore_signal(
            barrier, inc=1, device_id=(base + (j + d) % 16, mode), device_id_type=MESH
        )
        return carry

    for peer in (right, left, across):
        pl.semaphore_signal(barrier, inc=1, device_id=(leaf, peer), device_id_type=MESH)
    for peer in (partner, far0, far1):
        pl.semaphore_signal(barrier, inc=1, device_id=(peer * 16 + j, mode), device_id_type=MESH)
    lax.fori_loop(1, 16, greet_group, 0)
    for h in range(3):
        gt[mode, h] = coupling_ref[h].T
    init[q] = own_ref[0:24, :]
    pl.semaphore_wait(barrier, 21)

    def chunk(h, kind):
        if kind == 0:
            ref, peer = gt.at[mode, h], right
        elif kind == 1:
            ref, peer = gt.at[mode, h], left
        elif kind == 2:
            ref, peer = gt.at[left, h, pl.ds(0, 64)], right
        else:
            ref, peer = gt.at[right, h, pl.ds(64, 64)], left
        return remote(ref, ref, gsend.at[h, kind], grecv.at[h, kind], leaf, peer)

    def chunk_in(h, kind):
        if kind == 0:
            ref = gt.at[left, h]
        elif kind == 1:
            ref = gt.at[right, h]
        elif kind == 2:
            ref = gt.at[across, h, pl.ds(0, 64)]
        else:
            ref = gt.at[across, h, pl.ds(64, 64)]
        return remote(ref, ref, gsend.at[h, kind], grecv.at[h, kind], leaf, right)

    for h in range(3):
        chunk(h, 0).start()
        chunk(h, 1).start()

    def quarter_copy(src, dst, phase, peer):
        return remote(src, dst, csend.at[phase, peer], crecv.at[phase, q], peer * 16 + j, mode)

    def quarter_in(dst, phase, peer):
        return remote(dst, dst, csend.at[phase, peer], crecv.at[phase, peer], peer * 16 + j, mode)

    quarter_copy(init.at[q], init.at[q], 0, partner).start()
    quarter_copy(init.at[q, pl.ds(0, 8)], init.at[q, pl.ds(0, 8)], 0, far0).start()
    quarter_copy(init.at[q, pl.ds(0, 8)], init.at[q, pl.ds(0, 8)], 0, far1).start()
    quarter_in(init.at[partner], 0, partner).wait_recv()
    quarter_in(init.at[far0, pl.ds(0, 8)], 0, far0).wait_recv()
    quarter_in(init.at[far1, pl.ds(0, 8)], 0, far1).wait_recv()

    lane = lax.broadcasted_iota(jnp.int32, (48, 128), 1)
    row = lax.broadcasted_iota(jnp.int32, (48, 128), 0)
    low_lanes = lane < 64
    is_root = low_lanes & (row < 32)
    is_mid = (low_lanes & (row >= 32)) | (~low_lanes & (row < 16))
    front = jnp.concatenate([init[0, 0:8], init[1, 0:8], init[2, 0:8], init[3, 0:8], init[half_base, 8:24]], axis=0)
    back = jnp.concatenate([init[half_base + 1, 8:24], own_ref[24:56, :]], axis=0)
    ipk = jnp.where(low_lanes, front, pltpu.roll(back, 64, 1))
    omega = jnp.where(low_lanes, pltpu.roll(front, 64, 1), back)

    def group_start(phase, src_of, dst):
        def one(d, carry):
            t = (j + d) % 16
            remote(src_of(t), dst, psend.at[phase, t], precv.at[phase, j], base + t, mode).start()
            return carry

        lax.fori_loop(1, 16, one, 0)

    def group_wait(phase, src_of, dst_of):
        def one(d, carry):
            t = (j + d) % 16
            copy = remote(src_of(t), dst_of(t), psend.at[phase, t], precv.at[phase, t], base + t, mode)
            copy.wait_recv()
            return carry

        lax.fori_loop(1, 16, one, 0)

    def group_sent(phase, src_of, dst):
        def one(d, carry):
            t = (j + d) % 16
            remote(src_of(t), dst, psend.at[phase, t], precv.at[phase, j], base + t, mode).wait_send()
            return carry

        lax.fori_loop(1, 16, one, 0)

    def spread_start(s, values):
        agp[s] = values
        ag[s, j] = values
        group_start(s, lambda t: agp.at[s], ag.at[s, j])

    def spread_wait(s):
        group_wait(s, lambda t: agp.at[s], lambda t: ag.at[s, t])
        for t in range(16):
            block = ag[s, t]
            turned = pltpu.roll(block, 64, 1)
            for k in range(4):
                iv[root_row(k, t) : root_row(k, t) + 8, :] = block[8 * k : 8 * k + 8]
            iv[mid_row(0, t) : mid_row(0, t) + 16, :] = block[32:48]
            iv[mid_row(1, t) : mid_row(1, t) + 16, :] = turned[0:16]
            iv[low_row(t) : low_row(t) + 32, :] = turned[16:48]

    spread_start(0, ipk)

    coord = lax.broadcasted_iota(jnp.int32, (1, 128), 1)
    live = jnp.concatenate([(coord < sizes_ref[n]).astype(F32) for n in range(4)], axis=1)
    stiff = stiff_ref[...]
    inverse = live / stiff
    m = leaf_ref[...] * live * SCALE

    spread_wait(0)
    ivt = iv[:, 0:64].T
    coupled = jnp.zeros((64, 512), F32)

    iv_t = None
    for h in range(3):
        chunk_in(h, 0).wait_recv()
        chunk(h, 2).start()
        chunk_in(h, 1).wait_recv()
        chunk(h, 3).start()
    for h in range(3):
        chunk_in(h, 2).wait_recv()
        chunk_in(h, 3).wait_recv()

    for s in range(ITERS):
        if s > 0:
            spread_wait(s)
            ivt = iv[:, 0:64].T
        g2 = gt[...].reshape(1536, 512)
        coupled = nn(ivt, g2)
        modal_mass = live * m - inverse * coupled
        m = inverse * modal_mass
        if s == ITERS - 1:
            yl[mode] = m
            for k, peer in enumerate((right, left, across)):
                remote(yl.at[mode], yl.at[mode], ysend.at[0, k], yrecv.at[0, k], leaf, peer).start()
        tt[...] = nt(g2, jnp.concatenate([m, m], axis=0))
        for t in range(16):
            a = jnp.concatenate(
                [tt[root_row(k, t) : root_row(k, t) + 8, :] for k in range(4)]
                + [tt[mid_row(0, t) : mid_row(0, t) + 16, :]],
                axis=0,
            )
            b = jnp.concatenate(
                [tt[mid_row(1, t) : mid_row(1, t) + 16, :], tt[low_row(t) : low_row(t) + 32, :]],
                axis=0,
            )
            tp[s, t] = jnp.where(low_lanes, a, b)
        group_start(3 + s, lambda t: tp.at[s, t], rs.at[s, j])
        if s == 0:
            weighted = inverse * inverse
            for h in range(3):
                whole = jnp.concatenate([gt[c, h] for c in range(4)], axis=0)
                ms[h] = nt(whole * weighted, gt[mode, h])
            for t in range(16):
                for k in range(4):
                    mp[t, 8 * k : 8 * k + 8] = ms[0, 128 * k + 8 * t : 128 * k + 8 * t + 8]
                for k in range(2):
                    mp[t, 32 + 16 * k : 48 + 16 * k] = ms[1, 256 * k + 16 * t : 256 * k + 16 * t + 16]
                mp[t, 64:96] = ms[2, 32 * t : 32 * t + 32]
        rs[s, j] = tp[s, j]
        group_wait(3 + s, lambda t: tp.at[s, t], lambda t: rs.at[s, t])
        total = rs[s, 0]
        for t in range(1, 16):
            total = total + rs[s, t]
        cs[s] = total
        rootpart = pl.ds(0, 32)
        quarter_copy(cs.at[s], cb.at[s, q], 1 + s, partner).start()
        quarter_copy(cs.at[s, rootpart], cb.at[s, q, rootpart], 1 + s, far0).start()
        quarter_copy(cs.at[s, rootpart], cb.at[s, q, rootpart], 1 + s, far1).start()
        if s == 0:
            group_start(6, lambda t: mp.at[t], mrs.at[j])
            mrs[j] = mp[j]
        quarter_in(cb.at[s, partner], 1 + s, partner).wait_recv()
        quarter_in(cb.at[s, far0, rootpart], 1 + s, far0).wait_recv()
        quarter_in(cb.at[s, far1, rootpart], 1 + s, far1).wait_recv()
        near = jnp.where(is_root | is_mid, cb[s, partner], 0.0)
        far = jnp.where(is_root[0:32], cb[s, far0, 0:32] + cb[s, far1, 0:32], 0.0)
        far = jnp.concatenate([far, jnp.zeros((16, 128), F32)], axis=0)
        ipk = (ipk - (total + near + far)) / omega
        if s < ITERS - 1:
            spread_start(s + 1, ipk)

    cs[3] = ipk
    cs[4] = omega
    own_vals = []
    for k in (3, 4):
        turned = pltpu.roll(cs[k], 64, 1)
        odd = (q % 2) == 1
        mids = jnp.where(odd, turned[0:16], cs[k, 32:48])
        own_vals.append(
            jnp.concatenate([cs[k, pl.ds(pl.multiple_of(8 * q, 8), 8)], mids, turned[16:48]], axis=0)
        )
    own_next, own_omega = own_vals
    iy[mode] = own_next
    for k, peer in enumerate((right, left, across)):
        remote(iy.at[mode], iy.at[mode], ysend.at[1, k], yrecv.at[1, k], leaf, peer).start()
    y_from = (left, right, across)
    for k in range(3):
        remote(yl.at[mode], yl.at[y_from[k]], ysend.at[0, k], yrecv.at[0, k], leaf, right).wait_recv()
    heavy = m * stiff
    blocks = [nt(yl[c], heavy) for c in range(4)]
    for k in range(3):
        remote(iy.at[mode], iy.at[y_from[k]], ysend.at[1, k], yrecv.at[1, k], leaf, right).wait_recv()
    heavy_own = (own_next * own_omega)[:, 0:64].T
    blocks = [(blocks[c] + nt(iy[c][:, 0:64].T, heavy_own)) * (1.0 / ROWS) for c in range(4)]
    gp[...] = jnp.concatenate(
        [jnp.concatenate(blocks[0:2], axis=0), jnp.concatenate(blocks[2:4], axis=0)], axis=1
    )

    def piece(t):
        return gp.at[pl.ds(pl.multiple_of(8 * t, 8), 8)]

    group_start(7, piece, grs.at[j])
    grs[j] = gp[pl.ds(pl.multiple_of(8 * j, 8), 8)]
    group_wait(7, piece, lambda t: grs.at[t])
    total = grs[0]
    for t in range(1, 16):
        total = total + grs[t]
    gc[q] = total
    for peer in (partner, far0, far1):
        quarter_copy(gc.at[q], gc.at[q], 4, peer).start()
    for peer in (partner, far0, far1):
        quarter_in(gc.at[peer], 4, peer).wait_recv()
    gag[j] = (gc[0] + gc[1]) + (gc[2] + gc[3])
    group_start(8, lambda t: gag.at[j], gag.at[j])

    group_wait(6, lambda t: mp.at[t], lambda t: mrs.at[t])
    total = mrs[0]
    for t in range(1, 16):
        total = total + mrs[t]
    ms[0, 0:96] = total
    mid_of = pl.ds(pl.multiple_of(32 + 16 * (q % 2), 8), 16)
    mid_to = pl.ds(pl.multiple_of(48 - 16 * (q % 2), 8), 16)

    def root_of(k):
        return pl.ds(pl.multiple_of(8 * k, 8), 8)

    for peer in (partner, far0, far1):
        quarter_copy(ms.at[0, root_of(peer)], mc.at[q, pl.ds(0, 8)], 5, peer).start()
    quarter_copy(ms.at[0, mid_to], mc.at[q, pl.ds(8, 16)], 6, partner).start()

    group_wait(8, lambda t: gag.at[j], lambda t: gag.at[t])
    gy[mode] = gag[...].reshape(128, 128)
    for k, peer in enumerate((right, left, across)):
        remote(gy.at[mode], gy.at[mode], ysend.at[2, k], yrecv.at[2, k], leaf, peer).start()

    for peer in (partner, far0, far1):
        quarter_in(mc.at[peer, pl.ds(0, 8)], 5, peer).wait_recv()
    quarter_in(mc.at[partner, pl.ds(8, 16)], 6, partner).wait_recv()

    def unit(first, count):
        rows = lax.broadcasted_iota(jnp.int32, (count, 128), 0) + first
        cols = lax.broadcasted_iota(jnp.int32, (count, 128), 1) + mode * 128
        return (rows % 512 == cols).astype(F32)

    mroot_ref[...] = (
        ms[0, root_of(q)] + (mc[partner, 0:8] + mc[far0, 0:8] + mc[far1, 0:8]) + unit(leaf * 8, 8)
    )
    mmid_ref[...] = ms[0, mid_of] + mc[partner, 8:24] + unit(leaf * 16, 16)
    mlow_ref[...] = ms[0, 64:96] + unit(leaf * 32, 32)
    next_ref[...] = yl[...].reshape(256, 512)
    iface_ref[...] = iy[...]

    for k in range(3):
        remote(gy.at[mode], gy.at[y_from[k]], ysend.at[2, k], yrecv.at[2, k], leaf, right).wait_recv()
    for c in range(4):
        part = gy[c]
        gram_ref[c, 0:128] = part[:, 0:64]
        gram_ref[c, 128:256] = pltpu.roll(part, 64, 1)[:, 0:64]

    for h in range(3):
        for kind in range(4):
            chunk(h, kind).wait_send()
    quarter_copy(init.at[q], init.at[q], 0, partner).wait_send()
    quarter_copy(init.at[q, pl.ds(0, 8)], init.at[q, pl.ds(0, 8)], 0, far0).wait_send()
    quarter_copy(init.at[q, pl.ds(0, 8)], init.at[q, pl.ds(0, 8)], 0, far1).wait_send()
    for s in range(ITERS):
        group_sent(s, lambda t: agp.at[s], ag.at[s, j])
        group_sent(3 + s, lambda t: tp.at[s, t], rs.at[s, j])
        rootpart = pl.ds(0, 32)
        quarter_copy(cs.at[s], cb.at[s, q], 1 + s, partner).wait_send()
        quarter_copy(cs.at[s, rootpart], cb.at[s, q, rootpart], 1 + s, far0).wait_send()
        quarter_copy(cs.at[s, rootpart], cb.at[s, q, rootpart], 1 + s, far1).wait_send()
    group_sent(6, lambda t: mp.at[t], mrs.at[j])
    group_sent(7, piece, grs.at[j])
    group_sent(8, lambda t: gag.at[j], gag.at[j])
    for peer in (partner, far0, far1):
        quarter_copy(gc.at[q], gc.at[q], 4, peer).wait_send()
        quarter_copy(ms.at[0, root_of(peer)], mc.at[q, pl.ds(0, 8)], 5, peer).wait_send()
    quarter_copy(ms.at[0, mid_to], mc.at[q, pl.ds(8, 16)], 6, partner).wait_send()
    for k, peer in enumerate((right, left, across)):
        remote(yl.at[mode], yl.at[mode], ysend.at[0, k], yrecv.at[0, k], leaf, peer).wait_send()
        remote(iy.at[mode], iy.at[mode], ysend.at[1, k], yrecv.at[1, k], leaf, peer).wait_send()
        remote(gy.at[mode], gy.at[mode], ysend.at[2, k], yrecv.at[2, k], leaf, peer).wait_send()


def run_sweeps(leaf_sizes, stiff, coupling, start_leaf, own):
    vmem = pl.BlockSpec(memory_space=pltpu.VMEM)
    scratch = [
        (4, 3, 128, 512),
        (4, 24, 128),
        (1536, 128),
        (1536, 128),
        (3, 16, 48, 128),
        (3, 16, 48, 128),
        (5, 48, 128),
        (3, 4, 48, 128),
        (3, 48, 128),
        (3, 16, 48, 128),
        (4, 64, 512),
        (4, 56, 128),
        (128, 128),
        (16, 8, 128),
        (4, 8, 128),
        (16, 8, 128),
        (4, 128, 128),
        (16, 96, 128),
        (16, 96, 128),
        (4, 24, 128),
        (3, 512, 128),
    ]
    sems = [(3, 4), (3, 4), (9, 16), (9, 16), (7, 4), (7, 4), (3, 3), (3, 3)]
    shapes = [(4, 256, 64), (256, 512), (4, 56, 128), (8, 128), (16, 128), (32, 128)]
    return pl.pallas_call(
        sweeps_kernel,
        out_shape=[jax.ShapeDtypeStruct(shape, F32) for shape in shapes],
        in_specs=[pl.BlockSpec(memory_space=pltpu.SMEM)] + [vmem] * 4,
        out_specs=[vmem] * 6,
        scratch_shapes=[pltpu.VMEM(shape, F32) for shape in scratch]
        + [pltpu.SemaphoreType.DMA(shape) for shape in sems],
        compiler_params=pltpu.CompilerParams(
            collective_id=0, has_side_effects=True, vmem_limit_bytes=48 * 1024 * 1024
        ),
        name="sweeps",
    )(leaf_sizes, stiff, coupling, start_leaf, own)


def local(
    leaf_sizes,
    leaf_stiffness,
    coupling,
    omega_root,
    omega_mid,
    omega_low,
    start_leaf,
    start_root,
    start_mid,
    start_low,
):
    mode = lax.axis_index("mode")
    starts = jnp.concatenate([start_root, start_mid, start_low], axis=1).T * SCALE
    omegas = jnp.concatenate([omega_root, omega_mid, omega_low])
    own = jnp.concatenate([starts, jnp.broadcast_to(omegas[:, None], (56, 64))], axis=1)
    gram, modal, iface, mass_root, mass_mid, mass_low = run_sweeps(
        leaf_sizes, leaf_stiffness.reshape(1, -1), coupling, start_leaf, own
    )
    gram = gram.transpose(1, 0, 2).reshape(256, 256)
    gram = 0.5 * (gram + gram.T)
    factor = jnp.linalg.cholesky(gram)
    stacked = jnp.concatenate(
        [modal, iface[:, :, 0:64].transpose(0, 2, 1).reshape(256, 56)], axis=1
    )
    solved = jax.scipy.linalg.solve_triangular(factor, stacked, lower=True)
    rows = lax.dynamic_slice_in_dim(solved, mode * 64, 64, 0)
    return (
        rows[:, 0:512],
        rows[:, 512:520],
        rows[:, 520:536],
        rows[:, 536:568],
        mass_root,
        mass_mid,
        mass_low,
    )


def solution(mesh):
    placed = (
        P("leaf"),
        P("leaf"),
        P(None, "leaf", "mode"),
        P("leaf"),
        P("leaf"),
        P("leaf"),
        P("mode", "leaf"),
        P("mode", "leaf"),
        P("mode", "leaf"),
        P("mode", "leaf"),
    )
    return jax.shard_map(
        local,
        mesh=mesh,
        in_specs=placed,
        out_specs=(
            P("mode", "leaf"),
            P("mode", "leaf"),
            P("mode", "leaf"),
            P("mode", "leaf"),
            P("leaf", "mode"),
            P("leaf", "mode"),
            P("leaf", "mode"),
        ),
        check_vma=False,
    )
```

```python
import functools
import jax
import jax.numpy as jnp
from jax import lax
from jax.experimental import pallas as pl
from jax.experimental.pallas import tpu as pltpu
from jax.sharding import PartitionSpec as P

ITERS = 3
ROWS = 36352.0
SCALE = 2.0**-12
MESH = pl.DeviceIdType.MESH
HI = lax.Precision.HIGHEST
F32 = jnp.float32
BF16 = jnp.bfloat16
NEAR_FIRST = ((0, 1), (0, 3), (1, 0), (0, 2), (1, 1), (1, 3), (1, 2))


def nt(a, b):
    return lax.dot_general(a, b, (((1,), (1,)), ((), ())), precision=HI, preferred_element_type=F32)


def nn(a, b):
    return lax.dot_general(a, b, (((1,), (0,)), ((), ())), precision=HI, preferred_element_type=F32)


def tn(a, b):
    return lax.dot_general(a, b, (((0,), (0,)), ((), ())), precision=HI, preferred_element_type=F32)


def halves(x):
    high = x.astype(BF16)
    return high, (x - high.astype(F32)).astype(BF16)


def nn16(a, b):
    return lax.dot_general(a, b, (((1,), (0,)), ((), ())), preferred_element_type=F32)


def nt16(a, b):
    return lax.dot_general(a, b, (((1,), (1,)), ((), ())), preferred_element_type=F32)


def root_row(q, j):
    return q * 384 + 8 * j


def mid_row(half, j):
    return (2 * half + j // 8) * 384 + 128 + 16 * (j % 8)


def low_row(j):
    return (j // 4) * 384 + 256 + 32 * (j % 4)


def remote(src, dst, send, recv, leaf, mode):
    return pltpu.make_async_remote_copy(
        src_ref=src,
        dst_ref=dst,
        send_sem=send,
        recv_sem=recv,
        device_id=(leaf, mode),
        device_id_type=MESH,
    )


def sweeps_kernel(
    sizes_ref,
    stiff_ref,
    coupling_ref,
    leaf_ref,
    own_ref,
    gram_ref,
    next_ref,
    iface_ref,
    mroot_ref,
    mmid_ref,
    mlow_ref,
    gt,
    ghi,
    glo,
    init,
    iv,
    tt,
    tp,
    xb,
    xs,
    rs,
    cs,
    cb,
    ag,
    yl,
    iy,
    gp,
    grs,
    gc,
    gag,
    gy,
    mp,
    mxb,
    mxs,
    mrs,
    mc,
    ms,
    gsend,
    grecv,
    psend,
    precv,
    hsend,
    hrecv,
    xsend,
    xrecv,
    csend,
    crecv,
    ysend,
    yrecv,
):
    leaf = lax.axis_index("leaf")
    mode = lax.axis_index("mode")
    q = leaf // 16
    j = leaf % 16
    base = q * 16
    core = j % 2
    chip = j // 2
    chips = [((chip // 4 + dz) % 2) * 4 + (chip + dx) % 4 for dz, dx in NEAR_FIRST]
    right = (mode + 1) % 4
    left = (mode + 3) % 4
    across = (mode + 2) % 4
    partner = q + 1 - 2 * (q % 2)
    half_base = q - q % 2
    far0 = (q + 2) % 4
    far1 = (partner + 2) % 4

    barrier = pltpu.get_barrier_semaphore()

    def greet_group(d, carry):
        pl.semaphore_signal(
            barrier, inc=1, device_id=(base + (j + d) % 16, mode), device_id_type=MESH
        )
        return carry

    for peer in (right, left, across):
        pl.semaphore_signal(barrier, inc=1, device_id=(leaf, peer), device_id_type=MESH)
    for peer in (partner, far0, far1):
        pl.semaphore_signal(barrier, inc=1, device_id=(peer * 16 + j, mode), device_id_type=MESH)
    lax.fori_loop(1, 16, greet_group, 0)
    for h in range(3):
        gt[mode, h] = coupling_ref[h].T
    init[q] = own_ref[0:24, :]
    pl.semaphore_wait(barrier, 21)

    def chunk(h, kind):
        if kind == 0:
            ref, peer = gt.at[mode, h], right
        elif kind == 1:
            ref, peer = gt.at[mode, h], left
        elif kind == 2:
            ref, peer = gt.at[left, h, pl.ds(0, 64)], right
        else:
            ref, peer = gt.at[right, h, pl.ds(64, 64)], left
        return remote(ref, ref, gsend.at[h, kind], grecv.at[h, kind], leaf, peer)

    def chunk_in(h, kind):
        if kind == 0:
            ref = gt.at[left, h]
        elif kind == 1:
            ref = gt.at[right, h]
        elif kind == 2:
            ref = gt.at[across, h, pl.ds(0, 64)]
        else:
            ref = gt.at[across, h, pl.ds(64, 64)]
        return remote(ref, ref, gsend.at[h, kind], grecv.at[h, kind], leaf, right)

    for h in range(3):
        chunk(h, 0).start()
        chunk(h, 1).start()

    def quarter_copy(src, dst, phase, peer):
        return remote(src, dst, csend.at[phase, peer], crecv.at[phase, q], peer * 16 + j, mode)

    def quarter_in(dst, phase, peer):
        return remote(dst, dst, csend.at[phase, peer], crecv.at[phase, peer], peer * 16 + j, mode)

    quarter_copy(init.at[q], init.at[q], 0, partner).start()
    quarter_copy(init.at[q, pl.ds(0, 8)], init.at[q, pl.ds(0, 8)], 0, far0).start()
    quarter_copy(init.at[q, pl.ds(0, 8)], init.at[q, pl.ds(0, 8)], 0, far1).start()
    quarter_in(init.at[partner], 0, partner).wait_recv()
    quarter_in(init.at[far0, pl.ds(0, 8)], 0, far0).wait_recv()
    quarter_in(init.at[far1, pl.ds(0, 8)], 0, far1).wait_recv()

    lane = lax.broadcasted_iota(jnp.int32, (48, 128), 1)
    row = lax.broadcasted_iota(jnp.int32, (48, 128), 0)
    low_lanes = lane < 64
    is_root = low_lanes & (row < 32)
    is_mid = (low_lanes & (row >= 32)) | (~low_lanes & (row < 16))
    front = jnp.concatenate([init[0, 0:8], init[1, 0:8], init[2, 0:8], init[3, 0:8], init[half_base, 8:24]], axis=0)
    back = jnp.concatenate([init[half_base + 1, 8:24], own_ref[24:56, :]], axis=0)
    ipk = jnp.where(low_lanes, front, pltpu.roll(back, 64, 1))
    omega = jnp.where(low_lanes, pltpu.roll(front, 64, 1), back)

    def group_start(phase, src_of, dst):
        def one(d, carry):
            t = (j + d) % 16
            remote(src_of(t), dst, psend.at[phase, t], precv.at[phase, j], base + t, mode).start()
            return carry

        lax.fori_loop(1, 16, one, 0)

    def group_wait(phase, src_of, dst_of):
        def one(d, carry):
            t = (j + d) % 16
            copy = remote(src_of(t), dst_of(t), psend.at[phase, t], precv.at[phase, t], base + t, mode)
            copy.wait_recv()
            return carry

        lax.fori_loop(1, 16, one, 0)

    def group_sent(phase, src_of, dst):
        def one(d, carry):
            t = (j + d) % 16
            remote(src_of(t), dst, psend.at[phase, t], precv.at[phase, j], base + t, mode).wait_send()
            return carry

        lax.fori_loop(1, 16, one, 0)

    def to_chip(src, dst, phase, t):
        return remote(src, dst, hsend.at[phase, t], hrecv.at[phase, chip], base + 2 * t + core, mode)

    def from_chip(dst, phase, t):
        return remote(dst, dst, hsend.at[phase, t], hrecv.at[phase, t], base + 2 * t + core, mode)

    def to_core(src, dst, phase, slot):
        return remote(src, dst, xsend.at[phase, slot], xrecv.at[phase, slot], leaf + 1 - 2 * core, mode)

    def spread_start(s, values):
        ag[s, core, chip] = values
        mine = ag.at[s, core, chip]
        for t in reversed(chips):
            to_chip(mine, mine, s, t).start()
        to_core(mine, mine, s, chip).start()

    def unpack(s, c, t):
        block = ag[s, c, t]
        turned = pltpu.roll(block, 64, 1)
        n = 2 * t + c
        for k in range(4):
            iv[root_row(k, n) : root_row(k, n) + 8, :] = block[8 * k : 8 * k + 8]
        iv[mid_row(0, n) : mid_row(0, n) + 16, :] = block[32:48]
        iv[mid_row(1, n) : mid_row(1, n) + 16, :] = turned[0:16]
        iv[low_row(n) : low_row(n) + 32, :] = turned[16:48]

    def spread_wait(s):
        for t in chips:
            block = ag.at[s, core, t]
            from_chip(block, s, t).wait_recv()
            to_core(block, block, s, t).start()
        for t in [chip] + chips:
            block = ag.at[s, 1 - core, t]
            to_core(block, block, s, t).wait_recv()
        for c in range(2):
            for t in range(8):
                unpack(s, c, t)

    def reduce_start(phase, packed, landing):
        to_core(packed.at[1 - core], landing, phase, 0).start()

    def reduce_middle(phase, packed, landing, summed, arrived):
        to_core(packed.at[core], landing, phase, 0).wait_recv()
        summed[...] = packed[core] + landing[...]
        for t in reversed(chips):
            to_chip(summed.at[t], arrived.at[chip], phase, t).start()
        arrived[chip] = summed[chip]

    def reduce_end(phase, arrived):
        for t in chips:
            from_chip(arrived.at[t], phase, t).wait_recv()
        total = arrived[0]
        for t in range(1, 8):
            total = total + arrived[t]
        return total

    def reduce_sent(phase, packed, landing, summed, arrived):
        to_core(packed.at[1 - core], landing, phase, 0).wait_send()
        for t in chips:
            to_chip(summed.at[t], arrived.at[chip], phase, t).wait_send()

    spread_start(0, ipk)

    coord = lax.broadcasted_iota(jnp.int32, (1, 128), 1)
    live = jnp.concatenate([(coord < sizes_ref[n]).astype(F32) for n in range(4)], axis=1)
    stiff = stiff_ref[...]
    inverse = live / stiff
    m = leaf_ref[...] * live * SCALE

    weighted = inverse * inverse

    def split_chunk(c, h):
        ghi[c, h], glo[c, h] = halves(gt[c, h])

    def apply_chunk(c, h):
        first = pl.multiple_of(c * 384 + h * 128, 128)
        high, low = halves(iv[pl.ds(first, 128), :][:, 0:64].T)
        both = nn16(jnp.concatenate([high, low], axis=0), ghi[c, h])
        return both[0:64] + both[64:128] + nn16(high, glo[c, h])

    def mass_chunk(c, h):
        high, low = halves(gt[c, h] * weighted)
        own = jnp.concatenate([ghi[mode, h], glo[mode, h]], axis=0)
        both = nt16(high, own)
        ms[h, pl.ds(pl.multiple_of(c * 128, 128), 128), :] = (
            both[:, 0:128] + both[:, 128:256] + nt16(low, own[0:128])
        )

    for h in range(3):
        split_chunk(mode, h)
    spread_wait(0)
    coupled = apply_chunk(mode, 0) + apply_chunk(mode, 1) + apply_chunk(mode, 2)
    for h in range(3):
        chunk_in(h, 0).wait_recv()
        chunk(h, 2).start()
        chunk_in(h, 1).wait_recv()
        chunk(h, 3).start()
        for c in (left, right):
            split_chunk(c, h)
            coupled = coupled + apply_chunk(c, h)
            mass_chunk(c, h)
        mass_chunk(mode, h)
    for h in range(3):
        chunk_in(h, 2).wait_recv()
        chunk_in(h, 3).wait_recv()
        split_chunk(across, h)
        coupled = coupled + apply_chunk(across, h)
        if h < 2:
            mass_chunk(across, h)

    g2hi = ghi[...].reshape(1536, 512)
    g2lo = glo[...].reshape(1536, 512)
    for s in range(ITERS):
        if s > 0:
            spread_wait(s)
            high, low = halves(iv[:, 0:64].T)
            both = nn16(jnp.concatenate([high, low], axis=0), g2hi)
            coupled = both[0:64] + both[64:128] + nn16(high, g2lo)
        modal_mass = live * m - inverse * coupled
        m = inverse * modal_mass
        if s == ITERS - 1:
            yl[mode] = m
            for k, peer in enumerate((right, left, across)):
                remote(yl.at[mode], yl.at[mode], ysend.at[0, k], yrecv.at[0, k], leaf, peer).start()
        high, low = halves(m)
        twice = jnp.concatenate([high, high], axis=0)
        both = nt16(g2hi, jnp.concatenate([twice, low, low], axis=0))
        tt[...] = both[:, 0:128] + both[:, 128:256] + nt16(g2lo, twice)
        for t in range(16):
            a = jnp.concatenate(
                [tt[root_row(k, t) : root_row(k, t) + 8, :] for k in range(4)]
                + [tt[mid_row(0, t) : mid_row(0, t) + 16, :]],
                axis=0,
            )
            b = jnp.concatenate(
                [tt[mid_row(1, t) : mid_row(1, t) + 16, :], tt[low_row(t) : low_row(t) + 32, :]],
                axis=0,
            )
            tp[s, t % 2, t // 2] = jnp.where(low_lanes, a, b)
        reduce_start(3 + s, tp.at[s], xb.at[s])
        if s == 0:
            mass_chunk(across, 2)
            for t in range(16):
                for k in range(4):
                    mp[t % 2, t // 2, 8 * k : 8 * k + 8] = ms[0, 128 * k + 8 * t : 128 * k + 8 * t + 8]
                for k in range(2):
                    mp[t % 2, t // 2, 32 + 16 * k : 48 + 16 * k] = ms[1, 256 * k + 16 * t : 256 * k + 16 * t + 16]
                mp[t % 2, t // 2, 64:96] = ms[2, 32 * t : 32 * t + 32]
        reduce_middle(3 + s, tp.at[s], xb.at[s], xs.at[s], rs.at[s])
        if s == 0:
            reduce_start(6, mp, mxb)
        total = reduce_end(3 + s, rs.at[s])
        cs[s] = total
        rootpart = pl.ds(0, 32)
        quarter_copy(cs.at[s], cb.at[s, q], 1 + s, partner).start()
        quarter_copy(cs.at[s, rootpart], cb.at[s, q, rootpart], 1 + s, far0).start()
        quarter_copy(cs.at[s, rootpart], cb.at[s, q, rootpart], 1 + s, far1).start()
        if s == 0:
            reduce_middle(6, mp, mxb, mxs, mrs)
        quarter_in(cb.at[s, partner], 1 + s, partner).wait_recv()
        quarter_in(cb.at[s, far0, rootpart], 1 + s, far0).wait_recv()
        quarter_in(cb.at[s, far1, rootpart], 1 + s, far1).wait_recv()
        near = jnp.where(is_root | is_mid, cb[s, partner], 0.0)
        far = jnp.where(is_root[0:32], cb[s, far0, 0:32] + cb[s, far1, 0:32], 0.0)
        far = jnp.concatenate([far, jnp.zeros((16, 128), F32)], axis=0)
        ipk = (ipk - (total + near + far)) / omega
        if s < ITERS - 1:
            spread_start(s + 1, ipk)

    cs[3] = ipk
    cs[4] = omega
    own_vals = []
    for k in (3, 4):
        turned = pltpu.roll(cs[k], 64, 1)
        odd = (q % 2) == 1
        mids = jnp.where(odd, turned[0:16], cs[k, 32:48])
        own_vals.append(
            jnp.concatenate([cs[k, pl.ds(pl.multiple_of(8 * q, 8), 8)], mids, turned[16:48]], axis=0)
        )
    own_next, own_omega = own_vals
    iy[mode] = own_next
    for k, peer in enumerate((right, left, across)):
        remote(iy.at[mode], iy.at[mode], ysend.at[1, k], yrecv.at[1, k], leaf, peer).start()
    y_from = (left, right, across)
    for k in range(3):
        remote(yl.at[mode], yl.at[y_from[k]], ysend.at[0, k], yrecv.at[0, k], leaf, right).wait_recv()
    heavy = m * stiff
    blocks = [nt(yl[c], heavy) for c in range(4)]
    for k in range(3):
        remote(iy.at[mode], iy.at[y_from[k]], ysend.at[1, k], yrecv.at[1, k], leaf, right).wait_recv()
    heavy_own = (own_next * own_omega)[:, 0:64].T
    blocks = [(blocks[c] + nt(iy[c][:, 0:64].T, heavy_own)) * (1.0 / ROWS) for c in range(4)]
    gp[...] = jnp.concatenate(
        [jnp.concatenate(blocks[0:2], axis=0), jnp.concatenate(blocks[2:4], axis=0)], axis=1
    )

    def piece(t):
        return gp.at[pl.ds(pl.multiple_of(8 * t, 8), 8)]

    group_start(0, piece, grs.at[j])
    grs[j] = gp[pl.ds(pl.multiple_of(8 * j, 8), 8)]
    group_wait(0, piece, lambda t: grs.at[t])
    total = grs[0]
    for t in range(1, 16):
        total = total + grs[t]
    gc[q] = total
    for peer in (partner, far0, far1):
        quarter_copy(gc.at[q], gc.at[q], 4, peer).start()
    for peer in (partner, far0, far1):
        quarter_in(gc.at[peer], 4, peer).wait_recv()
    gag[j] = (gc[0] + gc[1]) + (gc[2] + gc[3])
    group_start(1, lambda t: gag.at[j], gag.at[j])

    total = reduce_end(6, mrs)
    ms[0, 0:96] = total
    mid_of = pl.ds(pl.multiple_of(32 + 16 * (q % 2), 8), 16)
    mid_to = pl.ds(pl.multiple_of(48 - 16 * (q % 2), 8), 16)

    def root_of(k):
        return pl.ds(pl.multiple_of(8 * k, 8), 8)

    for peer in (partner, far0, far1):
        quarter_copy(ms.at[0, root_of(peer)], mc.at[q, pl.ds(0, 8)], 5, peer).start()
    quarter_copy(ms.at[0, mid_to], mc.at[q, pl.ds(8, 16)], 6, partner).start()

    group_wait(1, lambda t: gag.at[j], lambda t: gag.at[t])
    gy[mode] = gag[...].reshape(128, 128)
    for k, peer in enumerate((right, left, across)):
        remote(gy.at[mode], gy.at[mode], ysend.at[2, k], yrecv.at[2, k], leaf, peer).start()

    for peer in (partner, far0, far1):
        quarter_in(mc.at[peer, pl.ds(0, 8)], 5, peer).wait_recv()
    quarter_in(mc.at[partner, pl.ds(8, 16)], 6, partner).wait_recv()

    def unit(first, count):
        rows = lax.broadcasted_iota(jnp.int32, (count, 128), 0) + first
        cols = lax.broadcasted_iota(jnp.int32, (count, 128), 1) + mode * 128
        return (rows % 512 == cols).astype(F32)

    mroot_ref[...] = (
        ms[0, root_of(q)] + (mc[partner, 0:8] + mc[far0, 0:8] + mc[far1, 0:8]) + unit(leaf * 8, 8)
    )
    mmid_ref[...] = ms[0, mid_of] + mc[partner, 8:24] + unit(leaf * 16, 16)
    mlow_ref[...] = ms[0, 64:96] + unit(leaf * 32, 32)
    next_ref[...] = yl[...].reshape(256, 512)
    iface_ref[...] = iy[...]

    for k in range(3):
        remote(gy.at[mode], gy.at[y_from[k]], ysend.at[2, k], yrecv.at[2, k], leaf, right).wait_recv()
    for c in range(4):
        part = gy[c]
        gram_ref[c, 0:128] = part[:, 0:64]
        gram_ref[c, 128:256] = pltpu.roll(part, 64, 1)[:, 0:64]

    for h in range(3):
        for kind in range(4):
            chunk(h, kind).wait_send()
    quarter_copy(init.at[q], init.at[q], 0, partner).wait_send()
    quarter_copy(init.at[q, pl.ds(0, 8)], init.at[q, pl.ds(0, 8)], 0, far0).wait_send()
    quarter_copy(init.at[q, pl.ds(0, 8)], init.at[q, pl.ds(0, 8)], 0, far1).wait_send()
    for s in range(ITERS):
        mine = ag.at[s, core, chip]
        for t in chips:
            to_chip(mine, mine, s, t).wait_send()
        for t in [chip] + chips:
            block = ag.at[s, core, t]
            to_core(block, block, s, t).wait_send()
        reduce_sent(3 + s, tp.at[s], xb.at[s], xs.at[s], rs.at[s])
        rootpart = pl.ds(0, 32)
        quarter_copy(cs.at[s], cb.at[s, q], 1 + s, partner).wait_send()
        quarter_copy(cs.at[s, rootpart], cb.at[s, q, rootpart], 1 + s, far0).wait_send()
        quarter_copy(cs.at[s, rootpart], cb.at[s, q, rootpart], 1 + s, far1).wait_send()
    reduce_sent(6, mp, mxb, mxs, mrs)
    group_sent(0, piece, grs.at[j])
    group_sent(1, lambda t: gag.at[j], gag.at[j])
    for peer in (partner, far0, far1):
        quarter_copy(gc.at[q], gc.at[q], 4, peer).wait_send()
        quarter_copy(ms.at[0, root_of(peer)], mc.at[q, pl.ds(0, 8)], 5, peer).wait_send()
    quarter_copy(ms.at[0, mid_to], mc.at[q, pl.ds(8, 16)], 6, partner).wait_send()
    for k, peer in enumerate((right, left, across)):
        remote(yl.at[mode], yl.at[mode], ysend.at[0, k], yrecv.at[0, k], leaf, peer).wait_send()
        remote(iy.at[mode], iy.at[mode], ysend.at[1, k], yrecv.at[1, k], leaf, peer).wait_send()
        remote(gy.at[mode], gy.at[mode], ysend.at[2, k], yrecv.at[2, k], leaf, peer).wait_send()


def run_sweeps(leaf_sizes, stiff, coupling, start_leaf, own):
    vmem = pl.BlockSpec(memory_space=pltpu.VMEM)
    scratch = [
        (4, 3, 128, 512),
        (4, 3, 128, 512),
        (4, 3, 128, 512),
        (4, 24, 128),
        (1536, 128),
        (1536, 128),
        (3, 2, 8, 48, 128),
        (3, 8, 48, 128),
        (3, 8, 48, 128),
        (3, 8, 48, 128),
        (5, 48, 128),
        (3, 4, 48, 128),
        (3, 2, 8, 48, 128),
        (4, 64, 512),
        (4, 56, 128),
        (128, 128),
        (16, 8, 128),
        (4, 8, 128),
        (16, 8, 128),
        (4, 128, 128),
        (2, 8, 96, 128),
        (8, 96, 128),
        (8, 96, 128),
        (8, 96, 128),
        (4, 24, 128),
        (3, 512, 128),
    ]
    sems = [(3, 4), (3, 4), (2, 16), (2, 16), (7, 8), (7, 8), (7, 8), (7, 8), (7, 4), (7, 4), (3, 3), (3, 3)]
    shapes = [(4, 256, 64), (256, 512), (4, 56, 128), (8, 128), (16, 128), (32, 128)]
    return pl.pallas_call(
        sweeps_kernel,
        out_shape=[jax.ShapeDtypeStruct(shape, F32) for shape in shapes],
        in_specs=[pl.BlockSpec(memory_space=pltpu.SMEM)] + [vmem] * 4,
        out_specs=[vmem] * 6,
        scratch_shapes=[pltpu.VMEM(shape, BF16 if n in (1, 2) else F32) for n, shape in enumerate(scratch)]
        + [pltpu.SemaphoreType.DMA(shape) for shape in sems],
        compiler_params=pltpu.CompilerParams(
            collective_id=0, has_side_effects=True, vmem_limit_bytes=48 * 1024 * 1024
        ),
        name="sweeps",
    )(leaf_sizes, stiff, coupling, start_leaf, own)


def factor_block(a):
    rows = [a[8 * r : 8 * r + 8, :] for r in range(8)]
    sub = lax.broadcasted_iota(jnp.int32, (8, 128), 0)
    pivots = []
    for p in range(8):
        cols = []
        for k in range(8):
            lane = 8 * p + k
            cols.append(
                [jnp.broadcast_to(rows[r][:, lane : lane + 1], (8, 128)) for r in range(p, 8)]
            )
        diag = []
        for k in range(8):
            pivot = jnp.broadcast_to(cols[k][0][k : k + 1, :], (8, 128))
            diag.append(pivot)
            scale = 1.0 / pivot
            factors = [c * scale for c in cols[k]]
            factors[0] = jnp.where(sub > k, factors[0], 0.0)
            for k2 in range(k + 1, 8):
                across = jnp.broadcast_to(cols[k2][0][k : k + 1, :], (8, 128))
                cols[k2] = [c - f * across for c, f in zip(cols[k2], factors)]
            lead = jnp.broadcast_to(rows[p][k : k + 1, :], (8, 128))
            for r in range(p, 8):
                rows[r] = rows[r] - factors[r - p] * lead
        scale = diag[0]
        for k in range(1, 8):
            scale = jnp.where(sub == k, diag[k], scale)
        pivots.append(lax.rsqrt(scale))
    return jnp.concatenate([row * pivot for row, pivot in zip(rows, pivots)], axis=0)


def finish_kernel(
    gram_ref, next_ref, iface_ref, mroot_ref, mmid_ref, mlow_ref,
    leaf_out, root_out, mid_out, low_out, mroot_out, mmid_out, mlow_out, full, lower
):
    mode = lax.axis_index("mode")
    mroot_out[...] = mroot_ref[...]
    mmid_out[...] = mmid_ref[...]
    mlow_out[...] = mlow_ref[...]
    gram = jnp.concatenate([gram_ref[c] for c in range(4)], axis=1)
    full[:, 0:256] = 0.5 * (gram + gram.T)
    r = lax.broadcasted_iota(jnp.int32, (256, 256), 0)
    c = lax.broadcasted_iota(jnp.int32, (256, 256), 1)
    full[:, 256:512] = (r == c).astype(F32)
    unit = (
        lax.broadcasted_iota(jnp.int32, (64, 64), 0) == lax.broadcasted_iota(jnp.int32, (64, 64), 1)
    ).astype(F32)
    for k in range(4):
        first = 64 * k
        block = full[first : first + 64, first : first + 64]
        weight = factor_block(jnp.concatenate([block, unit], axis=1))[:, 64:128]
        right = 128 * (k // 2)
        panel = nn(weight, full[first : first + 64, right:512])
        lower[first : first + 64, :] = panel[:, 256 - right : 512 - right]
        if k < 3:
            below = panel[:, first + 64 - right : 256 - right]
            full[first + 64 : 256, right:512] = full[first + 64 : 256, right:512] - tn(below, panel)
    own = lower[pl.ds(pl.multiple_of(mode * 64, 64), 64), :]
    leaf_out[...] = nn(own, next_ref[...])
    iface = jnp.concatenate([iface_ref[c][:, 0:64] for c in range(4)], axis=1)
    done = nt(own, iface)
    root_out[...] = done[:, 0:8]
    mid_out[...] = done[:, 8:24]
    low_out[...] = done[:, 24:56]


def run_finish(gram, modal, iface, masses):
    vmem = pl.BlockSpec(memory_space=pltpu.VMEM)
    shapes = [(64, 512), (64, 8), (64, 16), (64, 32), (8, 128), (16, 128), (32, 128)]
    return pl.pallas_call(
        finish_kernel,
        out_shape=[jax.ShapeDtypeStruct(shape, F32) for shape in shapes],
        in_specs=[vmem] * 6,
        out_specs=[vmem] * 7,
        scratch_shapes=[pltpu.VMEM((256, 512), F32), pltpu.VMEM((256, 256), F32)],
        compiler_params=pltpu.CompilerParams(vmem_limit_bytes=32 * 1024 * 1024),
        name="finish",
    )(gram, modal, iface, *masses)


def local(
    leaf_sizes,
    leaf_stiffness,
    coupling,
    omega_root,
    omega_mid,
    omega_low,
    start_leaf,
    start_root,
    start_mid,
    start_low,
):
    starts = jnp.concatenate([start_root, start_mid, start_low], axis=1).T * SCALE
    omegas = jnp.concatenate([omega_root, omega_mid, omega_low])
    own = jnp.concatenate([starts, jnp.broadcast_to(omegas[:, None], (56, 64))], axis=1)
    gram, modal, iface, *masses = run_sweeps(
        leaf_sizes, leaf_stiffness.reshape(1, -1), coupling, start_leaf, own
    )
    return tuple(run_finish(gram, modal, iface, masses))


def solution(mesh):
    placed = (
        P("leaf"),
        P("leaf"),
        P(None, "leaf", "mode"),
        P("leaf"),
        P("leaf"),
        P("leaf"),
        P("mode", "leaf"),
        P("mode", "leaf"),
        P("mode", "leaf"),
        P("mode", "leaf"),
    )
    return jax.shard_map(
        local,
        mesh=mesh,
        in_specs=placed,
        out_specs=(
            P("mode", "leaf"),
            P("mode", "leaf"),
            P("mode", "leaf"),
            P("mode", "leaf"),
            P("leaf", "mode"),
            P("leaf", "mode"),
            P("leaf", "mode"),
        ),
        check_vma=False,
    )
```

```python
import functools
import jax
import jax.numpy as jnp
from jax import lax
from jax.experimental import pallas as pl
from jax.experimental.pallas import tpu as pltpu
from jax.sharding import PartitionSpec as P

ITERS = 3
ROWS = 36352.0
SCALE = 2.0**-12
MESH = pl.DeviceIdType.MESH
HI = lax.Precision.HIGHEST
F32 = jnp.float32
BF16 = jnp.bfloat16
NEAR_FIRST = ((0, 1), (0, 3), (1, 0), (0, 2), (1, 1), (1, 3), (1, 2))


def nt(a, b):
    return lax.dot_general(a, b, (((1,), (1,)), ((), ())), precision=HI, preferred_element_type=F32)


def nn(a, b):
    return lax.dot_general(a, b, (((1,), (0,)), ((), ())), precision=HI, preferred_element_type=F32)


def tn(a, b):
    return lax.dot_general(a, b, (((0,), (0,)), ((), ())), precision=HI, preferred_element_type=F32)


def halves(x):
    high = x.astype(BF16)
    return high, (x - high.astype(F32)).astype(BF16)


def nn16(a, b):
    return lax.dot_general(a, b, (((1,), (0,)), ((), ())), preferred_element_type=F32)


def nt16(a, b):
    return lax.dot_general(a, b, (((1,), (1,)), ((), ())), preferred_element_type=F32)


def root_row(q, n):
    return q * 128 + 8 * n


def mid_row(half, n):
    return 512 + half * 256 + 16 * n


def low_row(n):
    return 1024 + 32 * n


def remote(src, dst, send, recv, leaf, mode):
    return pltpu.make_async_remote_copy(
        src_ref=src,
        dst_ref=dst,
        send_sem=send,
        recv_sem=recv,
        device_id=(leaf, mode),
        device_id_type=MESH,
    )


def column(ref):
    n = ref.shape[1]
    r = lax.broadcasted_iota(jnp.int32, (n, n), 0)
    c = lax.broadcasted_iota(jnp.int32, (n, n), 1)
    spread = jnp.where(r == c, jnp.broadcast_to(ref[...], (n, n)), 0.0)
    return jnp.broadcast_to(jnp.sum(spread, axis=1, keepdims=True), (n, 64))


def sweeps_kernel(
    sizes_ref,
    stiff_in,
    coupling_ref,
    leaf_in,
    sroot_in,
    smid_in,
    slow_in,
    oroot_in,
    omid_in,
    olow_in,
    gram_out,
    next_out,
    iface_out,
    mroot_out,
    mmid_out,
    mlow_out,
    gt,
    ghi,
    glo,
    raw,
    stiff_ref,
    leaf_ref,
    sroot_ref,
    smid_ref,
    slow_ref,
    oroot_ref,
    omid_ref,
    olow_ref,
    own,
    init,
    iv,
    tt,
    tp,
    rs,
    cs,
    cb,
    ag,
    fb,
    fr,
    yl,
    iy,
    gp,
    grs,
    gc,
    gag,
    iface_ref,
    mroot_ref,
    mmid_ref,
    mlow_ref,
    ms,
    mp,
    mxb,
    mxs,
    mrs,
    mc,
    lsem,
    osem,
    gsend,
    grecv,
    psend,
    precv,
    hsend,
    hrecv,
    xsend,
    xrecv,
    csend,
    crecv,
    ysend,
    yrecv,
    fsend,
    frecv,
):
    leaf = lax.axis_index("leaf")
    mode = lax.axis_index("mode")
    q = leaf // 16
    j = leaf % 16
    base = q * 16
    core = j % 2
    chip = j // 2
    chips = [((chip // 4 + dz) % 2) * 4 + (chip + dx) % 4 for dz, dx in NEAR_FIRST]
    right = (mode + 1) % 4
    left = (mode + 3) % 4
    across = (mode + 2) % 4
    modes = (right, left, across)
    partner = q + 1 - 2 * (q % 2)
    half_base = q - q % 2
    far0 = (q + 2) % 4
    far1 = (partner + 2) % 4
    quarters = (far0, far1, partner)

    loads = [pltpu.make_async_copy(coupling_ref.at[h], raw.at[h], lsem.at[h]) for h in range(3)]
    small = [
        (sroot_in, sroot_ref),
        (smid_in, smid_ref),
        (slow_in, slow_ref),
        (oroot_in, oroot_ref),
        (omid_in, omid_ref),
        (olow_in, olow_ref),
        (stiff_in, stiff_ref),
        (leaf_in, leaf_ref),
    ]
    loads += [pltpu.make_async_copy(a, b, lsem.at[3 + n]) for n, (a, b) in enumerate(small)]
    for load in loads:
        load.start()
    barrier = pltpu.get_barrier_semaphore()

    def greet_group(d, carry):
        pl.semaphore_signal(
            barrier, inc=1, device_id=(base + (j + d) % 16, mode), device_id_type=MESH
        )
        return carry

    for peer in modes:
        pl.semaphore_signal(barrier, inc=1, device_id=(leaf, peer), device_id_type=MESH)
    for peer in quarters:
        for d in range(4):
            pl.semaphore_signal(
                barrier, inc=1, device_id=(peer * 16 + j, (mode + d) % 4), device_id_type=MESH
            )
    lax.fori_loop(1, 16, greet_group, 0)
    for load in loads[3:]:
        load.wait()
    own[0:8] = jnp.concatenate([sroot_ref[...] * SCALE, column(oroot_ref)], axis=1)
    own[8:24] = jnp.concatenate([smid_ref[...] * SCALE, column(omid_ref)], axis=1)
    own[24:56] = jnp.concatenate([slow_ref[...] * SCALE, column(olow_ref)], axis=1)
    init[q] = own[0:24]
    for h in range(3):
        loads[h].wait()
        gt[h, mode] = raw[h].T
    pl.semaphore_wait(barrier, 30)

    def part(c, h, n):
        return gt.at[h, c, pl.ds(64 * n, 64)]

    def chunk(h, kind):
        c, n, peer = (
            (mode, 0, right),
            (mode, 1, left),
            (mode, 1, right),
            (mode, 0, left),
            (left, 0, right),
            (right, 1, left),
        )[kind]
        return remote(part(c, h, n), part(c, h, n), gsend.at[h, kind], grecv.at[h, kind], leaf, peer)

    def chunk_in(h, kind):
        c, n = ((left, 0), (right, 1), (left, 1), (right, 0), (across, 0), (across, 1))[kind]
        return remote(part(c, h, n), part(c, h, n), gsend.at[h, kind], grecv.at[h, kind], leaf, right)

    for kinds in ((0, 1), (2, 3)):
        for h in range(3):
            for kind in kinds:
                chunk(h, kind).start()

    def quarter_copy(src, dst, phase, peer):
        return remote(src, dst, csend.at[phase, peer], crecv.at[phase, q], peer * 16 + j, mode)

    def quarter_in(dst, phase, peer):
        return remote(dst, dst, csend.at[phase, peer], crecv.at[phase, peer], peer * 16 + j, mode)

    top = pl.ds(0, 8)
    init_out = [
        quarter_copy(init.at[q, top], init.at[q, top], 0, far0),
        quarter_copy(init.at[q, top], init.at[q, top], 0, far1),
        quarter_copy(init.at[q], init.at[q], 0, partner),
    ]
    for copy in init_out:
        copy.start()
    quarter_in(init.at[partner], 0, partner).wait_recv()
    quarter_in(init.at[far0, top], 0, far0).wait_recv()
    quarter_in(init.at[far1, top], 0, far1).wait_recv()

    low_lanes = lax.broadcasted_iota(jnp.int32, (16, 128), 1) < 64

    def packs(a, b):
        return (
            jnp.where(low_lanes, a, pltpu.roll(b, 64, 1)),
            jnp.where(low_lanes, pltpu.roll(a, 64, 1), b),
        )

    iroot, wroot = packs(
        jnp.concatenate([init[0, 0:8], init[1, 0:8]], axis=0),
        jnp.concatenate([init[2, 0:8], init[3, 0:8]], axis=0),
    )
    imid, wmid = packs(init[half_base, 8:24], init[half_base + 1, 8:24])
    ilow, wlow = packs(own[24:40], own[40:56])
    state = [iroot, imid, ilow]
    omega = [wroot, wmid, wlow]

    def group_start(phase, src_of, dst):
        def one(d, carry):
            t = (j + d) % 16
            remote(src_of(t), dst, psend.at[phase], precv.at[phase], base + t, mode).start()
            return carry

        lax.fori_loop(1, 16, one, 0)

    def group_all(phase, landing):
        some = landing.at[pl.ds(0, 15)]
        return remote(some, some, psend.at[phase], precv.at[phase], base + (j + 1) % 16, mode)

    def spread_start(s, h):
        ag[s, h, j] = state[h]
        group_start(3 * s + h, lambda t: ag.at[s, h, j], ag.at[s, h, j])

    def spread_wait(s, h):
        group_all(3 * s + h, ag.at[s, h]).wait_recv()
        for n in range(16):
            block = ag[s, h, n]
            turned = pltpu.roll(block, 64, 1)
            if h == 0:
                for k in range(2):
                    iv[root_row(k, n) : root_row(k, n) + 8, :] = block[8 * k : 8 * k + 8]
                    iv[root_row(k + 2, n) : root_row(k + 2, n) + 8, :] = turned[8 * k : 8 * k + 8]
            elif h == 1:
                iv[mid_row(0, n) : mid_row(0, n) + 16, :] = block
                iv[mid_row(1, n) : mid_row(1, n) + 16, :] = turned
            else:
                iv[low_row(n) : low_row(n) + 16, :] = block
                iv[low_row(n) + 16 : low_row(n) + 32, :] = turned

    def pack_terms(s, h):
        for n in range(16):
            if h == 0:
                a, b = [
                    jnp.concatenate(
                        [tt[root_row(k, n) : root_row(k, n) + 8], tt[root_row(k + 1, n) : root_row(k + 1, n) + 8]],
                        axis=0,
                    )
                    for k in (0, 2)
                ]
            elif h == 1:
                a, b = [tt[mid_row(k, n) : mid_row(k, n) + 16] for k in range(2)]
            else:
                a, b = tt[low_row(n) : low_row(n) + 16], tt[low_row(n) + 16 : low_row(n) + 32]
            tp[s, h, n] = jnp.where(low_lanes, a, b)

    def reduce_start(s, h):
        group_start(9 + 3 * s + h, lambda t: tp.at[s, h, t], rs.at[s, h, j])
        rs[s, h, j] = tp[s, h, j]

    def reduce_end(s, h):
        group_all(9 + 3 * s + h, rs.at[s, h]).wait_recv()
        total = rs[s, h, 0]
        for n in range(1, 16):
            total = total + rs[s, h, n]
        return total

    for h in range(3):
        spread_start(0, h)

    coord = lax.broadcasted_iota(jnp.int32, (1, 128), 1)
    live = jnp.concatenate([(coord < sizes_ref[n]).astype(F32) for n in range(4)], axis=1)
    stiff = stiff_ref[...]
    inverse = live / stiff
    weighted = inverse * inverse
    m = leaf_ref[...] * live * SCALE

    def split_chunk(c, h):
        ghi[h, c], glo[h, c] = halves(gt[h, c])

    def apply_chunk(c, h):
        first = pl.multiple_of(h * 512 + c * 128, 128)
        high, low = halves(iv[pl.ds(first, 128), :][:, 0:64].T)
        both = nn16(jnp.concatenate([high, low], axis=0), ghi[h, c])
        return both[0:64] + both[64:128] + nn16(high, glo[h, c])

    def mass_chunk(c, h):
        high, low = halves(gt[h, c] * weighted)
        mine = jnp.concatenate([ghi[h, mode], glo[h, mode]], axis=0)
        both = nt16(high, mine)
        ms[h, pl.ds(pl.multiple_of(c * 128, 128), 128), :] = (
            both[:, 0:128] + both[:, 128:256] + nt16(low, mine[0:128])
        )

    for h in range(3):
        for kind in (0, 1):
            chunk_in(h, kind).wait_recv()
            chunk(h, kind + 4).start()
        split_chunk(mode, h)
    for h in range(3):
        spread_wait(0, h)
    coupled = apply_chunk(mode, 0) + apply_chunk(mode, 1) + apply_chunk(mode, 2)
    for h in range(3):
        chunk_in(h, 2).wait_recv()
        chunk_in(h, 3).wait_recv()
        for c in (left, right):
            split_chunk(c, h)
            coupled = coupled + apply_chunk(c, h)
            mass_chunk(c, h)
        mass_chunk(mode, h)
    for h in range(3):
        chunk_in(h, 4).wait_recv()
        chunk_in(h, 5).wait_recv()
        split_chunk(across, h)
        coupled = coupled + apply_chunk(across, h)

    def to_chip(src, dst, phase, t):
        return remote(src, dst, hsend.at[phase, t], hrecv.at[phase, chip], base + 2 * t + core, mode)

    def from_chip(dst, phase, t):
        return remote(dst, dst, hsend.at[phase, t], hrecv.at[phase, t], base + 2 * t + core, mode)

    mass_core = remote(mp.at[1 - core], mxb, xsend.at[0], xrecv.at[0], leaf + 1 - 2 * core, mode)

    def pack_masses():
        for t in range(16):
            for k in range(4):
                mp[t % 2, t // 2, 8 * k : 8 * k + 8] = ms[0, 128 * k + 8 * t : 128 * k + 8 * t + 8]
            for k in range(2):
                mp[t % 2, t // 2, 32 + 16 * k : 48 + 16 * k] = ms[
                    1, 256 * k + 16 * t : 256 * k + 16 * t + 16
                ]
            mp[t % 2, t // 2, 64:96] = ms[2, 32 * t : 32 * t + 32]

    def y_copy(ref, phase, k):
        return remote(ref.at[mode], ref.at[mode], ysend.at[phase, k], yrecv.at[phase, k], leaf, modes[k])

    def y_in(ref, phase, k):
        came = ref.at[(left, right, across)[k]]
        return remote(came, came, ysend.at[phase, k], yrecv.at[phase, k], leaf, right)

    for s in range(ITERS):
        last = s == ITERS - 1
        if s > 0:
            coupled = jnp.zeros((64, 512), F32)
            for h in (2, 1, 0):
                spread_wait(s, h)
                high, low = halves(iv[512 * h : 512 * h + 512, :][:, 0:64].T)
                both = nn16(jnp.concatenate([high, low], axis=0), ghi[h].reshape(512, 512))
                coupled = coupled + (both[0:64] + both[64:128] + nn16(high, glo[h].reshape(512, 512)))
        modal_mass = live * m - inverse * coupled
        m = inverse * modal_mass
        high, low = halves(m)
        twice = jnp.concatenate([high, high], axis=0)
        four = jnp.concatenate([twice, low, low], axis=0)
        for h in range(3):
            both = nt16(ghi[h].reshape(512, 512), four)
            tt[512 * h : 512 * h + 512, :] = (
                both[:, 0:128] + both[:, 128:256] + nt16(glo[h].reshape(512, 512), twice)
            )
            pack_terms(s, h)
            reduce_start(s, h)
        if last:
            yl[mode] = m
            for k in range(3):
                y_copy(yl, 0, k).start()
        if s == 0:
            for h in range(3):
                mass_chunk(across, h)
            pack_masses()
            mass_core.start()
        if last:
            heavy = m * stiff
            break
        cs[s, 0] = reduce_end(s, 0)
        for peer in (far0, far1, partner):
            quarter_copy(cs.at[s, 0], cb.at[s, 0, q], 1 + s, peer).start()
        cs[s, 1] = reduce_end(s, 1)
        quarter_copy(cs.at[s, 1], cb.at[s, 1, q], 3 + s, partner).start()
        state[2] = (state[2] - reduce_end(s, 2)) / omega[2]
        spread_start(s + 1, 2)
        if s == 0:
            mass_core.wait_recv()
            mxs[...] = mp[core] + mxb[...]
            for t in reversed(chips):
                to_chip(mxs.at[t], mrs.at[chip], 0, t).start()
            mrs[chip] = mxs[chip]
        for peer in (partner, far0, far1):
            quarter_in(cb.at[s, 0, peer], 1 + s, peer).wait_recv()
        gone = (cs[s, 0] + cb[s, 0, partner]) + (cb[s, 0, far0] + cb[s, 0, far1])
        state[0] = (state[0] - gone) / omega[0]
        spread_start(s + 1, 0)
        quarter_in(cb.at[s, 1, partner], 3 + s, partner).wait_recv()
        state[1] = (state[1] - (cs[s, 1] + cb[s, 1, partner])) / omega[1]
        spread_start(s + 1, 1)
        if s == ITERS - 2:
            gp[0:16] = state[0]
            gp[16:32] = pltpu.roll(state[0], 64, 1)
            piece = pl.multiple_of(16 * (q // 2) + 8 * (q % 2), 8)
            iy[mode, 0:8] = gp[pl.ds(piece, 8)]
            odd = (q % 2) == 1
            iy[mode, 8:24] = jnp.where(odd, pltpu.roll(state[1], 64, 1), state[1])
            iy[mode, 24:40] = state[2]
            iy[mode, 40:56] = pltpu.roll(state[2], 64, 1)
            for k in range(3):
                y_copy(iy, 1, k).start()

    total = reduce_end(ITERS - 1, 0)
    turned = pltpu.roll(total, 64, 1)
    for k in range(2):
        fb[k, 0:8] = total[8 * k : 8 * k + 8]
        fb[k + 2, 0:8] = turned[8 * k : 8 * k + 8]

    def owner_copy(peer, d, rows):
        rows = pl.ds(0, rows)
        to = (mode + d) % 4
        return remote(
            fb.at[peer, rows], fr.at[mode, q, rows], fsend.at[peer, to], frecv.at[q, mode], peer * 16 + j, to
        )

    def owner_in(peer, c, rows):
        ref = fr.at[c, peer, pl.ds(0, rows)]
        return remote(ref, ref, fsend.at[peer, c], frecv.at[peer, c], peer * 16 + j, right)

    for peer in (far0, far1):
        for d in (2, 1, 3, 0):
            owner_copy(peer, d, 8).start()
    total = reduce_end(ITERS - 1, 1)
    turned = pltpu.roll(total, 64, 1)
    odd = (q % 2) == 1
    fb[q, 8:24] = jnp.where(odd, turned, total)
    fb[partner, 8:24] = jnp.where(odd, total, turned)
    for d in (2, 1, 3, 0):
        owner_copy(partner, d, 24).start()
    total = reduce_end(ITERS - 1, 2)
    fb[q, 24:40] = total
    fb[q, 40:56] = pltpu.roll(total, 64, 1)
    for d in (2, 1, 3):
        owner_copy(q, d, 56).start()
    fr[mode, q] = fb[q]

    for k in range(3):
        y_in(yl, 0, k).wait_recv()
        y_in(iy, 1, k).wait_recv()
    blocks = [nt(yl[c], heavy) for c in range(4)]
    results = [
        pltpu.make_async_copy(a, b, osem.at[n])
        for n, (a, b) in enumerate(
            (
                (yl, next_out),
                (iface_ref, iface_out),
                (mroot_ref, mroot_out),
                (mmid_ref, mmid_out),
                (mlow_ref, mlow_out),
                (gag, gram_out),
            )
        )
    ]
    results[0].start()
    for peer in (far0, far1):
        for d in range(4):
            owner_in(peer, (mode + d) % 4, 8).wait_recv()
    for d in range(4):
        owner_in(partner, (mode + d) % 4, 24).wait_recv()
    for d in range(1, 4):
        owner_in(q, (mode + d) % 4, 56).wait_recv()
    weights = pltpu.roll(own[...], 64, 1)
    for c in range(4):
        near = fr[c, q, 0:24] + fr[c, partner, 0:24]
        near = jnp.concatenate(
            [near[0:8] + (fr[c, far0, 0:8] + fr[c, far1, 0:8]), near[8:24], fr[c, q, 24:56]], axis=0
        )
        iface_ref[c] = (iy[c] - near) / weights
    results[1].start()
    heavy_own = (iface_ref[mode] * weights)[:, 0:64].T
    blocks = [
        (blocks[c] + nt(iface_ref[c][:, 0:64].T, heavy_own)) * (1.0 / ROWS) for c in range(4)
    ]
    gp[...] = jnp.concatenate(
        [jnp.concatenate(blocks[0:2], axis=0), jnp.concatenate(blocks[2:4], axis=0)], axis=1
    )

    def rows8(t):
        return pl.ds(pl.multiple_of(8 * t, 8), 8)

    group_start(18, lambda t: gp.at[rows8(t)], grs.at[j])
    grs[j] = gp[rows8(j)]
    for t in chips:
        from_chip(mrs.at[t], 0, t).wait_recv()
    total = mrs[0]
    for t in range(1, 8):
        total = total + mrs[t]
    ms[0, 0:96] = total
    mid_of = pl.ds(pl.multiple_of(32 + 16 * (q % 2), 8), 16)
    mid_to = pl.ds(pl.multiple_of(48 - 16 * (q % 2), 8), 16)
    mass_out = [quarter_copy(ms.at[0, rows8(k)], mc.at[q, top], 5, k) for k in quarters]
    mass_out.append(quarter_copy(ms.at[0, mid_to], mc.at[q, pl.ds(8, 16)], 6, partner))
    for copy in mass_out:
        copy.start()

    group_all(18, grs).wait_recv()
    total = grs[0]
    for t in range(1, 16):
        total = total + grs[t]
    gc[mode, q] = total

    def gram_copy(peer, d):
        to = (mode + d) % 4
        ref = gc.at[mode, q]
        return remote(ref, ref, fsend.at[peer + 4, to], frecv.at[q + 4, mode], peer * 16 + j, to)

    def gram_in(peer, c):
        ref = gc.at[c, peer]
        return remote(ref, ref, fsend.at[peer + 4, c], frecv.at[peer + 4, c], peer * 16 + j, right)

    for peer in quarters:
        for d in (2, 1, 3, 0):
            gram_copy(peer, d).start()
    for d in (2, 1, 3):
        gram_copy(q, d).start()

    for peer in quarters:
        quarter_in(mc.at[peer, top], 5, peer).wait_recv()
    quarter_in(mc.at[partner, pl.ds(8, 16)], 6, partner).wait_recv()

    def unit(first, count):
        rows = lax.broadcasted_iota(jnp.int32, (count, 128), 0) + first
        cols = lax.broadcasted_iota(jnp.int32, (count, 128), 1) + mode * 128
        return (rows % 512 == cols).astype(F32)

    mroot_ref[...] = (
        ms[0, rows8(q)] + (mc[partner, 0:8] + mc[far0, 0:8] + mc[far1, 0:8]) + unit(leaf * 8, 8)
    )
    mmid_ref[...] = ms[0, mid_of] + mc[partner, 8:24] + unit(leaf * 16, 16)
    mlow_ref[...] = ms[0, 64:96] + unit(leaf * 32, 32)
    for result in results[2:5]:
        result.start()
    for h in range(3):
        for kind in range(6):
            chunk(h, kind).wait_send()
    for copy in init_out:
        copy.wait_send()
    for s in range(ITERS):
        for h in range(3):
            group_all(3 * s + h, ag.at[s, h]).wait_send()
            group_all(9 + 3 * s + h, rs.at[s, h]).wait_send()
    for s in range(ITERS - 1):
        for peer in quarters:
            quarter_copy(cs.at[s, 0], cb.at[s, 0, q], 1 + s, peer).wait_send()
        quarter_copy(cs.at[s, 1], cb.at[s, 1, q], 3 + s, partner).wait_send()
    mass_core.wait_send()
    for t in chips:
        to_chip(mxs.at[t], mrs.at[chip], 0, t).wait_send()
    for k in range(3):
        y_copy(yl, 0, k).wait_send()
        y_copy(iy, 1, k).wait_send()

    for peer in quarters:
        for d in range(4):
            gram_in(peer, (mode + d) % 4).wait_recv()
    for d in range(1, 4):
        gram_in(q, (mode + d) % 4).wait_recv()
    for c in range(4):
        gag[j, c] = (gc[c, 0] + gc[c, 1]) + (gc[c, 2] + gc[c, 3])
    group_start(19, lambda t: gag.at[j], gag.at[j])
    for d in range(4):
        for peer in (far0, far1):
            owner_copy(peer, d, 8).wait_send()
        owner_copy(partner, d, 24).wait_send()
        if d > 0:
            owner_copy(q, d, 56).wait_send()
            gram_copy(q, d).wait_send()
        for peer in quarters:
            gram_copy(peer, d).wait_send()
    for copy in mass_out:
        copy.wait_send()
    group_all(18, grs).wait_send()
    group_all(19, gag).wait_recv()
    results[5].start()
    group_all(19, gag).wait_send()
    for result in results:
        result.wait()


def run_sweeps(leaf_sizes, stiff, coupling, start_leaf, starts, omegas):
    scratch = [
        (3, 4, 128, 512),
        (3, 4, 128, 512),
        (3, 4, 128, 512),
        (3, 512, 128),
        (1, 512),
        (64, 512),
        (8, 64),
        (16, 64),
        (32, 64),
        (1, 8),
        (1, 16),
        (1, 32),
        (56, 128),
        (4, 24, 128),
        (1536, 128),
        (1536, 128),
        (3, 3, 16, 16, 128),
        (3, 3, 16, 16, 128),
        (2, 2, 16, 128),
        (2, 2, 4, 16, 128),
        (3, 3, 16, 16, 128),
        (4, 56, 128),
        (4, 4, 56, 128),
        (4, 64, 512),
        (4, 56, 128),
        (128, 128),
        (16, 8, 128),
        (4, 4, 8, 128),
        (16, 4, 8, 128),
        (4, 56, 128),
        (8, 128),
        (16, 128),
        (32, 128),
        (3, 512, 128),
        (2, 8, 96, 128),
        (8, 96, 128),
        (8, 96, 128),
        (8, 96, 128),
        (4, 24, 128),
    ]
    sems = [(11,), (6,), (3, 6), (3, 6), (20,), (20,), (1, 8), (1, 8), (1,), (1,)]
    sems += [(7, 4), (7, 4), (2, 3), (2, 3), (8, 4), (8, 4)]
    shapes = [(16, 4, 8, 128), (4, 64, 512), (4, 56, 128), (8, 128), (16, 128), (32, 128)]
    return pl.pallas_call(
        sweeps_kernel,
        out_shape=[jax.ShapeDtypeStruct(shape, F32) for shape in shapes],
        in_specs=[pl.BlockSpec(memory_space=pltpu.SMEM)]
        + [pl.BlockSpec(memory_space=pltpu.HBM)] * 9,
        out_specs=[pl.BlockSpec(memory_space=pltpu.HBM)] * 6,
        scratch_shapes=[
            pltpu.VMEM(shape, BF16 if n in (1, 2) else F32) for n, shape in enumerate(scratch)
        ]
        + [pltpu.SemaphoreType.DMA(shape) for shape in sems],
        compiler_params=pltpu.CompilerParams(
            collective_id=0, has_side_effects=True, vmem_limit_bytes=64 * 1024 * 1024
        ),
        name="sweeps",
    )(leaf_sizes, stiff, coupling, start_leaf, *starts, *omegas)


def factor_block(a):
    rows = [a[8 * r : 8 * r + 8, :] for r in range(8)]
    sub = lax.broadcasted_iota(jnp.int32, (8, 128), 0)
    pivots = []
    for p in range(8):
        cols = []
        for k in range(8):
            lane = 8 * p + k
            cols.append(
                [jnp.broadcast_to(rows[r][:, lane : lane + 1], (8, 128)) for r in range(p, 8)]
            )
        diag = []
        for k in range(8):
            pivot = jnp.broadcast_to(cols[k][0][k : k + 1, :], (8, 128))
            diag.append(pivot)
            scale = 1.0 / pivot
            factors = [c * scale for c in cols[k]]
            factors[0] = jnp.where(sub > k, factors[0], 0.0)
            for k2 in range(k + 1, 8):
                across = jnp.broadcast_to(cols[k2][0][k : k + 1, :], (8, 128))
                cols[k2] = [c - f * across for c, f in zip(cols[k2], factors)]
            lead = jnp.broadcast_to(rows[p][k : k + 1, :], (8, 128))
            for r in range(p, 8):
                rows[r] = rows[r] - factors[r - p] * lead
        scale = diag[0]
        for k in range(1, 8):
            scale = jnp.where(sub == k, diag[k], scale)
        pivots.append(lax.rsqrt(scale))
    return jnp.concatenate([row * pivot for row, pivot in zip(rows, pivots)], axis=0)


def finish_kernel(
    gram_in,
    next_in,
    iface_in,
    mroot_in,
    mmid_in,
    mlow_in,
    leaf_out,
    root_out,
    mid_out,
    low_out,
    mroot_out,
    mmid_out,
    mlow_out,
    gram_ref,
    next_ref,
    iface_ref,
    full,
    lower,
    sem,
):
    mode = lax.axis_index("mode")
    moves = (
        (gram_in, gram_ref),
        (next_in, next_ref),
        (iface_in, iface_ref),
        (mroot_in, mroot_out),
        (mmid_in, mmid_out),
        (mlow_in, mlow_out),
    )
    moves = [pltpu.make_async_copy(a, b, sem.at[n]) for n, (a, b) in enumerate(moves)]
    for move in moves:
        move.start()
    moves[0].wait()
    low_lanes = lax.broadcasted_iota(jnp.int32, (128, 128), 1) < 64
    parts = [jnp.concatenate([gram_ref[t, c] for t in range(16)], axis=0) for c in range(4)]
    turned = [pltpu.roll(part, 64, 1) for part in parts]
    gram = jnp.concatenate(
        [
            jnp.concatenate([jnp.where(low_lanes, parts[c], turned[c + 1]) for c in (0, 2)], axis=1),
            jnp.concatenate([jnp.where(low_lanes, turned[c], parts[c + 1]) for c in (0, 2)], axis=1),
        ],
        axis=0,
    )
    full[:, 0:256] = 0.5 * (gram + gram.T)
    r = lax.broadcasted_iota(jnp.int32, (256, 256), 0)
    c = lax.broadcasted_iota(jnp.int32, (256, 256), 1)
    full[:, 256:512] = (r == c).astype(F32)
    unit = (
        lax.broadcasted_iota(jnp.int32, (64, 64), 0) == lax.broadcasted_iota(jnp.int32, (64, 64), 1)
    ).astype(F32)
    for k in range(4):
        first = 64 * k
        block = full[first : first + 64, first : first + 64]
        weight = factor_block(jnp.concatenate([block, unit], axis=1))[:, 64:128]
        right = 128 * (k // 2)
        panel = nn(weight, full[first : first + 64, right:512])
        lower[first : first + 64, :] = panel[:, 256 - right : 512 - right]
        if k < 3:
            below = panel[:, first + 64 - right : 256 - right]
            full[first + 64 : 256, right:512] = full[first + 64 : 256, right:512] - tn(below, panel)
    own = lower[pl.ds(pl.multiple_of(mode * 64, 64), 64), :]
    for move in moves[1:]:
        move.wait()
    leaf_out[...] = nn(own, next_ref[...].reshape(256, 512))
    iface = jnp.concatenate([iface_ref[c][:, 0:64] for c in range(4)], axis=1)
    done = nt(iface, own)
    root_out[...] = done[0:8]
    mid_out[...] = done[8:24]
    low_out[...] = done[24:56]


def run_finish(gram, modal, iface, masses):
    vmem = pl.BlockSpec(memory_space=pltpu.VMEM)
    hbm = pl.BlockSpec(memory_space=pltpu.HBM)
    shapes = [(64, 512), (8, 64), (16, 64), (32, 64), (8, 128), (16, 128), (32, 128)]
    return pl.pallas_call(
        finish_kernel,
        out_shape=[jax.ShapeDtypeStruct(shape, F32) for shape in shapes],
        in_specs=[hbm] * 6,
        out_specs=[vmem] * 4 + [hbm] * 3,
        scratch_shapes=[
            pltpu.VMEM((16, 4, 8, 128), F32),
            pltpu.VMEM((4, 64, 512), F32),
            pltpu.VMEM((4, 56, 128), F32),
            pltpu.VMEM((256, 512), F32),
            pltpu.VMEM((256, 256), F32),
            pltpu.SemaphoreType.DMA((6,)),
        ],
        compiler_params=pltpu.CompilerParams(vmem_limit_bytes=64 * 1024 * 1024),
        name="finish",
    )(gram, modal, iface, *masses)


def local(
    leaf_sizes,
    leaf_stiffness,
    coupling,
    omega_root,
    omega_mid,
    omega_low,
    start_leaf,
    start_root,
    start_mid,
    start_low,
):
    gram, modal, iface, *masses = run_sweeps(
        leaf_sizes,
        leaf_stiffness.reshape(1, -1),
        coupling,
        start_leaf,
        [start_root.T, start_mid.T, start_low.T],
        [omega_root.reshape(1, -1), omega_mid.reshape(1, -1), omega_low.reshape(1, -1)],
    )
    leaf, root, mid, low, *masses = run_finish(gram, modal, iface, masses)
    return (leaf, root.T, mid.T, low.T, *masses)


def solution(mesh):
    placed = (
        P("leaf"),
        P("leaf"),
        P(None, "leaf", "mode"),
        P("leaf"),
        P("leaf"),
        P("leaf"),
        P("mode", "leaf"),
        P("mode", "leaf"),
        P("mode", "leaf"),
        P("mode", "leaf"),
    )
    return jax.shard_map(
        local,
        mesh=mesh,
        in_specs=placed,
        out_specs=(
            P("mode", "leaf"),
            P("mode", "leaf"),
            P("mode", "leaf"),
            P("mode", "leaf"),
            P("leaf", "mode"),
            P("leaf", "mode"),
            P("leaf", "mode"),
        ),
        check_vma=False,
    )
```

```python
import functools
import jax
import jax.numpy as jnp
from jax import lax
from jax.experimental import pallas as pl
from jax.experimental.pallas import tpu as pltpu
from jax.sharding import PartitionSpec as P

ITERS = 3
ROWS = 36352.0
SCALE = 2.0**-12
MESH = pl.DeviceIdType.MESH
HI = lax.Precision.HIGHEST
F32 = jnp.float32
BF16 = jnp.bfloat16
NEAR_FIRST = ((0, 1), (0, 3), (1, 0), (0, 2), (1, 1), (1, 3), (1, 2))


def nt(a, b):
    return lax.dot_general(a, b, (((1,), (1,)), ((), ())), precision=HI, preferred_element_type=F32)


def nn(a, b):
    return lax.dot_general(a, b, (((1,), (0,)), ((), ())), precision=HI, preferred_element_type=F32)


def tn(a, b):
    return lax.dot_general(a, b, (((0,), (0,)), ((), ())), precision=HI, preferred_element_type=F32)


def halves(x):
    high = x.astype(BF16)
    return high, (x - high.astype(F32)).astype(BF16)


def nn16(a, b):
    return lax.dot_general(a, b, (((1,), (0,)), ((), ())), preferred_element_type=F32)


def nt16(a, b):
    return lax.dot_general(a, b, (((1,), (1,)), ((), ())), preferred_element_type=F32)


def root_row(q, n):
    return q * 128 + 8 * n


def mid_row(half, n):
    return 512 + half * 256 + 16 * n


def low_row(n):
    return 1024 + 32 * n


def remote(src, dst, send, recv, leaf, mode):
    return pltpu.make_async_remote_copy(
        src_ref=src,
        dst_ref=dst,
        send_sem=send,
        recv_sem=recv,
        device_id=(leaf, mode),
        device_id_type=MESH,
    )


def column(ref):
    n = ref.shape[1]
    r = lax.broadcasted_iota(jnp.int32, (n, n), 0)
    c = lax.broadcasted_iota(jnp.int32, (n, n), 1)
    spread = jnp.where(r == c, jnp.broadcast_to(ref[...], (n, n)), 0.0)
    return jnp.broadcast_to(jnp.sum(spread, axis=1, keepdims=True), (n, 64))


def sweeps_kernel(
    sizes_ref,
    stiff_in,
    coupling_ref,
    leaf_in,
    sroot_in,
    smid_in,
    slow_in,
    oroot_in,
    omid_in,
    olow_in,
    gram_out,
    next_out,
    iface_out,
    mroot_out,
    mmid_out,
    mlow_out,
    gt,
    ghi,
    glo,
    raw,
    stiff_ref,
    leaf_ref,
    sroot_ref,
    smid_ref,
    slow_ref,
    oroot_ref,
    omid_ref,
    olow_ref,
    own,
    init,
    iv,
    tt,
    tp,
    xb,
    xs,
    rs,
    cs,
    cb,
    ag,
    fb,
    fr,
    yl,
    iy,
    gp,
    grs,
    gc,
    gag,
    iface_ref,
    mroot_ref,
    mmid_ref,
    mlow_ref,
    ms,
    mp,
    mxb,
    mxs,
    mrs,
    mc,
    lsem,
    osem,
    gsend,
    grecv,
    psend,
    precv,
    hsend,
    hrecv,
    xsend,
    xrecv,
    csend,
    crecv,
    ysend,
    yrecv,
    fsend,
    frecv,
):
    leaf = lax.axis_index("leaf")
    mode = lax.axis_index("mode")
    q = leaf // 16
    j = leaf % 16
    base = q * 16
    core = j % 2
    chip = j // 2
    chips = [((chip // 4 + dz) % 2) * 4 + (chip + dx) % 4 for dz, dx in NEAR_FIRST]
    right = (mode + 1) % 4
    left = (mode + 3) % 4
    across = (mode + 2) % 4
    modes = (right, left, across)
    partner = q + 1 - 2 * (q % 2)
    half_base = q - q % 2
    far0 = (q + 2) % 4
    far1 = (partner + 2) % 4
    quarters = (far0, far1, partner)

    loads = [pltpu.make_async_copy(coupling_ref.at[h], raw.at[h], lsem.at[h]) for h in range(3)]
    small = [
        (sroot_in, sroot_ref),
        (smid_in, smid_ref),
        (slow_in, slow_ref),
        (oroot_in, oroot_ref),
        (omid_in, omid_ref),
        (olow_in, olow_ref),
        (stiff_in, stiff_ref),
        (leaf_in, leaf_ref),
    ]
    loads += [pltpu.make_async_copy(a, b, lsem.at[3 + n]) for n, (a, b) in enumerate(small)]
    for load in loads:
        load.start()
    barrier = pltpu.get_barrier_semaphore()

    def greet_group(d, carry):
        pl.semaphore_signal(
            barrier, inc=1, device_id=(base + (j + d) % 16, mode), device_id_type=MESH
        )
        return carry

    for peer in modes:
        pl.semaphore_signal(barrier, inc=1, device_id=(leaf, peer), device_id_type=MESH)
    for peer in quarters:
        for d in range(4):
            pl.semaphore_signal(
                barrier, inc=1, device_id=(peer * 16 + j, (mode + d) % 4), device_id_type=MESH
            )
    lax.fori_loop(1, 16, greet_group, 0)
    for load in loads[3:]:
        load.wait()
    own[0:8] = jnp.concatenate([sroot_ref[...] * SCALE, column(oroot_ref)], axis=1)
    own[8:24] = jnp.concatenate([smid_ref[...] * SCALE, column(omid_ref)], axis=1)
    own[24:56] = jnp.concatenate([slow_ref[...] * SCALE, column(olow_ref)], axis=1)
    init[q] = own[0:24]
    for h in range(3):
        loads[h].wait()
        gt[h, mode] = raw[h].T
    pl.semaphore_wait(barrier, 30)

    def part(c, h, n):
        return gt.at[h, c, pl.ds(64 * n, 64)]

    def chunk(h, kind):
        c, n, peer = (
            (mode, 0, right),
            (mode, 1, left),
            (mode, 1, right),
            (mode, 0, left),
            (left, 0, right),
            (right, 1, left),
        )[kind]
        return remote(part(c, h, n), part(c, h, n), gsend.at[h, kind], grecv.at[h, kind], leaf, peer)

    def chunk_in(h, kind):
        c, n = ((left, 0), (right, 1), (left, 1), (right, 0), (across, 0), (across, 1))[kind]
        return remote(part(c, h, n), part(c, h, n), gsend.at[h, kind], grecv.at[h, kind], leaf, right)

    for kinds in ((0, 1), (2, 3)):
        for h in range(3):
            for kind in kinds:
                chunk(h, kind).start()

    def quarter_copy(src, dst, phase, peer):
        return remote(src, dst, csend.at[phase, peer], crecv.at[phase, q], peer * 16 + j, mode)

    def quarter_in(dst, phase, peer):
        return remote(dst, dst, csend.at[phase, peer], crecv.at[phase, peer], peer * 16 + j, mode)

    top = pl.ds(0, 8)
    init_out = [
        quarter_copy(init.at[q, top], init.at[q, top], 0, far0),
        quarter_copy(init.at[q, top], init.at[q, top], 0, far1),
        quarter_copy(init.at[q], init.at[q], 0, partner),
    ]
    for copy in init_out:
        copy.start()
    quarter_in(init.at[partner], 0, partner).wait_recv()
    quarter_in(init.at[far0, top], 0, far0).wait_recv()
    quarter_in(init.at[far1, top], 0, far1).wait_recv()

    low_lanes = lax.broadcasted_iota(jnp.int32, (16, 128), 1) < 64

    def packs(a, b):
        return (
            jnp.where(low_lanes, a, pltpu.roll(b, 64, 1)),
            jnp.where(low_lanes, pltpu.roll(a, 64, 1), b),
        )

    iroot, wroot = packs(
        jnp.concatenate([init[0, 0:8], init[1, 0:8]], axis=0),
        jnp.concatenate([init[2, 0:8], init[3, 0:8]], axis=0),
    )
    imid, wmid = packs(init[half_base, 8:24], init[half_base + 1, 8:24])
    ilow, wlow = packs(own[24:40], own[40:56])
    state = [iroot, imid, ilow]
    omega = [wroot, wmid, wlow]

    def group_start(phase, src_of, dst):
        def one(d, carry):
            t = (j + d) % 16
            remote(src_of(t), dst, psend.at[phase], precv.at[phase], base + t, mode).start()
            return carry

        lax.fori_loop(1, 16, one, 0)

    def group_all(phase, landing):
        some = landing.at[pl.ds(0, 15)]
        return remote(some, some, psend.at[phase], precv.at[phase], base + (j + 1) % 16, mode)

    mine = 8 * core + chip
    other = leaf + 1 - 2 * core

    def chips_start(phase, src_of, dst):
        for t in reversed(chips):
            remote(src_of(t), dst, psend.at[phase], precv.at[phase], base + 2 * t + core, mode).start()

    def chips_all(phase, landing):
        some = landing.at[pl.ds(0, 7)]
        return remote(some, some, psend.at[phase], precv.at[phase], other, mode)

    def core_copy(n, src, dst):
        return remote(src, dst, xsend.at[n], xrecv.at[n], other, mode)

    def spread_start(s, h):
        slot = mine if h == 2 else j
        ag[s, h, slot] = state[h]
        block = ag.at[s, h, slot]
        if h == 2:
            chips_start(3 * s + h, lambda t: block, block)
        else:
            group_start(3 * s + h, lambda t: block, block)

    def pass_on(s, c):
        blocks = ag.at[s, 2, pl.ds(8 * c, 8)]
        return core_copy(s, blocks, blocks)

    def spread_forward(s):
        chips_all(3 * s + 2, ag.at[s, 2]).wait_recv()
        pass_on(s, core).start()

    def spread_wait(s, h):
        if h == 2:
            pass_on(s, 1 - core).wait_recv()
        else:
            group_all(3 * s + h, ag.at[s, h]).wait_recv()
        for n in range(16):
            block = ag[s, h, n]
            turned = pltpu.roll(block, 64, 1)
            if h == 0:
                for k in range(2):
                    iv[root_row(k, n) : root_row(k, n) + 8, :] = block[8 * k : 8 * k + 8]
                    iv[root_row(k + 2, n) : root_row(k + 2, n) + 8, :] = turned[8 * k : 8 * k + 8]
            elif h == 1:
                iv[mid_row(0, n) : mid_row(0, n) + 16, :] = block
                iv[mid_row(1, n) : mid_row(1, n) + 16, :] = turned
            else:
                first = low_row(2 * (n % 8) + n // 8)
                iv[first : first + 16, :] = block
                iv[first + 16 : first + 32, :] = turned

    def pack_terms(s, h):
        for n in range(16):
            if h == 0:
                a, b = [
                    jnp.concatenate(
                        [tt[root_row(k, n) : root_row(k, n) + 8], tt[root_row(k + 1, n) : root_row(k + 1, n) + 8]],
                        axis=0,
                    )
                    for k in (0, 2)
                ]
            elif h == 1:
                a, b = [tt[mid_row(k, n) : mid_row(k, n) + 16] for k in range(2)]
            else:
                a, b = tt[low_row(n) : low_row(n) + 16], tt[low_row(n) + 16 : low_row(n) + 32]
            tp[s, h, n if h == 0 else 8 * (n % 2) + n // 2] = jnp.where(low_lanes, a, b)

    def cross(s, h):
        return core_copy(1 + 2 * s + h + 1, tp.at[s, h, pl.ds(8 * (1 - core), 8)], xb.at[s, h - 1])

    def reduce_start(s, h):
        if h > 0:
            cross(s, h).start()
            return
        group_start(9 + 3 * s, lambda t: tp.at[s, 0, t], rs.at[s, 0, j])
        rs[s, 0, j] = tp[s, 0, j]

    def reduce_middle(s, h):
        cross(s, h).wait_recv()
        xs[s, h - 1] = tp[s, h, pl.ds(8 * core, 8)] + xb[s, h - 1]
        chips_start(9 + 3 * s + h, lambda t: xs.at[s, h - 1, t], rs.at[s, h, chip])
        rs[s, h, chip] = xs[s, h - 1, chip]

    def reduce_end(s, h):
        if h == 0:
            group_all(9 + 3 * s, rs.at[s, h]).wait_recv()
        else:
            chips_all(9 + 3 * s + h, rs.at[s, h]).wait_recv()
        total = rs[s, h, 0]
        for n in range(1, 16 if h == 0 else 8):
            total = total + rs[s, h, n]
        return total

    for h in range(3):
        spread_start(0, h)

    coord = lax.broadcasted_iota(jnp.int32, (1, 128), 1)
    live = jnp.concatenate([(coord < sizes_ref[n]).astype(F32) for n in range(4)], axis=1)
    stiff = stiff_ref[...]
    inverse = live / stiff
    weighted = inverse * inverse
    m = leaf_ref[...] * live * SCALE

    def split_chunk(c, h):
        ghi[h, c], glo[h, c] = halves(gt[h, c])

    def apply_chunk(c, h):
        first = pl.multiple_of(h * 512 + c * 128, 128)
        high, low = halves(iv[pl.ds(first, 128), :][:, 0:64].T)
        both = nn16(jnp.concatenate([high, low], axis=0), ghi[h, c])
        return both[0:64] + both[64:128] + nn16(high, glo[h, c])

    def project(h):
        high, low = halves(gt[h].reshape(512, 512) * weighted)
        mine = jnp.concatenate([ghi[h, mode], glo[h, mode]], axis=0)
        both = nt16(high, mine)
        ms[h] = both[:, 0:128] + both[:, 128:256] + nt16(low, mine[0:128])

    for h in range(3):
        for kind in (0, 1):
            chunk_in(h, kind).wait_recv()
            chunk(h, kind + 4).start()
        split_chunk(mode, h)
    spread_forward(0)
    for h in (0, 1, 2):
        spread_wait(0, h)
    coupled = apply_chunk(mode, 0) + apply_chunk(mode, 1) + apply_chunk(mode, 2)
    for h in range(3):
        chunk_in(h, 2).wait_recv()
        chunk_in(h, 3).wait_recv()
        for c in (left, right):
            split_chunk(c, h)
            coupled = coupled + apply_chunk(c, h)
    for h in range(3):
        chunk_in(h, 4).wait_recv()
        chunk_in(h, 5).wait_recv()
        split_chunk(across, h)
        coupled = coupled + apply_chunk(across, h)

    def mass_copy(h, t):
        rows = pl.ds(32 * h, 32)
        return remote(
            mxs.at[t, rows], mrs.at[chip, rows], hsend.at[h, t], hrecv.at[h, chip], base + 2 * t + core, mode
        )

    def mass_in(h, t):
        came = mrs.at[t, pl.ds(32 * h, 32)]
        return remote(came, came, hsend.at[h, t], hrecv.at[h, t], base + 2 * t + core, mode)

    def mass_part(h):
        for t in reversed(chips):
            mass_copy(h, t).start()

    mass_core = core_copy(9, mp.at[1 - core], mxb)

    def pack_masses():
        for t in range(16):
            for k in range(4):
                mp[t % 2, t // 2, 8 * k : 8 * k + 8] = ms[0, 128 * k + 8 * t : 128 * k + 8 * t + 8]
            for k in range(2):
                mp[t % 2, t // 2, 32 + 16 * k : 48 + 16 * k] = ms[
                    1, 256 * k + 16 * t : 256 * k + 16 * t + 16
                ]
            mp[t % 2, t // 2, 64:96] = ms[2, 32 * t : 32 * t + 32]

    def y_copy(ref, phase, k):
        return remote(ref.at[mode], ref.at[mode], ysend.at[phase, k], yrecv.at[phase, k], leaf, modes[k])

    def y_in(ref, phase, k):
        came = ref.at[(left, right, across)[k]]
        return remote(came, came, ysend.at[phase, k], yrecv.at[phase, k], leaf, right)

    for s in range(ITERS):
        last = s == ITERS - 1
        if s > 0:
            coupled = jnp.zeros((64, 512), F32)
            for h in (2, 0, 1):
                spread_wait(s, h)
                high, low = halves(iv[512 * h : 512 * h + 512, :][:, 0:64].T)
                both = nn16(jnp.concatenate([high, low], axis=0), ghi[h].reshape(512, 512))
                coupled = coupled + (both[0:64] + both[64:128] + nn16(high, glo[h].reshape(512, 512)))
        modal_mass = live * m - inverse * coupled
        m = inverse * modal_mass
        high, low = halves(m)
        twice = jnp.concatenate([high, high], axis=0)
        four = jnp.concatenate([twice, low, low], axis=0)
        for h in range(3):
            both = nt16(ghi[h].reshape(512, 512), four)
            tt[512 * h : 512 * h + 512, :] = (
                both[:, 0:128] + both[:, 128:256] + nt16(glo[h].reshape(512, 512), twice)
            )
            pack_terms(s, h)
            reduce_start(s, h)
        for h in (1, 2):
            reduce_middle(s, h)
        if last:
            yl[mode] = m
            for k in range(3):
                y_copy(yl, 0, k).start()
        if s == 0:
            for h in range(3):
                project(h)
            pack_masses()
            mass_core.start()
        if last:
            heavy = m * stiff
            break
        cs[s, 0] = reduce_end(s, 0)
        for peer in (far0, far1, partner):
            quarter_copy(cs.at[s, 0], cb.at[s, 0, q], 1 + s, peer).start()
        cs[s, 1] = reduce_end(s, 1)
        quarter_copy(cs.at[s, 1], cb.at[s, 1, q], 3 + s, partner).start()
        state[2] = (state[2] - reduce_end(s, 2)) / omega[2]
        spread_start(s + 1, 2)
        if s == 0:
            mass_core.wait_recv()
            mxs[...] = mp[core] + mxb[...]
            mrs[chip] = mxs[chip]
        mass_part(s)
        for peer in (partner, far0, far1):
            quarter_in(cb.at[s, 0, peer], 1 + s, peer).wait_recv()
        gone = (cs[s, 0] + cb[s, 0, partner]) + (cb[s, 0, far0] + cb[s, 0, far1])
        state[0] = (state[0] - gone) / omega[0]
        spread_start(s + 1, 0)
        quarter_in(cb.at[s, 1, partner], 3 + s, partner).wait_recv()
        state[1] = (state[1] - (cs[s, 1] + cb[s, 1, partner])) / omega[1]
        spread_start(s + 1, 1)
        spread_forward(s + 1)
        if s == ITERS - 2:
            gp[0:16] = state[0]
            gp[16:32] = pltpu.roll(state[0], 64, 1)
            piece = pl.multiple_of(16 * (q // 2) + 8 * (q % 2), 8)
            iy[mode, 0:8] = gp[pl.ds(piece, 8)]
            odd = (q % 2) == 1
            iy[mode, 8:24] = jnp.where(odd, pltpu.roll(state[1], 64, 1), state[1])
            iy[mode, 24:40] = state[2]
            iy[mode, 40:56] = pltpu.roll(state[2], 64, 1)
            for k in range(3):
                y_copy(iy, 1, k).start()

    total = reduce_end(ITERS - 1, 0)
    turned = pltpu.roll(total, 64, 1)
    for k in range(2):
        fb[k, 0:8] = total[8 * k : 8 * k + 8]
        fb[k + 2, 0:8] = turned[8 * k : 8 * k + 8]

    def owner_copy(peer, d, rows):
        rows = pl.ds(0, rows)
        to = (mode + d) % 4
        return remote(
            fb.at[peer, rows], fr.at[mode, q, rows], fsend.at[peer, to], frecv.at[q, mode], peer * 16 + j, to
        )

    def owner_in(peer, c, rows):
        ref = fr.at[c, peer, pl.ds(0, rows)]
        return remote(ref, ref, fsend.at[peer, c], frecv.at[peer, c], peer * 16 + j, right)

    for peer in (far0, far1):
        for d in (2, 1, 3, 0):
            owner_copy(peer, d, 8).start()
    total = reduce_end(ITERS - 1, 1)
    turned = pltpu.roll(total, 64, 1)
    odd = (q % 2) == 1
    fb[q, 8:24] = jnp.where(odd, turned, total)
    fb[partner, 8:24] = jnp.where(odd, total, turned)
    for d in (2, 1, 3, 0):
        owner_copy(partner, d, 24).start()
    total = reduce_end(ITERS - 1, 2)
    fb[q, 24:40] = total
    fb[q, 40:56] = pltpu.roll(total, 64, 1)
    for d in (2, 1, 3):
        owner_copy(q, d, 56).start()
    fr[mode, q] = fb[q]

    mass_part(2)
    for k in range(3):
        y_in(yl, 0, k).wait_recv()
        y_in(iy, 1, k).wait_recv()
    blocks = [nt(yl[c], heavy) for c in range(4)]
    results = [
        pltpu.make_async_copy(a, b, osem.at[n])
        for n, (a, b) in enumerate(
            (
                (yl, next_out),
                (iface_ref, iface_out),
                (mroot_ref, mroot_out),
                (mmid_ref, mmid_out),
                (mlow_ref, mlow_out),
                (gag, gram_out),
            )
        )
    ]
    results[0].start()
    for peer in (far0, far1):
        for d in range(4):
            owner_in(peer, (mode + d) % 4, 8).wait_recv()
    for d in range(4):
        owner_in(partner, (mode + d) % 4, 24).wait_recv()
    for d in range(1, 4):
        owner_in(q, (mode + d) % 4, 56).wait_recv()
    weights = pltpu.roll(own[...], 64, 1)
    for c in range(4):
        near = fr[c, q, 0:24] + fr[c, partner, 0:24]
        near = jnp.concatenate(
            [near[0:8] + (fr[c, far0, 0:8] + fr[c, far1, 0:8]), near[8:24], fr[c, q, 24:56]], axis=0
        )
        iface_ref[c] = (iy[c] - near) / weights
    results[1].start()
    heavy_own = (iface_ref[mode] * weights)[:, 0:64].T
    blocks = [
        (blocks[c] + nt(iface_ref[c][:, 0:64].T, heavy_own)) * (1.0 / ROWS) for c in range(4)
    ]
    gp[...] = jnp.concatenate(
        [jnp.concatenate(blocks[0:2], axis=0), jnp.concatenate(blocks[2:4], axis=0)], axis=1
    )

    def rows8(t):
        return pl.ds(pl.multiple_of(8 * t, 8), 8)

    group_start(18, lambda t: gp.at[rows8(t)], grs.at[j])
    grs[j] = gp[rows8(j)]
    for h in range(3):
        for t in chips:
            mass_in(h, t).wait_recv()
    total = mrs[0]
    for t in range(1, 8):
        total = total + mrs[t]
    ms[0, 0:96] = total
    mid_of = pl.ds(pl.multiple_of(32 + 16 * (q % 2), 8), 16)
    mid_to = pl.ds(pl.multiple_of(48 - 16 * (q % 2), 8), 16)
    mass_out = [quarter_copy(ms.at[0, rows8(k)], mc.at[q, top], 5, k) for k in quarters]
    mass_out.append(quarter_copy(ms.at[0, mid_to], mc.at[q, pl.ds(8, 16)], 6, partner))
    for copy in mass_out:
        copy.start()

    group_all(18, grs).wait_recv()
    total = grs[0]
    for t in range(1, 16):
        total = total + grs[t]
    gc[mode, q] = total

    def gram_copy(peer, d):
        to = (mode + d) % 4
        ref = gc.at[mode, q]
        return remote(ref, ref, fsend.at[peer + 4, to], frecv.at[q + 4, mode], peer * 16 + j, to)

    def gram_in(peer, c):
        ref = gc.at[c, peer]
        return remote(ref, ref, fsend.at[peer + 4, c], frecv.at[peer + 4, c], peer * 16 + j, right)

    for peer in quarters:
        for d in (2, 1, 3, 0):
            gram_copy(peer, d).start()
    for d in (2, 1, 3):
        gram_copy(q, d).start()

    for peer in quarters:
        quarter_in(mc.at[peer, top], 5, peer).wait_recv()
    quarter_in(mc.at[partner, pl.ds(8, 16)], 6, partner).wait_recv()

    def unit(first, count):
        rows = lax.broadcasted_iota(jnp.int32, (count, 128), 0) + first
        cols = lax.broadcasted_iota(jnp.int32, (count, 128), 1) + mode * 128
        return (rows % 512 == cols).astype(F32)

    mroot_ref[...] = (
        ms[0, rows8(q)] + (mc[partner, 0:8] + mc[far0, 0:8] + mc[far1, 0:8]) + unit(leaf * 8, 8)
    )
    mmid_ref[...] = ms[0, mid_of] + mc[partner, 8:24] + unit(leaf * 16, 16)
    mlow_ref[...] = ms[0, 64:96] + unit(leaf * 32, 32)
    for result in results[2:5]:
        result.start()
    for h in range(3):
        for kind in range(6):
            chunk(h, kind).wait_send()
    for copy in init_out:
        copy.wait_send()
    for s in range(ITERS):
        for h in range(3):
            if h == 0:
                group_all(3 * s, ag.at[s, h]).wait_send()
                group_all(9 + 3 * s, rs.at[s, h]).wait_send()
                pass_on(s, core).wait_send()
                continue
            (group_all if h == 1 else chips_all)(3 * s + h, ag.at[s, h]).wait_send()
            chips_all(9 + 3 * s + h, rs.at[s, h]).wait_send()
            cross(s, h).wait_send()
    for s in range(ITERS - 1):
        for peer in quarters:
            quarter_copy(cs.at[s, 0], cb.at[s, 0, q], 1 + s, peer).wait_send()
        quarter_copy(cs.at[s, 1], cb.at[s, 1, q], 3 + s, partner).wait_send()
    mass_core.wait_send()
    for h in range(3):
        for t in chips:
            mass_copy(h, t).wait_send()
    for k in range(3):
        y_copy(yl, 0, k).wait_send()
        y_copy(iy, 1, k).wait_send()

    for peer in quarters:
        for d in range(4):
            gram_in(peer, (mode + d) % 4).wait_recv()
    for d in range(1, 4):
        gram_in(q, (mode + d) % 4).wait_recv()
    for c in range(4):
        gag[j, c] = (gc[c, 0] + gc[c, 1]) + (gc[c, 2] + gc[c, 3])
    group_start(19, lambda t: gag.at[j], gag.at[j])
    for d in range(4):
        for peer in (far0, far1):
            owner_copy(peer, d, 8).wait_send()
        owner_copy(partner, d, 24).wait_send()
        if d > 0:
            owner_copy(q, d, 56).wait_send()
            gram_copy(q, d).wait_send()
        for peer in quarters:
            gram_copy(peer, d).wait_send()
    for copy in mass_out:
        copy.wait_send()
    group_all(18, grs).wait_send()
    group_all(19, gag).wait_recv()
    results[5].start()
    group_all(19, gag).wait_send()
    for result in results:
        result.wait()


def run_sweeps(leaf_sizes, stiff, coupling, start_leaf, starts, omegas):
    scratch = [
        (3, 4, 128, 512),
        (3, 4, 128, 512),
        (3, 4, 128, 512),
        (3, 512, 128),
        (1, 512),
        (64, 512),
        (8, 64),
        (16, 64),
        (32, 64),
        (1, 8),
        (1, 16),
        (1, 32),
        (56, 128),
        (4, 24, 128),
        (1536, 128),
        (1536, 128),
        (3, 3, 16, 16, 128),
        (3, 2, 8, 16, 128),
        (3, 2, 8, 16, 128),
        (3, 3, 16, 16, 128),
        (2, 2, 16, 128),
        (2, 2, 4, 16, 128),
        (3, 3, 16, 16, 128),
        (4, 56, 128),
        (4, 4, 56, 128),
        (4, 64, 512),
        (4, 56, 128),
        (128, 128),
        (16, 8, 128),
        (4, 4, 8, 128),
        (16, 4, 8, 128),
        (4, 56, 128),
        (8, 128),
        (16, 128),
        (32, 128),
        (3, 512, 128),
        (2, 8, 96, 128),
        (8, 96, 128),
        (8, 96, 128),
        (8, 96, 128),
        (4, 24, 128),
    ]
    sems = [(11,), (6,), (3, 6), (3, 6), (20,), (20,), (3, 8), (3, 8), (10,), (10,)]
    sems += [(7, 4), (7, 4), (2, 3), (2, 3), (8, 4), (8, 4)]
    shapes = [(16, 4, 8, 128), (4, 64, 512), (4, 56, 128), (8, 128), (16, 128), (32, 128)]
    return pl.pallas_call(
        sweeps_kernel,
        out_shape=[jax.ShapeDtypeStruct(shape, F32) for shape in shapes],
        in_specs=[pl.BlockSpec(memory_space=pltpu.SMEM)]
        + [pl.BlockSpec(memory_space=pltpu.HBM)] * 9,
        out_specs=[pl.BlockSpec(memory_space=pltpu.HBM)] * 6,
        scratch_shapes=[
            pltpu.VMEM(shape, BF16 if n in (1, 2) else F32) for n, shape in enumerate(scratch)
        ]
        + [pltpu.SemaphoreType.DMA(shape) for shape in sems],
        compiler_params=pltpu.CompilerParams(
            collective_id=0, has_side_effects=True, vmem_limit_bytes=64 * 1024 * 1024
        ),
        name="sweeps",
    )(leaf_sizes, stiff, coupling, start_leaf, *starts, *omegas)


def factor_block(a):
    rows = [a[8 * r : 8 * r + 8, :] for r in range(8)]
    sub = lax.broadcasted_iota(jnp.int32, (8, 128), 0)
    pivots = []
    for p in range(8):
        cols = []
        for k in range(8):
            pick = jnp.full((8, 128), 8 * p + k, jnp.int32)
            cols.append([jnp.take_along_axis(rows[r], pick, axis=1) for r in range(p, 8)])
        diag = []
        for k in range(0, 8, 2):
            head, cross = [jnp.broadcast_to(cols[k][0][n : n + 1, :], (8, 128)) for n in (k, k + 1)]
            tail = jnp.broadcast_to(cols[k + 1][0][k + 1 : k + 2, :], (8, 128))
            det = head * tail - cross * cross
            inv0 = 1.0 / head
            inv1 = head * (1.0 / det)
            ratio = cross * inv0
            diag += [head, det * inv0]
            first = [c * inv0 for c in cols[k]]
            first[0] = jnp.where(sub > k, first[0], 0.0)
            second = [(c - f * cross) * inv1 for c, f in zip(cols[k + 1], first)]
            second[0] = jnp.where(sub > k + 1, second[0], 0.0)
            for k2 in range(k + 2, 8):
                up0 = jnp.broadcast_to(cols[k2][0][k : k + 1, :], (8, 128))
                up1 = jnp.broadcast_to(cols[k2][0][k + 1 : k + 2, :], (8, 128)) - ratio * up0
                cols[k2] = [c - (f * up0 + g * up1) for c, f, g in zip(cols[k2], first, second)]
            lead0 = jnp.broadcast_to(rows[p][k : k + 1, :], (8, 128))
            lead1 = jnp.broadcast_to(rows[p][k + 1 : k + 2, :], (8, 128)) - ratio * lead0
            for r in range(p, 8):
                rows[r] = rows[r] - (first[r - p] * lead0 + second[r - p] * lead1)
        scale = diag[0]
        for k in range(1, 8):
            scale = jnp.where(sub == k, diag[k], scale)
        pivots.append(lax.rsqrt(scale))
    return jnp.concatenate([row * pivot for row, pivot in zip(rows, pivots)], axis=0)


def finish_kernel(
    gram_in,
    next_in,
    iface_in,
    mroot_in,
    mmid_in,
    mlow_in,
    leaf_out,
    root_out,
    mid_out,
    low_out,
    mroot_out,
    mmid_out,
    mlow_out,
    gram_ref,
    next_ref,
    iface_ref,
    full,
    lower,
    sem,
):
    mode = lax.axis_index("mode")
    moves = (
        (gram_in, gram_ref),
        (next_in, next_ref),
        (iface_in, iface_ref),
        (mroot_in, mroot_out),
        (mmid_in, mmid_out),
        (mlow_in, mlow_out),
    )
    moves = [pltpu.make_async_copy(a, b, sem.at[n]) for n, (a, b) in enumerate(moves)]
    for move in moves:
        move.start()
    moves[0].wait()
    low_lanes = lax.broadcasted_iota(jnp.int32, (128, 128), 1) < 64
    parts = [jnp.concatenate([gram_ref[t, c] for t in range(16)], axis=0) for c in range(4)]
    turned = [pltpu.roll(part, 64, 1) for part in parts]
    gram = jnp.concatenate(
        [
            jnp.concatenate([jnp.where(low_lanes, parts[c], turned[c + 1]) for c in (0, 2)], axis=1),
            jnp.concatenate([jnp.where(low_lanes, turned[c], parts[c + 1]) for c in (0, 2)], axis=1),
        ],
        axis=0,
    )
    gram = 0.5 * (gram + gram.T)
    r = lax.broadcasted_iota(jnp.int32, (256, 256), 0)
    c = lax.broadcasted_iota(jnp.int32, (256, 256), 1)
    corner = jnp.where(r == c, gram, 0.0)
    down = lax.rsqrt(jnp.sum(corner, axis=1, keepdims=True))
    over = lax.rsqrt(jnp.sum(corner, axis=0, keepdims=True))
    full[:, 0:256] = gram * down * over
    full[:, 256:512] = jnp.where(r == c, jnp.broadcast_to(down, (256, 256)), 0.0)
    unit = (
        lax.broadcasted_iota(jnp.int32, (64, 64), 0) == lax.broadcasted_iota(jnp.int32, (64, 64), 1)
    ).astype(F32)
    for k in range(4):
        first = 64 * k
        block = full[first : first + 64, first : first + 64]
        weight = factor_block(jnp.concatenate([block, unit], axis=1))[:, 64:128]
        right = 128 * (k // 2)
        panel = nn(weight, full[first : first + 64, right:512])
        lower[first : first + 64, :] = panel[:, 256 - right : 512 - right]
        if k < 3:
            below = panel[:, first + 64 - right : 256 - right]
            full[first + 64 : 256, right:512] = full[first + 64 : 256, right:512] - tn(below, panel)
    own = lower[pl.ds(pl.multiple_of(mode * 64, 64), 64), :]
    for move in moves[1:]:
        move.wait()
    leaf_out[...] = nn(own, next_ref[...].reshape(256, 512))
    iface = jnp.concatenate([iface_ref[c][:, 0:64] for c in range(4)], axis=1)
    done = nt(iface, own)
    root_out[...] = done[0:8]
    mid_out[...] = done[8:24]
    low_out[...] = done[24:56]


def run_finish(gram, modal, iface, masses):
    vmem = pl.BlockSpec(memory_space=pltpu.VMEM)
    hbm = pl.BlockSpec(memory_space=pltpu.HBM)
    shapes = [(64, 512), (8, 64), (16, 64), (32, 64), (8, 128), (16, 128), (32, 128)]
    return pl.pallas_call(
        finish_kernel,
        out_shape=[jax.ShapeDtypeStruct(shape, F32) for shape in shapes],
        in_specs=[hbm] * 6,
        out_specs=[vmem] * 4 + [hbm] * 3,
        scratch_shapes=[
            pltpu.VMEM((16, 4, 8, 128), F32),
            pltpu.VMEM((4, 64, 512), F32),
            pltpu.VMEM((4, 56, 128), F32),
            pltpu.VMEM((256, 512), F32),
            pltpu.VMEM((256, 256), F32),
            pltpu.SemaphoreType.DMA((6,)),
        ],
        compiler_params=pltpu.CompilerParams(vmem_limit_bytes=64 * 1024 * 1024),
        name="finish",
    )(gram, modal, iface, *masses)


def local(
    leaf_sizes,
    leaf_stiffness,
    coupling,
    omega_root,
    omega_mid,
    omega_low,
    start_leaf,
    start_root,
    start_mid,
    start_low,
):
    gram, modal, iface, *masses = run_sweeps(
        leaf_sizes,
        leaf_stiffness.reshape(1, -1),
        coupling,
        start_leaf,
        [start_root.T, start_mid.T, start_low.T],
        [omega_root.reshape(1, -1), omega_mid.reshape(1, -1), omega_low.reshape(1, -1)],
    )
    leaf, root, mid, low, *masses = run_finish(gram, modal, iface, masses)
    return (leaf, root.T, mid.T, low.T, *masses)


def solution(mesh):
    placed = (
        P("leaf"),
        P("leaf"),
        P(None, "leaf", "mode"),
        P("leaf"),
        P("leaf"),
        P("leaf"),
        P("mode", "leaf"),
        P("mode", "leaf"),
        P("mode", "leaf"),
        P("mode", "leaf"),
    )
    return jax.shard_map(
        local,
        mesh=mesh,
        in_specs=placed,
        out_specs=(
            P("mode", "leaf"),
            P("mode", "leaf"),
            P("mode", "leaf"),
            P("mode", "leaf"),
            P("leaf", "mode"),
            P("leaf", "mode"),
            P("leaf", "mode"),
        ),
        check_vma=False,
    )
```

```python
import functools
import jax
import jax.numpy as jnp
from jax import lax
from jax.experimental import pallas as pl
from jax.experimental.pallas import tpu as pltpu
from jax.sharding import PartitionSpec as P

ITERS = 3
ROWS = 36352.0
SCALE = 2.0**-12
MESH = pl.DeviceIdType.MESH
HI = lax.Precision.HIGHEST
F32 = jnp.float32
BF16 = jnp.bfloat16
NEAR_FIRST = ((0, 1), (0, 3), (1, 0), (0, 2), (1, 1), (1, 3), (1, 2))


def nt(a, b):
    return lax.dot_general(a, b, (((1,), (1,)), ((), ())), precision=HI, preferred_element_type=F32)


def nn(a, b):
    return lax.dot_general(a, b, (((1,), (0,)), ((), ())), precision=HI, preferred_element_type=F32)


def tn(a, b):
    return lax.dot_general(a, b, (((0,), (0,)), ((), ())), precision=HI, preferred_element_type=F32)


def halves(x):
    high = x.astype(BF16)
    return high, (x - high.astype(F32)).astype(BF16)


def nn16(a, b):
    return lax.dot_general(a, b, (((1,), (0,)), ((), ())), preferred_element_type=F32)


def nt16(a, b):
    return lax.dot_general(a, b, (((1,), (1,)), ((), ())), preferred_element_type=F32)


def root_row(q, n):
    return q * 128 + 8 * n


def mid_row(half, n):
    return 512 + half * 256 + 16 * n


def low_row(n):
    return 1024 + 32 * n


def remote(src, dst, send, recv, leaf, mode):
    return pltpu.make_async_remote_copy(
        src_ref=src,
        dst_ref=dst,
        send_sem=send,
        recv_sem=recv,
        device_id=(leaf, mode),
        device_id_type=MESH,
    )


def column(ref):
    n = ref.shape[1]
    r = lax.broadcasted_iota(jnp.int32, (n, n), 0)
    c = lax.broadcasted_iota(jnp.int32, (n, n), 1)
    spread = jnp.where(r == c, jnp.broadcast_to(ref[...], (n, n)), 0.0)
    return jnp.broadcast_to(jnp.sum(spread, axis=1, keepdims=True), (n, 64))


def sweeps_kernel(
    sizes_ref,
    stiff_in,
    coupling_ref,
    leaf_in,
    sroot_in,
    smid_in,
    slow_in,
    oroot_in,
    omid_in,
    olow_in,
    gram_out,
    next_out,
    iface_out,
    mroot_out,
    mmid_out,
    mlow_out,
    gt,
    ghi,
    glo,
    raw,
    stiff_ref,
    leaf_ref,
    sroot_ref,
    smid_ref,
    slow_ref,
    oroot_ref,
    omid_ref,
    olow_ref,
    own,
    init,
    iv,
    tt,
    tp,
    xb,
    xs,
    rs,
    cs,
    cb,
    ag,
    fb,
    fr,
    yl,
    iy,
    gp,
    grs,
    gc,
    gag,
    iface_ref,
    mroot_ref,
    mmid_ref,
    mlow_ref,
    ms,
    mp,
    mxb,
    mxs,
    mrs,
    mc,
    lsem,
    osem,
    gsend,
    grecv,
    psend,
    precv,
    hsend,
    hrecv,
    xsend,
    xrecv,
    csend,
    crecv,
    ysend,
    yrecv,
    fsend,
    frecv,
):
    leaf = lax.axis_index("leaf")
    mode = lax.axis_index("mode")
    q = leaf // 16
    j = leaf % 16
    base = q * 16
    core = j % 2
    chip = j // 2
    chips = [((chip // 4 + dz) % 2) * 4 + (chip + dx) % 4 for dz, dx in NEAR_FIRST]
    right = (mode + 1) % 4
    left = (mode + 3) % 4
    across = (mode + 2) % 4
    modes = (right, left, across)
    partner = q + 1 - 2 * (q % 2)
    half_base = q - q % 2
    far0 = (q + 2) % 4
    far1 = (partner + 2) % 4
    quarters = (far0, far1, partner)

    around = [(j + d) % 16 for d in range(1, 16)]
    barrier = pltpu.get_barrier_semaphore()

    def greet(to_leaf, to_mode):
        pl.semaphore_signal(barrier, inc=1, device_id=(to_leaf, to_mode), device_id_type=MESH)

    for peer in quarters:
        for to in (mode,) + modes:
            greet(peer * 16 + j, to)
    for to in modes:
        greet(leaf, to)
    for t in around:
        greet(base + t, mode)

    loads = [pltpu.make_async_copy(coupling_ref.at[h], raw.at[h], lsem.at[h]) for h in range(3)]
    small = [
        (sroot_in, sroot_ref),
        (smid_in, smid_ref),
        (slow_in, slow_ref),
        (oroot_in, oroot_ref),
        (omid_in, omid_ref),
        (olow_in, olow_ref),
        (stiff_in, stiff_ref),
        (leaf_in, leaf_ref),
    ]
    loads += [pltpu.make_async_copy(a, b, lsem.at[3 + n]) for n, (a, b) in enumerate(small)]
    for load in loads:
        load.start()
    for load in loads[3:]:
        load.wait()
    own[0:8] = jnp.concatenate([sroot_ref[...] * SCALE, column(oroot_ref)], axis=1)
    own[8:24] = jnp.concatenate([smid_ref[...] * SCALE, column(omid_ref)], axis=1)
    own[24:56] = jnp.concatenate([slow_ref[...] * SCALE, column(olow_ref)], axis=1)
    init[q] = own[0:24]
    for h in range(3):
        loads[h].wait()
        gt[h, mode] = raw[h].T
    pl.semaphore_wait(barrier, 30)

    def part(c, h, n):
        return gt.at[h, c, pl.ds(64 * n, 64)]

    def chunk(h, kind):
        c, n, peer = (
            (mode, 0, right),
            (mode, 1, left),
            (mode, 1, right),
            (mode, 0, left),
            (left, 0, right),
            (right, 1, left),
        )[kind]
        return remote(part(c, h, n), part(c, h, n), gsend.at[h, kind], grecv.at[h, kind], leaf, peer)

    def chunk_in(h, kind):
        c, n = ((left, 0), (right, 1), (left, 1), (right, 0), (across, 0), (across, 1))[kind]
        return remote(part(c, h, n), part(c, h, n), gsend.at[h, kind], grecv.at[h, kind], leaf, right)

    for kinds in ((0, 1), (2, 3)):
        for h in range(3):
            for kind in kinds:
                chunk(h, kind).start()

    def quarter_copy(src, dst, phase, peer):
        return remote(src, dst, csend.at[phase, peer], crecv.at[phase, q], peer * 16 + j, mode)

    def quarter_in(dst, phase, peer):
        return remote(dst, dst, csend.at[phase, peer], crecv.at[phase, peer], peer * 16 + j, mode)

    top = pl.ds(0, 8)
    init_out = [
        quarter_copy(init.at[q, top], init.at[q, top], 0, far0),
        quarter_copy(init.at[q, top], init.at[q, top], 0, far1),
        quarter_copy(init.at[q], init.at[q], 0, partner),
    ]
    for copy in init_out:
        copy.start()
    quarter_in(init.at[partner], 0, partner).wait_recv()
    quarter_in(init.at[far0, top], 0, far0).wait_recv()
    quarter_in(init.at[far1, top], 0, far1).wait_recv()

    low_lanes = lax.broadcasted_iota(jnp.int32, (16, 128), 1) < 64

    def packs(a, b):
        return (
            jnp.where(low_lanes, a, pltpu.roll(b, 64, 1)),
            jnp.where(low_lanes, pltpu.roll(a, 64, 1), b),
        )

    iroot, wroot = packs(
        jnp.concatenate([init[0, 0:8], init[1, 0:8]], axis=0),
        jnp.concatenate([init[2, 0:8], init[3, 0:8]], axis=0),
    )
    imid, wmid = packs(init[half_base, 8:24], init[half_base + 1, 8:24])
    ilow, wlow = packs(own[24:40], own[40:56])
    state = [iroot, imid, ilow]
    omega = [wroot, wmid, wlow]

    def group_start(phase, src_of, dst):
        for t in around:
            remote(src_of(t), dst, psend.at[phase], precv.at[phase], base + t, mode).start()

    def group_all(phase, landing):
        some = landing.at[pl.ds(0, 15)]
        return remote(some, some, psend.at[phase], precv.at[phase], base + (j + 1) % 16, mode)

    mine = 8 * core + chip
    other = leaf + 1 - 2 * core

    def chips_start(phase, src_of, dst):
        for t in reversed(chips):
            remote(src_of(t), dst, psend.at[phase], precv.at[phase], base + 2 * t + core, mode).start()

    def chips_all(phase, landing):
        some = landing.at[pl.ds(0, 7)]
        return remote(some, some, psend.at[phase], precv.at[phase], other, mode)

    def core_copy(n, src, dst):
        return remote(src, dst, xsend.at[n], xrecv.at[n], other, mode)

    def spread_start(s, h):
        slot = mine if h == 2 else j
        ag[s, h, slot] = state[h]
        block = ag.at[s, h, slot]
        if h == 2:
            chips_start(3 * s + h, lambda t: block, block)
        else:
            group_start(3 * s + h, lambda t: block, block)

    def pass_on(s, c):
        blocks = ag.at[s, 2, pl.ds(8 * c, 8)]
        return core_copy(s, blocks, blocks)

    def spread_forward(s):
        chips_all(3 * s + 2, ag.at[s, 2]).wait_recv()
        pass_on(s, core).start()

    def spread_wait(s, h):
        if h == 2:
            pass_on(s, 1 - core).wait_recv()
        else:
            group_all(3 * s + h, ag.at[s, h]).wait_recv()
        for n in range(16):
            block = ag[s, h, n]
            turned = pltpu.roll(block, 64, 1)
            if h == 0:
                for k in range(2):
                    iv[root_row(k, n) : root_row(k, n) + 8, :] = block[8 * k : 8 * k + 8]
                    iv[root_row(k + 2, n) : root_row(k + 2, n) + 8, :] = turned[8 * k : 8 * k + 8]
            elif h == 1:
                iv[mid_row(0, n) : mid_row(0, n) + 16, :] = block
                iv[mid_row(1, n) : mid_row(1, n) + 16, :] = turned
            else:
                first = low_row(2 * (n % 8) + n // 8)
                iv[first : first + 16, :] = block
                iv[first + 16 : first + 32, :] = turned

    def pack_terms(s, h):
        for n in range(16):
            if h == 0:
                a, b = [
                    jnp.concatenate(
                        [tt[root_row(k, n) : root_row(k, n) + 8], tt[root_row(k + 1, n) : root_row(k + 1, n) + 8]],
                        axis=0,
                    )
                    for k in (0, 2)
                ]
            elif h == 1:
                a, b = [tt[mid_row(k, n) : mid_row(k, n) + 16] for k in range(2)]
            else:
                a, b = tt[low_row(n) : low_row(n) + 16], tt[low_row(n) + 16 : low_row(n) + 32]
            tp[s, h, n if h == 0 else 8 * (n % 2) + n // 2] = jnp.where(low_lanes, a, b)

    def cross(s, h):
        return core_copy(1 + 2 * s + h + 1, tp.at[s, h, pl.ds(8 * (1 - core), 8)], xb.at[s, h - 1])

    def reduce_start(s, h):
        if h > 0:
            cross(s, h).start()
            return
        group_start(9 + 3 * s, lambda t: tp.at[s, 0, t], rs.at[s, 0, j])
        rs[s, 0, j] = tp[s, 0, j]

    def reduce_middle(s, h):
        cross(s, h).wait_recv()
        xs[s, h - 1] = tp[s, h, pl.ds(8 * core, 8)] + xb[s, h - 1]
        chips_start(9 + 3 * s + h, lambda t: xs.at[s, h - 1, t], rs.at[s, h, chip])
        rs[s, h, chip] = xs[s, h - 1, chip]

    def reduce_end(s, h):
        if h == 0:
            group_all(9 + 3 * s, rs.at[s, h]).wait_recv()
        else:
            chips_all(9 + 3 * s + h, rs.at[s, h]).wait_recv()
        total = rs[s, h, 0]
        for n in range(1, 16 if h == 0 else 8):
            total = total + rs[s, h, n]
        return total

    for h in range(3):
        spread_start(0, h)

    coord = lax.broadcasted_iota(jnp.int32, (1, 128), 1)
    live = jnp.concatenate([(coord < sizes_ref[n]).astype(F32) for n in range(4)], axis=1)
    stiff = stiff_ref[...]
    inverse = live / stiff
    weighted = inverse * inverse
    m = leaf_ref[...] * live * SCALE

    def split_chunk(c, h):
        ghi[h, c], glo[h, c] = halves(gt[h, c])

    def apply_chunk(c, h):
        first = pl.multiple_of(h * 512 + c * 128, 128)
        high, low = halves(iv[pl.ds(first, 128), :][:, 0:64].T)
        both = nn16(jnp.concatenate([high, low], axis=0), ghi[h, c])
        return both[0:64] + both[64:128] + nn16(high, glo[h, c])

    def project(h):
        high, low = halves(gt[h].reshape(512, 512) * weighted)
        mine = jnp.concatenate([ghi[h, mode], glo[h, mode]], axis=0)
        both = nt16(high, mine)
        ms[h] = both[:, 0:128] + both[:, 128:256] + nt16(low, mine[0:128])

    for h in range(3):
        for kind in (0, 1):
            chunk_in(h, kind).wait_recv()
            chunk(h, kind + 4).start()
        split_chunk(mode, h)
    spread_forward(0)
    for h in (0, 1, 2):
        spread_wait(0, h)
    coupled = apply_chunk(mode, 0) + apply_chunk(mode, 1) + apply_chunk(mode, 2)
    for h in range(3):
        chunk_in(h, 2).wait_recv()
        chunk_in(h, 3).wait_recv()
        for c in (left, right):
            split_chunk(c, h)
            coupled = coupled + apply_chunk(c, h)
    for h in range(3):
        chunk_in(h, 4).wait_recv()
        chunk_in(h, 5).wait_recv()
        split_chunk(across, h)
        coupled = coupled + apply_chunk(across, h)

    def mass_copy(h, t):
        rows = pl.ds(32 * h, 32)
        return remote(
            mxs.at[t, rows], mrs.at[chip, rows], hsend.at[h, t], hrecv.at[h, chip], base + 2 * t + core, mode
        )

    def mass_in(h, t):
        came = mrs.at[t, pl.ds(32 * h, 32)]
        return remote(came, came, hsend.at[h, t], hrecv.at[h, t], base + 2 * t + core, mode)

    def mass_part(h):
        for t in reversed(chips):
            mass_copy(h, t).start()

    mass_core = core_copy(9, mp.at[1 - core], mxb)

    def pack_masses():
        for t in range(16):
            for k in range(4):
                mp[t % 2, t // 2, 8 * k : 8 * k + 8] = ms[0, 128 * k + 8 * t : 128 * k + 8 * t + 8]
            for k in range(2):
                mp[t % 2, t // 2, 32 + 16 * k : 48 + 16 * k] = ms[
                    1, 256 * k + 16 * t : 256 * k + 16 * t + 16
                ]
            mp[t % 2, t // 2, 64:96] = ms[2, 32 * t : 32 * t + 32]

    def y_copy(ref, phase, k):
        return remote(ref.at[mode], ref.at[mode], ysend.at[phase, k], yrecv.at[phase, k], leaf, modes[k])

    def y_in(ref, phase, k):
        came = ref.at[(left, right, across)[k]]
        return remote(came, came, ysend.at[phase, k], yrecv.at[phase, k], leaf, right)

    for s in range(ITERS):
        last = s == ITERS - 1
        if s > 0:
            coupled = jnp.zeros((64, 512), F32)
            for h in (2, 0, 1):
                spread_wait(s, h)
                high, low = halves(iv[512 * h : 512 * h + 512, :][:, 0:64].T)
                both = nn16(jnp.concatenate([high, low], axis=0), ghi[h].reshape(512, 512))
                coupled = coupled + (both[0:64] + both[64:128] + nn16(high, glo[h].reshape(512, 512)))
        modal_mass = live * m - inverse * coupled
        m = inverse * modal_mass
        high, low = halves(m)
        twice = jnp.concatenate([high, high], axis=0)
        four = jnp.concatenate([twice, low, low], axis=0)
        for h in range(3):
            both = nt16(ghi[h].reshape(512, 512), four)
            tt[512 * h : 512 * h + 512, :] = (
                both[:, 0:128] + both[:, 128:256] + nt16(glo[h].reshape(512, 512), twice)
            )
            pack_terms(s, h)
            reduce_start(s, h)
        for h in (1, 2):
            reduce_middle(s, h)
        if last:
            yl[mode] = m
            for k in range(3):
                y_copy(yl, 0, k).start()
        if s == 0:
            for h in range(3):
                project(h)
            pack_masses()
            mass_core.start()
        if last:
            heavy = m * stiff
            break
        cs[s, 0] = reduce_end(s, 0)
        for peer in (far0, far1, partner):
            quarter_copy(cs.at[s, 0], cb.at[s, 0, q], 1 + s, peer).start()
        cs[s, 1] = reduce_end(s, 1)
        quarter_copy(cs.at[s, 1], cb.at[s, 1, q], 3 + s, partner).start()
        state[2] = (state[2] - reduce_end(s, 2)) / omega[2]
        spread_start(s + 1, 2)
        if s == 0:
            mass_core.wait_recv()
            mxs[...] = mp[core] + mxb[...]
            mrs[chip] = mxs[chip]
        mass_part(s)
        for peer in (partner, far0, far1):
            quarter_in(cb.at[s, 0, peer], 1 + s, peer).wait_recv()
        gone = (cs[s, 0] + cb[s, 0, partner]) + (cb[s, 0, far0] + cb[s, 0, far1])
        state[0] = (state[0] - gone) / omega[0]
        spread_start(s + 1, 0)
        quarter_in(cb.at[s, 1, partner], 3 + s, partner).wait_recv()
        state[1] = (state[1] - (cs[s, 1] + cb[s, 1, partner])) / omega[1]
        spread_start(s + 1, 1)
        spread_forward(s + 1)
        if s == ITERS - 2:
            gp[0:16] = state[0]
            gp[16:32] = pltpu.roll(state[0], 64, 1)
            piece = pl.multiple_of(16 * (q // 2) + 8 * (q % 2), 8)
            iy[mode, 0:8] = gp[pl.ds(piece, 8)]
            odd = (q % 2) == 1
            iy[mode, 8:24] = jnp.where(odd, pltpu.roll(state[1], 64, 1), state[1])
            iy[mode, 24:40] = state[2]
            iy[mode, 40:56] = pltpu.roll(state[2], 64, 1)
            for k in range(3):
                y_copy(iy, 1, k).start()

    total = reduce_end(ITERS - 1, 0)
    turned = pltpu.roll(total, 64, 1)
    for k in range(2):
        fb[k, 0:8] = total[8 * k : 8 * k + 8]
        fb[k + 2, 0:8] = turned[8 * k : 8 * k + 8]

    def owner_copy(peer, d, rows):
        rows = pl.ds(0, rows)
        to = (mode + d) % 4
        return remote(
            fb.at[peer, rows], fr.at[mode, q, rows], fsend.at[peer, to], frecv.at[q, mode], peer * 16 + j, to
        )

    def owner_in(peer, c, rows):
        ref = fr.at[c, peer, pl.ds(0, rows)]
        return remote(ref, ref, fsend.at[peer, c], frecv.at[peer, c], peer * 16 + j, right)

    for peer in (far0, far1):
        for d in (2, 1, 3, 0):
            owner_copy(peer, d, 8).start()
    total = reduce_end(ITERS - 1, 1)
    turned = pltpu.roll(total, 64, 1)
    odd = (q % 2) == 1
    fb[q, 8:24] = jnp.where(odd, turned, total)
    fb[partner, 8:24] = jnp.where(odd, total, turned)
    for d in (2, 1, 3, 0):
        owner_copy(partner, d, 24).start()
    total = reduce_end(ITERS - 1, 2)
    fb[q, 24:40] = total
    fb[q, 40:56] = pltpu.roll(total, 64, 1)
    for d in (2, 1, 3):
        owner_copy(q, d, 56).start()
    fr[mode, q] = fb[q]

    mass_part(2)
    for k in range(3):
        y_in(yl, 0, k).wait_recv()
        y_in(iy, 1, k).wait_recv()
    blocks = [nt(yl[c], heavy) for c in range(4)]
    results = [
        pltpu.make_async_copy(a, b, osem.at[n])
        for n, (a, b) in enumerate(
            (
                (yl, next_out),
                (iface_ref, iface_out),
                (mroot_ref, mroot_out),
                (mmid_ref, mmid_out),
                (mlow_ref, mlow_out),
                (gag, gram_out),
            )
        )
    ]
    results[0].start()
    for peer in (far0, far1):
        for d in range(4):
            owner_in(peer, (mode + d) % 4, 8).wait_recv()
    for d in range(4):
        owner_in(partner, (mode + d) % 4, 24).wait_recv()
    for d in range(1, 4):
        owner_in(q, (mode + d) % 4, 56).wait_recv()
    weights = pltpu.roll(own[...], 64, 1)
    for c in range(4):
        near = fr[c, q, 0:24] + fr[c, partner, 0:24]
        near = jnp.concatenate(
            [near[0:8] + (fr[c, far0, 0:8] + fr[c, far1, 0:8]), near[8:24], fr[c, q, 24:56]], axis=0
        )
        iface_ref[c] = (iy[c] - near) / weights
    results[1].start()
    heavy_own = (iface_ref[mode] * weights)[:, 0:64].T
    blocks = [
        (blocks[c] + nt(iface_ref[c][:, 0:64].T, heavy_own)) * (1.0 / ROWS) for c in range(4)
    ]
    gp[...] = jnp.concatenate(
        [jnp.concatenate(blocks[0:2], axis=0), jnp.concatenate(blocks[2:4], axis=0)], axis=1
    )

    def rows8(t):
        return pl.ds(pl.multiple_of(8 * t, 8), 8)

    group_start(18, lambda t: gp.at[rows8(t)], grs.at[j])
    grs[j] = gp[rows8(j)]
    for h in range(3):
        for t in chips:
            mass_in(h, t).wait_recv()
    total = mrs[0]
    for t in range(1, 8):
        total = total + mrs[t]
    ms[0, 0:96] = total
    mid_of = pl.ds(pl.multiple_of(32 + 16 * (q % 2), 8), 16)
    mid_to = pl.ds(pl.multiple_of(48 - 16 * (q % 2), 8), 16)
    mass_out = [quarter_copy(ms.at[0, rows8(k)], mc.at[q, top], 5, k) for k in quarters]
    mass_out.append(quarter_copy(ms.at[0, mid_to], mc.at[q, pl.ds(8, 16)], 6, partner))
    for copy in mass_out:
        copy.start()

    group_all(18, grs).wait_recv()
    total = grs[0]
    for t in range(1, 16):
        total = total + grs[t]
    gc[mode, q] = total

    def gram_copy(peer, d):
        to = (mode + d) % 4
        ref = gc.at[mode, q]
        return remote(ref, ref, fsend.at[peer + 4, to], frecv.at[q + 4, mode], peer * 16 + j, to)

    def gram_in(peer, c):
        ref = gc.at[c, peer]
        return remote(ref, ref, fsend.at[peer + 4, c], frecv.at[peer + 4, c], peer * 16 + j, right)

    for peer in quarters:
        for d in (2, 1, 3, 0):
            gram_copy(peer, d).start()
    for d in (2, 1, 3):
        gram_copy(q, d).start()

    for peer in quarters:
        quarter_in(mc.at[peer, top], 5, peer).wait_recv()
    quarter_in(mc.at[partner, pl.ds(8, 16)], 6, partner).wait_recv()

    def unit(first, count):
        rows = lax.broadcasted_iota(jnp.int32, (count, 128), 0) + first
        cols = lax.broadcasted_iota(jnp.int32, (count, 128), 1) + mode * 128
        return (rows % 512 == cols).astype(F32)

    mroot_ref[...] = (
        ms[0, rows8(q)] + (mc[partner, 0:8] + mc[far0, 0:8] + mc[far1, 0:8]) + unit(leaf * 8, 8)
    )
    mmid_ref[...] = ms[0, mid_of] + mc[partner, 8:24] + unit(leaf * 16, 16)
    mlow_ref[...] = ms[0, 64:96] + unit(leaf * 32, 32)
    for result in results[2:5]:
        result.start()
    for h in range(3):
        for kind in range(6):
            chunk(h, kind).wait_send()
    for copy in init_out:
        copy.wait_send()
    for s in range(ITERS):
        for h in range(3):
            if h == 0:
                group_all(3 * s, ag.at[s, h]).wait_send()
                group_all(9 + 3 * s, rs.at[s, h]).wait_send()
                pass_on(s, core).wait_send()
                continue
            (group_all if h == 1 else chips_all)(3 * s + h, ag.at[s, h]).wait_send()
            chips_all(9 + 3 * s + h, rs.at[s, h]).wait_send()
            cross(s, h).wait_send()
    for s in range(ITERS - 1):
        for peer in quarters:
            quarter_copy(cs.at[s, 0], cb.at[s, 0, q], 1 + s, peer).wait_send()
        quarter_copy(cs.at[s, 1], cb.at[s, 1, q], 3 + s, partner).wait_send()
    mass_core.wait_send()
    for h in range(3):
        for t in chips:
            mass_copy(h, t).wait_send()
    for k in range(3):
        y_copy(yl, 0, k).wait_send()
        y_copy(iy, 1, k).wait_send()

    for peer in quarters:
        for d in range(4):
            gram_in(peer, (mode + d) % 4).wait_recv()
    for d in range(1, 4):
        gram_in(q, (mode + d) % 4).wait_recv()
    sums = [(gc[c, 0] + gc[c, 1]) + (gc[c, 2] + gc[c, 3]) for c in range(4)]
    gag[j, 0] = sums[0]
    gag[j, 1] = sums[1]
    gag[j, 2] = jnp.where(low_lanes[0:8], pltpu.roll(sums[2], 64, 1), sums[3])
    group_start(19, lambda t: gag.at[j], gag.at[j])
    for d in range(4):
        for peer in (far0, far1):
            owner_copy(peer, d, 8).wait_send()
        owner_copy(partner, d, 24).wait_send()
        if d > 0:
            owner_copy(q, d, 56).wait_send()
            gram_copy(q, d).wait_send()
        for peer in quarters:
            gram_copy(peer, d).wait_send()
    for copy in mass_out:
        copy.wait_send()
    group_all(18, grs).wait_send()
    group_all(19, gag).wait_recv()
    results[5].start()
    group_all(19, gag).wait_send()
    for result in results:
        result.wait()


def run_sweeps(leaf_sizes, stiff, coupling, start_leaf, starts, omegas):
    scratch = [
        (3, 4, 128, 512),
        (3, 4, 128, 512),
        (3, 4, 128, 512),
        (3, 512, 128),
        (1, 512),
        (64, 512),
        (8, 64),
        (16, 64),
        (32, 64),
        (1, 8),
        (1, 16),
        (1, 32),
        (56, 128),
        (4, 24, 128),
        (1536, 128),
        (1536, 128),
        (3, 3, 16, 16, 128),
        (3, 2, 8, 16, 128),
        (3, 2, 8, 16, 128),
        (3, 3, 16, 16, 128),
        (2, 2, 16, 128),
        (2, 2, 4, 16, 128),
        (3, 3, 16, 16, 128),
        (4, 56, 128),
        (4, 4, 56, 128),
        (4, 64, 512),
        (4, 56, 128),
        (128, 128),
        (16, 8, 128),
        (4, 4, 8, 128),
        (16, 3, 8, 128),
        (4, 56, 128),
        (8, 128),
        (16, 128),
        (32, 128),
        (3, 512, 128),
        (2, 8, 96, 128),
        (8, 96, 128),
        (8, 96, 128),
        (8, 96, 128),
        (4, 24, 128),
    ]
    sems = [(11,), (6,), (3, 6), (3, 6), (20,), (20,), (3, 8), (3, 8), (10,), (10,)]
    sems += [(7, 4), (7, 4), (2, 3), (2, 3), (8, 4), (8, 4)]
    shapes = [(16, 3, 8, 128), (4, 64, 512), (4, 56, 128), (8, 128), (16, 128), (32, 128)]
    return pl.pallas_call(
        sweeps_kernel,
        out_shape=[jax.ShapeDtypeStruct(shape, F32) for shape in shapes],
        in_specs=[pl.BlockSpec(memory_space=pltpu.SMEM)]
        + [pl.BlockSpec(memory_space=pltpu.HBM)] * 9,
        out_specs=[pl.BlockSpec(memory_space=pltpu.HBM)] * 6,
        scratch_shapes=[
            pltpu.VMEM(shape, BF16 if n in (1, 2) else F32) for n, shape in enumerate(scratch)
        ]
        + [pltpu.SemaphoreType.DMA(shape) for shape in sems],
        compiler_params=pltpu.CompilerParams(
            collective_id=0, has_side_effects=True, vmem_limit_bytes=64 * 1024 * 1024
        ),
        name="sweeps",
    )(leaf_sizes, stiff, coupling, start_leaf, *starts, *omegas)


def factor_block(a):
    rows = [a[8 * r : 8 * r + 8, :] for r in range(8)]
    sub = lax.broadcasted_iota(jnp.int32, (8, 128), 0)
    pivots = []
    for p in range(8):
        cols = []
        for k in range(8):
            pick = jnp.full((8, 128), 8 * p + k, jnp.int32)
            cols.append([jnp.take_along_axis(rows[r], pick, axis=1) for r in range(p, 8)])
        diag = []
        for k in range(0, 8, 2):
            head, cross = [jnp.broadcast_to(cols[k][0][n : n + 1, :], (8, 128)) for n in (k, k + 1)]
            tail = jnp.broadcast_to(cols[k + 1][0][k + 1 : k + 2, :], (8, 128))
            det = head * tail - cross * cross
            inv0 = 1.0 / head
            inv1 = head * (1.0 / det)
            ratio = cross * inv0
            diag += [head, det * inv0]
            first = [c * inv0 for c in cols[k]]
            first[0] = jnp.where(sub > k, first[0], 0.0)
            second = [(c - f * cross) * inv1 for c, f in zip(cols[k + 1], first)]
            second[0] = jnp.where(sub > k + 1, second[0], 0.0)
            for k2 in range(k + 2, 8):
                up0 = jnp.broadcast_to(cols[k2][0][k : k + 1, :], (8, 128))
                up1 = jnp.broadcast_to(cols[k2][0][k + 1 : k + 2, :], (8, 128)) - ratio * up0
                cols[k2] = [c - (f * up0 + g * up1) for c, f, g in zip(cols[k2], first, second)]
            lead0 = jnp.broadcast_to(rows[p][k : k + 1, :], (8, 128))
            lead1 = jnp.broadcast_to(rows[p][k + 1 : k + 2, :], (8, 128)) - ratio * lead0
            for r in range(p, 8):
                rows[r] = rows[r] - (first[r - p] * lead0 + second[r - p] * lead1)
        scale = diag[0]
        for k in range(1, 8):
            scale = jnp.where(sub == k, diag[k], scale)
        pivots.append(lax.rsqrt(scale))
    return jnp.concatenate([row * pivot for row, pivot in zip(rows, pivots)], axis=0)


def finish_kernel(
    gram_in,
    next_in,
    iface_in,
    mroot_in,
    mmid_in,
    mlow_in,
    leaf_out,
    root_out,
    mid_out,
    low_out,
    mroot_out,
    mmid_out,
    mlow_out,
    gram_ref,
    next_ref,
    iface_ref,
    full,
    lower,
    sem,
):
    mode = lax.axis_index("mode")
    moves = (
        (gram_in, gram_ref),
        (next_in, next_ref),
        (iface_in, iface_ref),
        (mroot_in, mroot_out),
        (mmid_in, mmid_out),
        (mlow_in, mlow_out),
    )
    moves = [pltpu.make_async_copy(a, b, sem.at[n]) for n, (a, b) in enumerate(moves)]
    for move in moves:
        move.start()
    moves[0].wait()
    low_lanes = lax.broadcasted_iota(jnp.int32, (128, 128), 1) < 64
    parts = [jnp.concatenate([gram_ref[t, c] for t in range(16)], axis=0) for c in range(3)]
    turned = [pltpu.roll(parts[c], 64, 1) for c in range(2)]
    first = jnp.where(low_lanes, parts[0], turned[1])
    cross = jnp.where(low_lanes, turned[0], parts[1])
    first = 0.5 * (first + first.T)
    second = 0.5 * (parts[2] + parts[2].T)
    gram = jnp.concatenate(
        [jnp.concatenate([first, cross.T], axis=1), jnp.concatenate([cross, second], axis=1)], axis=0
    )
    r = lax.broadcasted_iota(jnp.int32, (256, 256), 0)
    c = lax.broadcasted_iota(jnp.int32, (256, 256), 1)
    corner = jnp.where(r == c, gram, 0.0)
    down = lax.rsqrt(jnp.sum(corner, axis=1, keepdims=True))
    over = lax.rsqrt(jnp.sum(corner, axis=0, keepdims=True))
    full[:, 0:256] = gram * down * over
    full[:, 256:512] = jnp.where(r == c, jnp.broadcast_to(down, (256, 256)), 0.0)
    unit = (
        lax.broadcasted_iota(jnp.int32, (64, 64), 0) == lax.broadcasted_iota(jnp.int32, (64, 64), 1)
    ).astype(F32)
    for k in range(4):
        first = 64 * k
        block = full[first : first + 64, first : first + 64]
        weight = factor_block(jnp.concatenate([block, unit], axis=1))[:, 64:128]
        right = 128 * (k // 2)
        panel = nn(weight, full[first : first + 64, right:512])
        lower[first : first + 64, :] = panel[:, 256 - right : 512 - right]
        if k < 3:
            below = panel[:, first + 64 - right : 256 - right]
            full[first + 64 : 256, right:512] = full[first + 64 : 256, right:512] - tn(below, panel)
    own = lower[pl.ds(pl.multiple_of(mode * 64, 64), 64), :]
    for move in moves[1:]:
        move.wait()
    leaf_out[...] = nn(own, next_ref[...].reshape(256, 512))
    iface = jnp.concatenate([iface_ref[c][:, 0:64] for c in range(4)], axis=1)
    done = nt(iface, own)
    root_out[...] = done[0:8]
    mid_out[...] = done[8:24]
    low_out[...] = done[24:56]


def run_finish(gram, modal, iface, masses):
    vmem = pl.BlockSpec(memory_space=pltpu.VMEM)
    hbm = pl.BlockSpec(memory_space=pltpu.HBM)
    shapes = [(64, 512), (8, 64), (16, 64), (32, 64), (8, 128), (16, 128), (32, 128)]
    return pl.pallas_call(
        finish_kernel,
        out_shape=[jax.ShapeDtypeStruct(shape, F32) for shape in shapes],
        in_specs=[hbm] * 6,
        out_specs=[vmem] * 4 + [hbm] * 3,
        scratch_shapes=[
            pltpu.VMEM((16, 3, 8, 128), F32),
            pltpu.VMEM((4, 64, 512), F32),
            pltpu.VMEM((4, 56, 128), F32),
            pltpu.VMEM((256, 512), F32),
            pltpu.VMEM((256, 256), F32),
            pltpu.SemaphoreType.DMA((6,)),
        ],
        compiler_params=pltpu.CompilerParams(vmem_limit_bytes=64 * 1024 * 1024),
        name="finish",
    )(gram, modal, iface, *masses)


def local(
    leaf_sizes,
    leaf_stiffness,
    coupling,
    omega_root,
    omega_mid,
    omega_low,
    start_leaf,
    start_root,
    start_mid,
    start_low,
):
    gram, modal, iface, *masses = run_sweeps(
        leaf_sizes,
        leaf_stiffness.reshape(1, -1),
        coupling,
        start_leaf,
        [start_root.T, start_mid.T, start_low.T],
        [omega_root.reshape(1, -1), omega_mid.reshape(1, -1), omega_low.reshape(1, -1)],
    )
    leaf, root, mid, low, *masses = run_finish(gram, modal, iface, masses)
    return (leaf, root.T, mid.T, low.T, *masses)


def solution(mesh):
    placed = (
        P("leaf"),
        P("leaf"),
        P(None, "leaf", "mode"),
        P("leaf"),
        P("leaf"),
        P("leaf"),
        P("mode", "leaf"),
        P("mode", "leaf"),
        P("mode", "leaf"),
        P("mode", "leaf"),
    )
    return jax.shard_map(
        local,
        mesh=mesh,
        in_specs=placed,
        out_specs=(
            P("mode", "leaf"),
            P("mode", "leaf"),
            P("mode", "leaf"),
            P("mode", "leaf"),
            P("leaf", "mode"),
            P("leaf", "mode"),
            P("leaf", "mode"),
        ),
        check_vma=False,
    )
```

```python
import functools
import jax
import jax.numpy as jnp
from jax import lax
from jax.experimental import pallas as pl
from jax.experimental.pallas import tpu as pltpu
from jax.sharding import PartitionSpec as P

ITERS = 3
ROWS = 36352.0
SCALE = 2.0**-12
MESH = pl.DeviceIdType.MESH
HI = lax.Precision.HIGHEST
F32 = jnp.float32
BF16 = jnp.bfloat16
NEAR_FIRST = ((0, 1), (0, 3), (1, 0), (0, 2), (1, 1), (1, 3), (1, 2))


def nt(a, b):
    return lax.dot_general(a, b, (((1,), (1,)), ((), ())), precision=HI, preferred_element_type=F32)


def nn(a, b):
    return lax.dot_general(a, b, (((1,), (0,)), ((), ())), precision=HI, preferred_element_type=F32)


def tn(a, b):
    return lax.dot_general(a, b, (((0,), (0,)), ((), ())), precision=HI, preferred_element_type=F32)


def halves(x):
    high = x.astype(BF16)
    return high, (x - high.astype(F32)).astype(BF16)


def nn16(a, b):
    return lax.dot_general(a, b, (((1,), (0,)), ((), ())), preferred_element_type=F32)


def nt16(a, b):
    return lax.dot_general(a, b, (((1,), (1,)), ((), ())), preferred_element_type=F32)


def root_row(q, n):
    return q * 128 + 8 * n


def mid_row(half, n):
    return 512 + half * 256 + 16 * n


def low_row(n):
    return 1024 + 32 * n


def remote(src, dst, send, recv, leaf, mode):
    return pltpu.make_async_remote_copy(
        src_ref=src,
        dst_ref=dst,
        send_sem=send,
        recv_sem=recv,
        device_id=(leaf, mode),
        device_id_type=MESH,
    )


def column(ref):
    n = ref.shape[1]
    r = lax.broadcasted_iota(jnp.int32, (n, n), 0)
    c = lax.broadcasted_iota(jnp.int32, (n, n), 1)
    spread = jnp.where(r == c, jnp.broadcast_to(ref[...], (n, n)), 0.0)
    return jnp.broadcast_to(jnp.sum(spread, axis=1, keepdims=True), (n, 64))


def sweeps_kernel(
    sizes_ref,
    stiff_in,
    coupling_ref,
    leaf_in,
    sroot_in,
    smid_in,
    slow_in,
    oroot_in,
    omid_in,
    olow_in,
    gram_out,
    next_out,
    iface_out,
    mroot_out,
    mmid_out,
    mlow_out,
    gt,
    ghi,
    glo,
    raw,
    stiff_ref,
    leaf_ref,
    sroot_ref,
    smid_ref,
    slow_ref,
    oroot_ref,
    omid_ref,
    olow_ref,
    own,
    init,
    iv,
    tt,
    tp,
    xb,
    xs,
    rs,
    cs,
    cb,
    ag,
    fb,
    fr,
    yl,
    iy,
    gp,
    grs,
    gc,
    gag,
    iface_ref,
    mroot_ref,
    mmid_ref,
    mlow_ref,
    ms,
    mp,
    mxb,
    mxs,
    mrs,
    mc,
    lsem,
    osem,
    gsend,
    grecv,
    psend,
    precv,
    hsend,
    hrecv,
    xsend,
    xrecv,
    csend,
    crecv,
    ysend,
    yrecv,
    fsend,
    frecv,
):
    leaf = lax.axis_index("leaf")
    mode = lax.axis_index("mode")
    q = leaf // 16
    j = leaf % 16
    base = q * 16
    core = j % 2
    chip = j // 2
    chips = [((chip // 4 + dz) % 2) * 4 + (chip + dx) % 4 for dz, dx in NEAR_FIRST]
    right = (mode + 1) % 4
    left = (mode + 3) % 4
    across = (mode + 2) % 4
    modes = (right, left, across)
    partner = q + 1 - 2 * (q % 2)
    half_base = q - q % 2
    far0 = (q + 2) % 4
    far1 = (partner + 2) % 4
    quarters = (far0, far1, partner)

    around = [(j + d) % 16 for d in range(1, 16)]
    barrier = pltpu.get_barrier_semaphore()

    def greet(to_leaf, to_mode):
        pl.semaphore_signal(barrier, inc=1, device_id=(to_leaf, to_mode), device_id_type=MESH)

    for peer in quarters:
        for to in (mode,) + modes:
            greet(peer * 16 + j, to)
    for to in modes:
        greet(leaf, to)
    for t in around:
        greet(base + t, mode)

    loads = [pltpu.make_async_copy(coupling_ref.at[h], raw.at[h], lsem.at[h]) for h in range(3)]
    small = [
        (sroot_in, sroot_ref),
        (smid_in, smid_ref),
        (slow_in, slow_ref),
        (oroot_in, oroot_ref),
        (omid_in, omid_ref),
        (olow_in, olow_ref),
        (stiff_in, stiff_ref),
        (leaf_in, leaf_ref),
    ]
    loads += [pltpu.make_async_copy(a, b, lsem.at[3 + n]) for n, (a, b) in enumerate(small)]
    for load in loads:
        load.start()
    for load in loads[3:]:
        load.wait()
    own[0:8] = jnp.concatenate([sroot_ref[...] * SCALE, column(oroot_ref)], axis=1)
    own[8:24] = jnp.concatenate([smid_ref[...] * SCALE, column(omid_ref)], axis=1)
    own[24:56] = jnp.concatenate([slow_ref[...] * SCALE, column(olow_ref)], axis=1)
    init[q] = own[0:24]
    for h in range(3):
        loads[h].wait()
        gt[h, mode] = raw[h].T
    pl.semaphore_wait(barrier, 30)

    def part(c, h, n):
        return gt.at[h, c, pl.ds(64 * n, 64)]

    def chunk(h, kind):
        c, n, peer = (
            (mode, 0, right),
            (mode, 1, left),
            (mode, 1, right),
            (mode, 0, left),
            (left, 0, right),
            (right, 1, left),
        )[kind]
        return remote(part(c, h, n), part(c, h, n), gsend.at[h, kind], grecv.at[h, kind], leaf, peer)

    def chunk_in(h, kind):
        c, n = ((left, 0), (right, 1), (left, 1), (right, 0), (across, 0), (across, 1))[kind]
        return remote(part(c, h, n), part(c, h, n), gsend.at[h, kind], grecv.at[h, kind], leaf, right)

    for kinds in ((0, 1), (2, 3)):
        for h in range(3):
            for kind in kinds:
                chunk(h, kind).start()

    def quarter_copy(src, dst, phase, peer):
        return remote(src, dst, csend.at[phase, peer], crecv.at[phase, q], peer * 16 + j, mode)

    def quarter_in(dst, phase, peer):
        return remote(dst, dst, csend.at[phase, peer], crecv.at[phase, peer], peer * 16 + j, mode)

    top = pl.ds(0, 8)
    init_out = [
        quarter_copy(init.at[q, top], init.at[q, top], 0, far0),
        quarter_copy(init.at[q, top], init.at[q, top], 0, far1),
        quarter_copy(init.at[q], init.at[q], 0, partner),
    ]
    for copy in init_out:
        copy.start()
    quarter_in(init.at[partner], 0, partner).wait_recv()
    quarter_in(init.at[far0, top], 0, far0).wait_recv()
    quarter_in(init.at[far1, top], 0, far1).wait_recv()

    low_lanes = lax.broadcasted_iota(jnp.int32, (16, 128), 1) < 64

    def packs(a, b):
        return (
            jnp.where(low_lanes, a, pltpu.roll(b, 64, 1)),
            jnp.where(low_lanes, pltpu.roll(a, 64, 1), b),
        )

    iroot, wroot = packs(
        jnp.concatenate([init[0, 0:8], init[1, 0:8]], axis=0),
        jnp.concatenate([init[2, 0:8], init[3, 0:8]], axis=0),
    )
    imid, wmid = packs(init[half_base, 8:24], init[half_base + 1, 8:24])
    ilow, wlow = packs(own[24:40], own[40:56])
    state = [iroot, imid, ilow]
    omega = [wroot, wmid, wlow]

    def group_start(phase, src_of, dst):
        for t in around:
            remote(src_of(t), dst, psend.at[phase], precv.at[phase], base + t, mode).start()

    def group_all(phase, landing):
        some = landing.at[pl.ds(0, 15)]
        return remote(some, some, psend.at[phase], precv.at[phase], base + (j + 1) % 16, mode)

    mine = 8 * core + chip
    other = leaf + 1 - 2 * core

    def chips_start(phase, src_of, dst):
        for t in reversed(chips):
            remote(src_of(t), dst, psend.at[phase], precv.at[phase], base + 2 * t + core, mode).start()

    def chips_all(phase, landing):
        some = landing.at[pl.ds(0, 7)]
        return remote(some, some, psend.at[phase], precv.at[phase], other, mode)

    def core_copy(n, src, dst):
        return remote(src, dst, xsend.at[n], xrecv.at[n], other, mode)

    def spread_start(s, h):
        slot = mine if h == 2 else j
        ag[s, h, slot] = state[h]
        block = ag.at[s, h, slot]
        if h == 2:
            chips_start(3 * s + h, lambda t: block, block)
        else:
            group_start(3 * s + h, lambda t: block, block)

    def pass_on(s, c):
        blocks = ag.at[s, 2, pl.ds(8 * c, 8)]
        return core_copy(s, blocks, blocks)

    def spread_forward(s):
        chips_all(3 * s + 2, ag.at[s, 2]).wait_recv()
        pass_on(s, core).start()

    def spread_wait(s, h):
        if h == 2:
            pass_on(s, 1 - core).wait_recv()
        else:
            group_all(3 * s + h, ag.at[s, h]).wait_recv()
        for n in range(16):
            block = ag[s, h, n]
            turned = pltpu.roll(block, 64, 1)
            if h == 0:
                for k in range(2):
                    iv[root_row(k, n) : root_row(k, n) + 8, :] = block[8 * k : 8 * k + 8]
                    iv[root_row(k + 2, n) : root_row(k + 2, n) + 8, :] = turned[8 * k : 8 * k + 8]
            elif h == 1:
                iv[mid_row(0, n) : mid_row(0, n) + 16, :] = block
                iv[mid_row(1, n) : mid_row(1, n) + 16, :] = turned
            else:
                first = low_row(2 * (n % 8) + n // 8)
                iv[first : first + 16, :] = block
                iv[first + 16 : first + 32, :] = turned

    def pack_terms(s, h):
        for n in range(16):
            if h == 0:
                a, b = [
                    jnp.concatenate(
                        [tt[root_row(k, n) : root_row(k, n) + 8], tt[root_row(k + 1, n) : root_row(k + 1, n) + 8]],
                        axis=0,
                    )
                    for k in (0, 2)
                ]
            elif h == 1:
                a, b = [tt[mid_row(k, n) : mid_row(k, n) + 16] for k in range(2)]
            else:
                a, b = tt[low_row(n) : low_row(n) + 16], tt[low_row(n) + 16 : low_row(n) + 32]
            tp[s, h, n if h == 0 else 8 * (n % 2) + n // 2] = jnp.where(low_lanes, a, b)

    def cross(s, h):
        return core_copy(1 + 2 * s + h + 1, tp.at[s, h, pl.ds(8 * (1 - core), 8)], xb.at[s, h - 1])

    def reduce_start(s, h):
        if h > 0:
            cross(s, h).start()
            return
        group_start(9 + 3 * s, lambda t: tp.at[s, 0, t], rs.at[s, 0, j])
        rs[s, 0, j] = tp[s, 0, j]

    def reduce_middle(s, h):
        cross(s, h).wait_recv()
        xs[s, h - 1] = tp[s, h, pl.ds(8 * core, 8)] + xb[s, h - 1]
        chips_start(9 + 3 * s + h, lambda t: xs.at[s, h - 1, t], rs.at[s, h, chip])
        rs[s, h, chip] = xs[s, h - 1, chip]

    def reduce_end(s, h):
        if h == 0:
            group_all(9 + 3 * s, rs.at[s, h]).wait_recv()
        else:
            chips_all(9 + 3 * s + h, rs.at[s, h]).wait_recv()
        total = rs[s, h, 0]
        for n in range(1, 16 if h == 0 else 8):
            total = total + rs[s, h, n]
        return total

    for h in range(3):
        spread_start(0, h)

    coord = lax.broadcasted_iota(jnp.int32, (1, 128), 1)
    live = jnp.concatenate([(coord < sizes_ref[n]).astype(F32) for n in range(4)], axis=1)
    stiff = stiff_ref[...]
    inverse = live / stiff
    weighted = inverse * inverse
    m = leaf_ref[...] * live * SCALE

    def split_chunk(c, h):
        ghi[h, c], glo[h, c] = halves(gt[h, c])

    def apply_chunk(c, h):
        first = pl.multiple_of(h * 512 + c * 128, 128)
        high, low = halves(iv[pl.ds(first, 128), :][:, 0:64].T)
        both = nn16(jnp.concatenate([high, low], axis=0), ghi[h, c])
        return both[0:64] + both[64:128] + nn16(high, glo[h, c])

    def project(h):
        high, low = halves(gt[h].reshape(512, 512) * weighted)
        mine = jnp.concatenate([ghi[h, mode], glo[h, mode]], axis=0)
        both = nt16(high, mine)
        ms[h] = both[:, 0:128] + both[:, 128:256] + nt16(low, mine[0:128])

    for h in range(3):
        for kind in (0, 1):
            chunk_in(h, kind).wait_recv()
            chunk(h, kind + 4).start()
        split_chunk(mode, h)
    spread_forward(0)
    for h in (0, 1, 2):
        spread_wait(0, h)
    coupled = apply_chunk(mode, 0) + apply_chunk(mode, 1) + apply_chunk(mode, 2)
    for h in range(3):
        chunk_in(h, 2).wait_recv()
        chunk_in(h, 3).wait_recv()
        for c in (left, right):
            split_chunk(c, h)
            coupled = coupled + apply_chunk(c, h)
    for h in range(3):
        chunk_in(h, 4).wait_recv()
        chunk_in(h, 5).wait_recv()
        split_chunk(across, h)
        coupled = coupled + apply_chunk(across, h)

    def mass_copy(h, t):
        rows = pl.ds(32 * h, 32)
        return remote(
            mxs.at[t, rows], mrs.at[chip, rows], hsend.at[h, t], hrecv.at[h, chip], base + 2 * t + core, mode
        )

    def mass_in(h, t):
        came = mrs.at[t, pl.ds(32 * h, 32)]
        return remote(came, came, hsend.at[h, t], hrecv.at[h, t], base + 2 * t + core, mode)

    def mass_part(h):
        for t in reversed(chips):
            mass_copy(h, t).start()

    mass_core = core_copy(9, mp.at[1 - core], mxb)

    def pack_masses():
        for t in range(16):
            for k in range(4):
                mp[t % 2, t // 2, 8 * k : 8 * k + 8] = ms[0, 128 * k + 8 * t : 128 * k + 8 * t + 8]
            for k in range(2):
                mp[t % 2, t // 2, 32 + 16 * k : 48 + 16 * k] = ms[
                    1, 256 * k + 16 * t : 256 * k + 16 * t + 16
                ]
            mp[t % 2, t // 2, 64:96] = ms[2, 32 * t : 32 * t + 32]

    def y_copy(ref, phase, k):
        return remote(ref.at[mode], ref.at[mode], ysend.at[phase, k], yrecv.at[phase, k], leaf, modes[k])

    def y_in(ref, phase, k):
        came = ref.at[(left, right, across)[k]]
        return remote(came, came, ysend.at[phase, k], yrecv.at[phase, k], leaf, right)

    for s in range(ITERS):
        last = s == ITERS - 1
        if s > 0:
            coupled = jnp.zeros((64, 512), F32)
            for h in (2, 0, 1):
                spread_wait(s, h)
                high, low = halves(iv[512 * h : 512 * h + 512, :][:, 0:64].T)
                both = nn16(jnp.concatenate([high, low], axis=0), ghi[h].reshape(512, 512))
                coupled = coupled + (both[0:64] + both[64:128] + nn16(high, glo[h].reshape(512, 512)))
        modal_mass = live * m - inverse * coupled
        m = inverse * modal_mass
        high, low = halves(m)
        twice = jnp.concatenate([high, high], axis=0)
        four = jnp.concatenate([twice, low, low], axis=0)
        for h in range(3):
            both = nt16(ghi[h].reshape(512, 512), four)
            tt[512 * h : 512 * h + 512, :] = (
                both[:, 0:128] + both[:, 128:256] + nt16(glo[h].reshape(512, 512), twice)
            )
            pack_terms(s, h)
            reduce_start(s, h)
        for h in (1, 2):
            reduce_middle(s, h)
        if last:
            yl[mode] = m
            for k in range(3):
                y_copy(yl, 0, k).start()
        if s == 0:
            for h in range(3):
                project(h)
            pack_masses()
            mass_core.start()
        if last:
            heavy = m * stiff
            break
        cs[s, 0] = reduce_end(s, 0)
        for peer in (far0, far1, partner):
            quarter_copy(cs.at[s, 0], cb.at[s, 0, q], 1 + s, peer).start()
        cs[s, 1] = reduce_end(s, 1)
        quarter_copy(cs.at[s, 1], cb.at[s, 1, q], 3 + s, partner).start()
        state[2] = (state[2] - reduce_end(s, 2)) / omega[2]
        spread_start(s + 1, 2)
        if s == 0:
            mass_core.wait_recv()
            mxs[...] = mp[core] + mxb[...]
            mrs[chip] = mxs[chip]
        mass_part(s)
        for peer in (partner, far0, far1):
            quarter_in(cb.at[s, 0, peer], 1 + s, peer).wait_recv()
        gone = (cs[s, 0] + cb[s, 0, partner]) + (cb[s, 0, far0] + cb[s, 0, far1])
        state[0] = (state[0] - gone) / omega[0]
        spread_start(s + 1, 0)
        quarter_in(cb.at[s, 1, partner], 3 + s, partner).wait_recv()
        state[1] = (state[1] - (cs[s, 1] + cb[s, 1, partner])) / omega[1]
        spread_start(s + 1, 1)
        spread_forward(s + 1)
        if s == ITERS - 2:
            gp[0:16] = state[0]
            gp[16:32] = pltpu.roll(state[0], 64, 1)
            piece = pl.multiple_of(16 * (q // 2) + 8 * (q % 2), 8)
            iy[mode, 0:8] = gp[pl.ds(piece, 8)]
            odd = (q % 2) == 1
            iy[mode, 8:24] = jnp.where(odd, pltpu.roll(state[1], 64, 1), state[1])
            iy[mode, 24:40] = state[2]
            iy[mode, 40:56] = pltpu.roll(state[2], 64, 1)
            for k in range(3):
                y_copy(iy, 1, k).start()

    total = reduce_end(ITERS - 1, 0)
    turned = pltpu.roll(total, 64, 1)
    for k in range(2):
        fb[k, 0:8] = total[8 * k : 8 * k + 8]
        fb[k + 2, 0:8] = turned[8 * k : 8 * k + 8]

    def owner_copy(peer, d, rows):
        rows = pl.ds(0, rows)
        to = (mode + d) % 4
        return remote(
            fb.at[peer, rows], fr.at[mode, q, rows], fsend.at[peer, to], frecv.at[q, mode], peer * 16 + j, to
        )

    def owner_in(peer, c, rows):
        ref = fr.at[c, peer, pl.ds(0, rows)]
        return remote(ref, ref, fsend.at[peer, c], frecv.at[peer, c], peer * 16 + j, right)

    for peer in (far0, far1):
        for d in (2, 1, 3, 0):
            owner_copy(peer, d, 8).start()
    total = reduce_end(ITERS - 1, 1)
    turned = pltpu.roll(total, 64, 1)
    odd = (q % 2) == 1
    fb[q, 8:24] = jnp.where(odd, turned, total)
    fb[partner, 8:24] = jnp.where(odd, total, turned)
    for d in (2, 1, 3, 0):
        owner_copy(partner, d, 24).start()
    total = reduce_end(ITERS - 1, 2)
    fb[q, 24:40] = total
    fb[q, 40:56] = pltpu.roll(total, 64, 1)
    for d in (2, 1, 3):
        owner_copy(q, d, 56).start()
    fr[mode, q] = fb[q]

    mass_part(2)
    for k in range(3):
        y_in(yl, 0, k).wait_recv()
        y_in(iy, 1, k).wait_recv()
    leaf_part = nt(yl[...].reshape(256, 512), heavy * (1.0 / ROWS))
    results = [
        pltpu.make_async_copy(a, b, osem.at[n])
        for n, (a, b) in enumerate(
            (
                (yl, next_out),
                (iface_ref, iface_out),
                (mroot_ref, mroot_out),
                (mmid_ref, mmid_out),
                (mlow_ref, mlow_out),
                (gag, gram_out),
            )
        )
    ]
    results[0].start()
    for peer in (far0, far1):
        for d in range(4):
            owner_in(peer, (mode + d) % 4, 8).wait_recv()
    for d in range(4):
        owner_in(partner, (mode + d) % 4, 24).wait_recv()
    for d in range(1, 4):
        owner_in(q, (mode + d) % 4, 56).wait_recv()
    weights = pltpu.roll(own[...], 64, 1)
    for c in range(4):
        near = fr[c, q, 0:24] + fr[c, partner, 0:24]
        near = jnp.concatenate(
            [near[0:8] + (fr[c, far0, 0:8] + fr[c, far1, 0:8]), near[8:24], fr[c, q, 24:56]], axis=0
        )
        iface_ref[c] = (iy[c] - near) / weights
    results[1].start()
    heavy_own = (iface_ref[mode] * weights * (1.0 / ROWS))[:, 0:64].T
    front = lax.broadcasted_iota(jnp.int32, (56, 128), 1) < 64
    pairs = [jnp.where(front, iface_ref[c], pltpu.roll(iface_ref[c + 1], 64, 1)) for c in (0, 2)]
    block = leaf_part + nt(jnp.concatenate(pairs, axis=1).T, heavy_own)
    gp[...] = jnp.concatenate([block[0:128], block[128:256]], axis=1)

    def rows8(t):
        return pl.ds(pl.multiple_of(8 * t, 8), 8)

    group_start(18, lambda t: gp.at[rows8(t)], grs.at[j])
    grs[j] = gp[rows8(j)]
    for h in range(3):
        for t in chips:
            mass_in(h, t).wait_recv()
    total = mrs[0]
    for t in range(1, 8):
        total = total + mrs[t]
    ms[0, 0:96] = total
    mid_of = pl.ds(pl.multiple_of(32 + 16 * (q % 2), 8), 16)
    mid_to = pl.ds(pl.multiple_of(48 - 16 * (q % 2), 8), 16)
    mass_out = [quarter_copy(ms.at[0, rows8(k)], mc.at[q, top], 5, k) for k in quarters]
    mass_out.append(quarter_copy(ms.at[0, mid_to], mc.at[q, pl.ds(8, 16)], 6, partner))
    for copy in mass_out:
        copy.start()

    group_all(18, grs).wait_recv()
    total = grs[0]
    for t in range(1, 16):
        total = total + grs[t]
    gc[mode, q] = total

    def gram_copy(peer, d):
        to = (mode + d) % 4
        ref = gc.at[mode, q]
        return remote(ref, ref, fsend.at[peer + 4, to], frecv.at[q + 4, mode], peer * 16 + j, to)

    def gram_in(peer, c):
        ref = gc.at[c, peer]
        return remote(ref, ref, fsend.at[peer + 4, c], frecv.at[peer + 4, c], peer * 16 + j, right)

    for peer in quarters:
        for d in (2, 1, 3, 0):
            gram_copy(peer, d).start()
    for d in (2, 1, 3):
        gram_copy(q, d).start()

    for peer in quarters:
        quarter_in(mc.at[peer, top], 5, peer).wait_recv()
    quarter_in(mc.at[partner, pl.ds(8, 16)], 6, partner).wait_recv()

    def unit(first, count):
        rows = lax.broadcasted_iota(jnp.int32, (count, 128), 0) + first
        cols = lax.broadcasted_iota(jnp.int32, (count, 128), 1) + mode * 128
        return (rows % 512 == cols).astype(F32)

    mroot_ref[...] = (
        ms[0, rows8(q)] + (mc[partner, 0:8] + mc[far0, 0:8] + mc[far1, 0:8]) + unit(leaf * 8, 8)
    )
    mmid_ref[...] = ms[0, mid_of] + mc[partner, 8:24] + unit(leaf * 16, 16)
    mlow_ref[...] = ms[0, 64:96] + unit(leaf * 32, 32)
    for result in results[2:5]:
        result.start()
    for h in range(3):
        for kind in range(6):
            chunk(h, kind).wait_send()
    for copy in init_out:
        copy.wait_send()
    for s in range(ITERS):
        for h in range(3):
            if h == 0:
                group_all(3 * s, ag.at[s, h]).wait_send()
                group_all(9 + 3 * s, rs.at[s, h]).wait_send()
                pass_on(s, core).wait_send()
                continue
            (group_all if h == 1 else chips_all)(3 * s + h, ag.at[s, h]).wait_send()
            chips_all(9 + 3 * s + h, rs.at[s, h]).wait_send()
            cross(s, h).wait_send()
    for s in range(ITERS - 1):
        for peer in quarters:
            quarter_copy(cs.at[s, 0], cb.at[s, 0, q], 1 + s, peer).wait_send()
        quarter_copy(cs.at[s, 1], cb.at[s, 1, q], 3 + s, partner).wait_send()
    mass_core.wait_send()
    for h in range(3):
        for t in chips:
            mass_copy(h, t).wait_send()
    for k in range(3):
        y_copy(yl, 0, k).wait_send()
        y_copy(iy, 1, k).wait_send()

    for peer in quarters:
        for d in range(4):
            gram_in(peer, (mode + d) % 4).wait_recv()
    for d in range(1, 4):
        gram_in(q, (mode + d) % 4).wait_recv()
    sums = [(gc[c, 0] + gc[c, 1]) + (gc[c, 2] + gc[c, 3]) for c in range(4)]
    gag[j, 0] = sums[0]
    gag[j, 1] = sums[1]
    gag[j, 2] = jnp.where(low_lanes[0:8], pltpu.roll(sums[2], 64, 1), sums[3])
    group_start(19, lambda t: gag.at[j], gag.at[j])
    for d in range(4):
        for peer in (far0, far1):
            owner_copy(peer, d, 8).wait_send()
        owner_copy(partner, d, 24).wait_send()
        if d > 0:
            owner_copy(q, d, 56).wait_send()
            gram_copy(q, d).wait_send()
        for peer in quarters:
            gram_copy(peer, d).wait_send()
    for copy in mass_out:
        copy.wait_send()
    group_all(18, grs).wait_send()
    group_all(19, gag).wait_recv()
    results[5].start()
    group_all(19, gag).wait_send()
    for result in results:
        result.wait()


def run_sweeps(leaf_sizes, stiff, coupling, start_leaf, starts, omegas):
    scratch = [
        (3, 4, 128, 512),
        (3, 4, 128, 512),
        (3, 4, 128, 512),
        (3, 512, 128),
        (1, 512),
        (64, 512),
        (8, 64),
        (16, 64),
        (32, 64),
        (1, 8),
        (1, 16),
        (1, 32),
        (56, 128),
        (4, 24, 128),
        (1536, 128),
        (1536, 128),
        (3, 3, 16, 16, 128),
        (3, 2, 8, 16, 128),
        (3, 2, 8, 16, 128),
        (3, 3, 16, 16, 128),
        (2, 2, 16, 128),
        (2, 2, 4, 16, 128),
        (3, 3, 16, 16, 128),
        (4, 56, 128),
        (4, 4, 56, 128),
        (4, 64, 512),
        (4, 56, 128),
        (128, 128),
        (16, 8, 128),
        (4, 4, 8, 128),
        (16, 3, 8, 128),
        (4, 56, 128),
        (8, 128),
        (16, 128),
        (32, 128),
        (3, 512, 128),
        (2, 8, 96, 128),
        (8, 96, 128),
        (8, 96, 128),
        (8, 96, 128),
        (4, 24, 128),
    ]
    sems = [(11,), (6,), (3, 6), (3, 6), (20,), (20,), (3, 8), (3, 8), (10,), (10,)]
    sems += [(7, 4), (7, 4), (2, 3), (2, 3), (8, 4), (8, 4)]
    shapes = [(16, 3, 8, 128), (4, 64, 512), (4, 56, 128), (8, 128), (16, 128), (32, 128)]
    return pl.pallas_call(
        sweeps_kernel,
        out_shape=[jax.ShapeDtypeStruct(shape, F32) for shape in shapes],
        in_specs=[pl.BlockSpec(memory_space=pltpu.SMEM)]
        + [pl.BlockSpec(memory_space=pltpu.HBM)] * 9,
        out_specs=[pl.BlockSpec(memory_space=pltpu.HBM)] * 6,
        scratch_shapes=[
            pltpu.VMEM(shape, BF16 if n in (1, 2) else F32) for n, shape in enumerate(scratch)
        ]
        + [pltpu.SemaphoreType.DMA(shape) for shape in sems],
        compiler_params=pltpu.CompilerParams(
            collective_id=0, has_side_effects=True, vmem_limit_bytes=64 * 1024 * 1024
        ),
        name="sweeps",
    )(leaf_sizes, stiff, coupling, start_leaf, *starts, *omegas)


def factor_block(a):
    rows = [a[8 * r : 8 * r + 8, :] for r in range(8)]
    sub = lax.broadcasted_iota(jnp.int32, (8, 128), 0)
    pivots = []
    for p in range(8):
        cols = []
        for k in range(8):
            pick = jnp.full((8, 128), 8 * p + k, jnp.int32)
            cols.append([jnp.take_along_axis(rows[r], pick, axis=1) for r in range(p, 8)])
        diag = []
        for k in range(0, 8, 2):
            head, cross = [jnp.broadcast_to(cols[k][0][n : n + 1, :], (8, 128)) for n in (k, k + 1)]
            tail = jnp.broadcast_to(cols[k + 1][0][k + 1 : k + 2, :], (8, 128))
            det = head * tail - cross * cross
            inv0 = 1.0 / head
            inv1 = head * (1.0 / det)
            ratio = cross * inv0
            diag += [head, det * inv0]
            first = [c * inv0 for c in cols[k]]
            first[0] = jnp.where(sub > k, first[0], 0.0)
            second = [(c - f * cross) * inv1 for c, f in zip(cols[k + 1], first)]
            second[0] = jnp.where(sub > k + 1, second[0], 0.0)
            for k2 in range(k + 2, 8):
                up0 = jnp.broadcast_to(cols[k2][0][k : k + 1, :], (8, 128))
                up1 = jnp.broadcast_to(cols[k2][0][k + 1 : k + 2, :], (8, 128)) - ratio * up0
                cols[k2] = [c - (f * up0 + g * up1) for c, f, g in zip(cols[k2], first, second)]
            lead0 = jnp.broadcast_to(rows[p][k : k + 1, :], (8, 128))
            lead1 = jnp.broadcast_to(rows[p][k + 1 : k + 2, :], (8, 128)) - ratio * lead0
            for r in range(p, 8):
                rows[r] = rows[r] - (first[r - p] * lead0 + second[r - p] * lead1)
        scale = diag[0]
        for k in range(1, 8):
            scale = jnp.where(sub == k, diag[k], scale)
        pivots.append(lax.rsqrt(scale))
    return jnp.concatenate([row * pivot for row, pivot in zip(rows, pivots)], axis=0)


def finish_kernel(
    gram_in,
    next_in,
    iface_in,
    mroot_in,
    mmid_in,
    mlow_in,
    leaf_out,
    root_out,
    mid_out,
    low_out,
    mroot_out,
    mmid_out,
    mlow_out,
    gram_ref,
    next_ref,
    iface_ref,
    full,
    lower,
    sem,
):
    mode = lax.axis_index("mode")
    moves = (
        (gram_in, gram_ref),
        (next_in, next_ref),
        (iface_in, iface_ref),
        (mroot_in, mroot_out),
        (mmid_in, mmid_out),
        (mlow_in, mlow_out),
    )
    moves = [pltpu.make_async_copy(a, b, sem.at[n]) for n, (a, b) in enumerate(moves)]
    for move in moves:
        move.start()
    moves[0].wait()
    low_lanes = lax.broadcasted_iota(jnp.int32, (128, 128), 1) < 64
    parts = [jnp.concatenate([gram_ref[t, c] for t in range(16)], axis=0) for c in range(3)]
    turned = [pltpu.roll(parts[c], 64, 1) for c in range(2)]
    first = jnp.where(low_lanes, parts[0], turned[1])
    cross = jnp.where(low_lanes, turned[0], parts[1])
    first = 0.5 * (first + first.T)
    second = 0.5 * (parts[2] + parts[2].T)
    gram = jnp.concatenate(
        [jnp.concatenate([first, cross.T], axis=1), jnp.concatenate([cross, second], axis=1)], axis=0
    )
    r = lax.broadcasted_iota(jnp.int32, (256, 256), 0)
    c = lax.broadcasted_iota(jnp.int32, (256, 256), 1)
    corner = jnp.where(r == c, gram, 0.0)
    down = lax.rsqrt(jnp.sum(corner, axis=1, keepdims=True))
    over = lax.rsqrt(jnp.sum(corner, axis=0, keepdims=True))
    full[:, 0:256] = gram * down * over
    full[:, 256:512] = jnp.where(r == c, jnp.broadcast_to(down, (256, 256)), 0.0)
    unit = (
        lax.broadcasted_iota(jnp.int32, (64, 64), 0) == lax.broadcasted_iota(jnp.int32, (64, 64), 1)
    ).astype(F32)
    for k in range(4):
        first = 64 * k
        block = full[first : first + 64, first : first + 64]
        weight = factor_block(jnp.concatenate([block, unit], axis=1))[:, 64:128]
        right = 128 * (k // 2)
        panel = nn(weight, full[first : first + 64, right:512])
        lower[first : first + 64, :] = panel[:, 256 - right : 512 - right]
        if k < 3:
            below = panel[:, first + 64 - right : 256 - right]
            full[first + 64 : 256, right:512] = full[first + 64 : 256, right:512] - tn(below, panel)
    own = lower[pl.ds(pl.multiple_of(mode * 64, 64), 64), :]
    for move in moves[1:]:
        move.wait()
    leaf_out[...] = nn(own, next_ref[...].reshape(256, 512))
    iface = jnp.concatenate([iface_ref[c][:, 0:64] for c in range(4)], axis=1)
    done = nt(iface, own)
    root_out[...] = done[0:8]
    mid_out[...] = done[8:24]
    low_out[...] = done[24:56]


def run_finish(gram, modal, iface, masses):
    vmem = pl.BlockSpec(memory_space=pltpu.VMEM)
    hbm = pl.BlockSpec(memory_space=pltpu.HBM)
    shapes = [(64, 512), (8, 64), (16, 64), (32, 64), (8, 128), (16, 128), (32, 128)]
    return pl.pallas_call(
        finish_kernel,
        out_shape=[jax.ShapeDtypeStruct(shape, F32) for shape in shapes],
        in_specs=[hbm] * 6,
        out_specs=[vmem] * 4 + [hbm] * 3,
        scratch_shapes=[
            pltpu.VMEM((16, 3, 8, 128), F32),
            pltpu.VMEM((4, 64, 512), F32),
            pltpu.VMEM((4, 56, 128), F32),
            pltpu.VMEM((256, 512), F32),
            pltpu.VMEM((256, 256), F32),
            pltpu.SemaphoreType.DMA((6,)),
        ],
        compiler_params=pltpu.CompilerParams(vmem_limit_bytes=64 * 1024 * 1024),
        name="finish",
    )(gram, modal, iface, *masses)


def local(
    leaf_sizes,
    leaf_stiffness,
    coupling,
    omega_root,
    omega_mid,
    omega_low,
    start_leaf,
    start_root,
    start_mid,
    start_low,
):
    gram, modal, iface, *masses = run_sweeps(
        leaf_sizes,
        leaf_stiffness.reshape(1, -1),
        coupling,
        start_leaf,
        [start_root.T, start_mid.T, start_low.T],
        [omega_root.reshape(1, -1), omega_mid.reshape(1, -1), omega_low.reshape(1, -1)],
    )
    leaf, root, mid, low, *masses = run_finish(gram, modal, iface, masses)
    return (leaf, root.T, mid.T, low.T, *masses)


def solution(mesh):
    placed = (
        P("leaf"),
        P("leaf"),
        P(None, "leaf", "mode"),
        P("leaf"),
        P("leaf"),
        P("leaf"),
        P("mode", "leaf"),
        P("mode", "leaf"),
        P("mode", "leaf"),
        P("mode", "leaf"),
    )
    return jax.shard_map(
        local,
        mesh=mesh,
        in_specs=placed,
        out_specs=(
            P("mode", "leaf"),
            P("mode", "leaf"),
            P("mode", "leaf"),
            P("mode", "leaf"),
            P("leaf", "mode"),
            P("leaf", "mode"),
            P("leaf", "mode"),
        ),
        check_vma=False,
    )
```
